32 devices in a mesh: dp: 4 (over y, core), mp: 8 (over z, x).
Axes of the slice: x: 2, y: 2, z: 4, core: 2. Of those that a mesh axis runs over, the one named last changes fastest.
Arguments:
- patches: bfloat16 [18432, 1024], P(('dp', 'mp')), may hold values from -6 to 6
- grid_sizes: int32 [32], P(('dp', 'mp')), may hold values from 16 to 24, as said below
- w_reduce_a: bfloat16 [1024, 256], P(None, 'mp'), may hold values from -0.1875 to 0.1875
- taps_a: bfloat16 [9, 256], P(None, 'mp'), may hold values from -2 to 2
- w_expand_a: bfloat16 [256, 1024], P('mp'), may hold values from -0.375 to 0.375
- gain_a: bfloat16 [1024], P('mp'), may hold values from 0.099609375 to 1.8984375
- w_reduce_b: bfloat16 [1024, 256], P(None, 'mp'), may hold values from -0.1875 to 0.1875
- taps_b: bfloat16 [9, 256], P(None, 'mp'), may hold values from -2 to 2
- w_expand_b: bfloat16 [256, 1024], P('mp'), may hold values from -0.375 to 0.375
- gain_b: bfloat16 [1024], P('mp'), may hold values from 0.099609375 to 1.8984375
- w_in: bfloat16 [1024, 4096], P(None, 'mp'), may hold values from -0.1875 to 0.1875
- w_out: bfloat16 [4096, 4096], P('mp'), may hold values from -0.09375 to 0.09375
- d_tokens: bfloat16 [4608, 4096], P(('dp', 'mp')), may hold values from -6 to 6
Outputs:
- tokens: bfloat16 [4608, 4096], P(('dp', 'mp'))
- d_patches: float32 [18432, 1024], P(('dp', 'mp'))
- grad_reduce_a: float32 [1024, 256], P(None, 'mp')
- grad_taps_a: float32 [9, 256], P(None, 'mp')
- grad_expand_a: float32 [256, 1024], P('mp')
- grad_gain_a: float32 [1024], P('mp')
- grad_reduce_b: float32 [1024, 256], P(None, 'mp')
- grad_taps_b: float32 [9, 256], P(None, 'mp')
- grad_expand_b: float32 [256, 1024], P('mp')
- grad_gain_b: float32 [1024], P('mp')
- grad_in: float32 [1024, 4096], P(None, 'mp')
- grad_out: float32 [4096, 4096], P('mp')
The draws below stay inside these ranges and needn't reach their ends.
Inputs may be any that keep to these rules, and one draw needn't show every extreme that they name: `grid_sizes`: each value is 16 or 24; an image of side 16 holds its features in the top-left 16 x 16 cells of its 24 x 24 rows, and its other rows are read by nothing.
All inputs are finite; a program needn't handle non-finite values.
Results may differ from the reference program's by a relative error of at most 0.02.
Values may be sent and summed in bfloat16 or wider, within the bound.
A program may use at most 320 MiB of HBM per device.

```python
import jax
import jax.numpy as jnp
from jax import lax

D = 1024
C = 256
H = 4096
OUT = 4096
GRID = 24
SMALL_GRID = 16
POOL = 12
IMAGES = 32


def draw_grid_sizes(key, part):
    key = jax.random.fold_in(key, 11)
    coin_flips = jax.random.randint(key, (IMAGES,), 0, 2)
    grid_sides = SMALL_GRID + (GRID - SMALL_GRID) * coin_flips
    grid_sides = grid_sides.at[0].set(GRID).at[1].set(SMALL_GRID)
    return grid_sides.astype(jnp.int32)


def level_of(key, shape, split, least, top_value):
    def one(axis_at, shards_of):
        heights = jax.random.uniform(jax.random.fold_in(jax.random.fold_in(key, 6), axis_at), (shards_of,), jnp.float32, least / len(split), top_value / len(split))
        return jnp.repeat(jnp.exp(heights), shape[axis_at] // shards_of).reshape((-1,) + (1,) * (len(shape) - axis_at - 1))

    loudness = one(*split[0])
    for cut in split[1:]:
        loudness = loudness * one(*cut)
    return loudness


def gaussian(stream_key, shape, spread, reach, shards=(), kind=jnp.bfloat16):
    array = jax.random.normal(stream_key, shape, jnp.float32) * spread
    if len(shards) > 0:
        array = level_of(stream_key, shape, shards, -0.22, 0.18) * array
    return jnp.clip(array, min=-reach, max=reach).astype(kind)


def setup_inputs(seed: int = 0) -> dict:
    key_of = jax.random.split(jax.random.key(seed), 14)
    patches = gaussian(key_of[0], (IMAGES * GRID * GRID, D), 1.0, 6.0, ((0, 32),))
    grid_sizes = draw_grid_sizes(jax.random.fold_in(key_of[13], 71), 0)
    w_reduce_a = gaussian(key_of[2], (D, C), D ** -0.5, 0.1875, ((1, 8),))
    taps_a = gaussian(key_of[3], (9, C), 9 ** -0.5, 2.0, ((1, 8),))
    w_expand_a = gaussian(key_of[4], (C, D), C ** -0.5, 0.375, ((0, 8),))
    gain_a = jnp.clip(1.0 + 0.18 * jax.random.normal(key_of[5], (D,), jnp.float32), 0.099609375, 1.8984375).astype(jnp.bfloat16)
    w_reduce_b = gaussian(key_of[6], (D, C), D ** -0.5, 0.1875, ((1, 8),))
    taps_b = gaussian(key_of[7], (9, C), 9 ** -0.5, 2.0, ((1, 8),))
    w_expand_b = gaussian(key_of[8], (C, D), C ** -0.5, 0.375, ((0, 8),))
    gain_b = jnp.clip(1.0 + 0.18 * jax.random.normal(key_of[9], (D,), jnp.float32), 0.099609375, 1.8984375).astype(jnp.bfloat16)
    w_in = gaussian(key_of[10], (D, H), D ** -0.5, 0.1875, ((1, 8),))
    w_out = gaussian(key_of[11], (H, OUT), H ** -0.5, 0.09375, ((0, 8),))
    d_tokens = gaussian(key_of[12], (IMAGES * POOL * POOL, OUT), 1.0, 6.0, ((0, 32),))
    return {"patches": patches, "grid_sizes": grid_sizes, "w_reduce_a": w_reduce_a, "taps_a": taps_a, "w_expand_a": w_expand_a, "gain_a": gain_a, "w_reduce_b": w_reduce_b, "taps_b": taps_b, "w_expand_b": w_expand_b, "gain_b": gain_b, "w_in": w_in, "w_out": w_out, "d_tokens": d_tokens}


epsilon = 1e-05
highest = lax.Precision.HIGHEST

@jax.custom_vjp
def low(v):
    return lax.optimization_barrier(v.astype(jnp.bfloat16)).astype(jnp.float32)

@jax.custom_vjp
def low_back(v):
    return v

def low_keep(v):
    return (low(v), None)

def low_pass(kept, grad):
    return (grad,)

def back_keep(v):
    return (v, None)

def back_low(kept, grad):
    return (low(grad),)
low.defvjp(low_keep, low_pass)
low_back.defvjp(back_keep, back_low)

def matmul(left, right):
    return jnp.dot(left, right, precision=highest)

def depthwise(feature_map, tap_weights):
    extent = feature_map.shape[-2]
    padding = [(0, 0)] * (feature_map.ndim - 3) + [(1, 1), (1, 1), (0, 0)]
    padded = jnp.pad(feature_map, padding)
    result = jnp.zeros_like(feature_map)
    for tap_row in range(3):
        for tap_col in range(3):
            result = result + padded[..., tap_row:tap_row + extent, tap_col:tap_col + extent, :] * tap_weights[3 * tap_row + tap_col]
    return result

def bottleneck(feature_map, w_reduce, tap_weights, w_expand, norm_gain, cell_mask):
    extent = feature_map.shape[0]
    features = feature_map.shape[2]
    flat_rows = feature_map.reshape(extent * extent, features)
    reduced = low_back(matmul(low(flat_rows), w_reduce))
    activated = jax.nn.silu(reduced).reshape(extent, extent, -1) * cell_mask[:, :, None]
    spatial = depthwise(activated, tap_weights)
    narrow = low(jax.nn.silu(spatial)).reshape(extent * extent, -1)
    widened = low_back(matmul(narrow, w_expand))
    centred = widened - lax.optimization_barrier(jnp.mean(widened, axis=1, keepdims=True))
    normed = centred * lax.rsqrt(lax.optimization_barrier(jnp.mean(centred * centred, axis=1, keepdims=True)) + epsilon)
    return feature_map + (normed * norm_gain).reshape(extent, extent, features)

def pool_table(grid_side):
    bin_index = jnp.arange(POOL, dtype=jnp.int32)
    bin_lower = bin_index * grid_side // POOL
    bin_upper = ((bin_index + 1) * grid_side + POOL - 1) // POOL
    cell_index = jnp.arange(GRID, dtype=jnp.int32)
    inside = (cell_index[None, :] >= bin_lower[:, None]) & (cell_index[None, :] < bin_upper[:, None])
    weights = jnp.where(inside, 1.0, 0.0) / (bin_upper - bin_lower)[:, None]
    return weights.astype(jnp.float32)

def relay(parameters, picture, grid_side):
    reduce_a, conv_a, expand_a, scale_a, reduce_b, conv_b, expand_b, scale_b, read_in, read_out = parameters
    cell_index = jnp.arange(GRID, dtype=jnp.int32)
    inside = jnp.where(cell_index < grid_side, 1.0, 0.0).astype(jnp.float32)
    segment_one = bottleneck(picture, reduce_a, conv_a, expand_a, scale_a, inside[:, None] * inside[None, :])
    pool_weights = pool_table(grid_side)
    pooled = jnp.einsum('ia,jb,abd->ijd', pool_weights, pool_weights, segment_one, precision=highest)
    second = bottleneck(pooled, reduce_b, conv_b, expand_b, scale_b, jnp.ones((POOL, POOL), jnp.float32))
    queries = low(second.reshape(POOL * POOL, -1))
    hidden = low_back(matmul(queries, read_in))
    active = low(jax.nn.gelu(hidden, approximate=False))
    return matmul(active, read_out)

def reference(patches, grid_sizes, w_reduce_a, taps_a, w_expand_a, gain_a, w_reduce_b, taps_b, w_expand_b, gain_b, w_in, w_out, d_tokens):
    parameters = tuple((weight.astype(jnp.float32) for weight in (w_reduce_a, taps_a, w_expand_a, gain_a, w_reduce_b, taps_b, w_expand_b, gain_b, w_in, w_out)))
    features = patches.shape[1]
    pictures = patches.astype(jnp.float32).reshape(-1, GRID, GRID, features)

    def per_image(params_in, element):
        return relay(params_in, element[0], element[1])
    checked = jax.checkpoint(per_image)

    def forward(pictures_in, params_in):
        return lax.map(lambda element: checked(params_in, element), (pictures_in, grid_sizes))
    outputs, pullback = jax.vjp(forward, pictures, parameters)
    cotangent = d_tokens.astype(jnp.float32).reshape(outputs.shape)
    d_pictures, d_params = pullback(cotangent)
    tokens = outputs.reshape(-1, outputs.shape[2]).astype(jnp.bfloat16)
    d_patches = d_pictures.reshape(-1, features)
    return (tokens, d_patches, d_params[0], d_params[1], d_params[2], d_params[3], d_params[4], d_params[5], d_params[6], d_params[7], d_params[8], d_params[9])
```

```python
import jax
import jax.numpy as jnp
from jax import lax
from jax.experimental import pallas as pl
from jax.experimental.pallas import tpu as pltpu
from jax.sharding import PartitionSpec as P

GRID = 24
SMALL_GRID = 16
POOL = 12


epsilon = 1e-05
highest = lax.Precision.HIGHEST
root_half = 0.7071067811865476
inv_root_tau = 0.3989422804014327


def silu_slope(values):
    sigmoid = jax.nn.sigmoid(values)
    return sigmoid * (1.0 + values * (1.0 - sigmoid))


def gelu_exact(values):
    return 0.5 * values * (1.0 + lax.erf(values * root_half))


def gelu_slope(values):
    return (
        0.5 * (1.0 + lax.erf(values * root_half))
        + values * jnp.exp(-0.5 * values * values) * inv_root_tau
    )


def outer_rows(left, right):
    return lax.dot_general(
        left, right, (((0,), (0,)), ((), ())), preferred_element_type=jnp.float32
    )


def times_trans(left, right):
    return lax.dot_general(
        left, right, (((1,), (1,)), ((), ())), preferred_element_type=jnp.float32
    )


def map_padding(ndims):
    return [(0, 0)] * (ndims - 3) + [(1, 1), (1, 1), (0, 0)]


def depthwise(feature_map, tap_weights):
    extent = feature_map.shape[-2]
    padded = jnp.pad(feature_map, map_padding(feature_map.ndim))
    result = jnp.zeros_like(feature_map)
    for tap_row in range(3):
        for tap_col in range(3):
            result = (
                result
                + padded[..., tap_row : tap_row + extent, tap_col : tap_col + extent, :]
                * tap_weights[3 * tap_row + tap_col]
            )
    return result


def depthwise_back(upstream, feature_map, tap_weights):
    extent = upstream.shape[-2]
    upstream_pad = jnp.pad(upstream, map_padding(upstream.ndim))
    feature_pad = jnp.pad(feature_map, map_padding(feature_map.ndim))
    d_feature = jnp.zeros_like(upstream)
    tap_grads = []
    leading = tuple(range(upstream.ndim - 1))
    for tap_row in range(3):
        for tap_col in range(3):
            d_feature = (
                d_feature
                + upstream_pad[
                    ..., 2 - tap_row : 2 - tap_row + extent, 2 - tap_col : 2 - tap_col + extent, :
                ]
                * tap_weights[3 * tap_row + tap_col]
            )
            shifted = feature_pad[..., tap_row : tap_row + extent, tap_col : tap_col + extent, :]
            tap_grads.append(jnp.sum(shifted * upstream, axis=leading))
    return (d_feature, jnp.stack(tap_grads))


def block_forward(feature_rows, low_rows, weights_set, extent):
    w_reduce, tap_weights, w_expand, norm_gain = weights_set
    channels = w_reduce.shape[1]
    row_count = feature_rows.shape[0]
    reduced = jnp.dot(low_rows, w_reduce, preferred_element_type=jnp.float32)
    activated = jax.nn.silu(reduced).reshape(-1, extent, extent, channels)
    spatial = depthwise(activated, tap_weights.astype(jnp.float32)).reshape(row_count, channels)
    narrow = jax.nn.silu(spatial).astype(jnp.bfloat16)
    widened = jnp.dot(narrow, w_expand, preferred_element_type=jnp.float32)
    centred = widened - jnp.mean(widened, axis=1, keepdims=True)
    inv_scale = lax.rsqrt(jnp.mean(centred * centred, axis=1, keepdims=True) + epsilon)
    normed = centred * inv_scale
    result = feature_rows + normed * norm_gain.astype(jnp.float32)
    return (result, (reduced, activated, spatial, narrow, normed, inv_scale))


def block_backward(d_result, low_rows, weights_set, saved):
    w_reduce, tap_weights, w_expand, norm_gain = weights_set
    reduced, activated, spatial, narrow, normed, inv_scale = saved
    d_gain = jnp.sum(d_result * normed, axis=0)
    d_normed = d_result * norm_gain.astype(jnp.float32)
    d_widened = inv_scale * (
        d_normed
        - jnp.mean(d_normed, axis=1, keepdims=True)
        - normed * jnp.mean(d_normed * normed, axis=1, keepdims=True)
    )
    d_widened = d_widened.astype(jnp.bfloat16)
    grad_expand = outer_rows(narrow, d_widened)
    d_spatial = times_trans(d_widened, w_expand) * silu_slope(spatial)
    d_activated, grad_taps = depthwise_back(
        d_spatial.reshape(activated.shape), activated, tap_weights.astype(jnp.float32)
    )
    d_reduced = (d_activated.reshape(reduced.shape) * silu_slope(reduced)).astype(jnp.bfloat16)
    grad_reduce = outer_rows(low_rows, d_reduced)
    d_rows = d_result + times_trans(d_reduced, w_reduce)
    return (d_rows, (grad_reduce, grad_taps, grad_expand, d_gain))


def crop_rows(pixels, extent):
    features = pixels.shape[-1]
    return pixels.reshape(GRID, GRID, features)[:extent, :extent].reshape(extent * extent, features)


def widen_grid(values, extent):
    features = values.shape[-1]
    return jnp.pad(
        values.reshape(extent, extent, features), ((0, GRID - extent), (0, GRID - extent), (0, 0))
    )


def first_forward(weights_set, extent):

    def compute(pixels):
        cropped = crop_rows(pixels, extent)
        result, unused = block_forward(cropped.astype(jnp.float32), cropped, weights_set, extent)
        return widen_grid(result, extent)

    return compute


def first_backward(weights_set, extent):

    def compute(pixels, upstream):
        cropped = crop_rows(pixels, extent)
        sliced = crop_rows(upstream, extent)
        unused, saved = block_forward(cropped.astype(jnp.float32), cropped, weights_set, extent)
        d_rows, grads = block_backward(sliced, cropped, weights_set, saved)
        return (widen_grid(d_rows, extent).reshape(GRID * GRID, -1), grads)

    return compute


def pool_table(grid_side):
    bin_index = lax.iota(jnp.int32, POOL)
    bin_lower = bin_index * grid_side // POOL
    bin_upper = ((bin_index + 1) * grid_side + POOL - 1) // POOL
    cell_index = lax.iota(jnp.int32, GRID)
    inside = (cell_index[None, :] >= bin_lower[:, None]) & (
        cell_index[None, :] < bin_upper[:, None]
    )
    weights = jnp.where(inside, 1.0, 0.0) / (bin_upper - bin_lower)[:, None]
    return weights.astype(jnp.float32)


def body(
    patches,
    grid_sizes,
    w_reduce_a,
    taps_a,
    w_expand_a,
    gain_a,
    w_reduce_b,
    taps_b,
    w_expand_b,
    gain_b,
    w_in,
    w_out,
    d_tokens,
):
    gathered = (
        lax.all_gather(w_reduce_a, "mp", axis=1, tiled=True),
        lax.all_gather(taps_a, "mp", axis=1, tiled=True),
        lax.all_gather(w_expand_a, "mp", axis=0, tiled=True),
        lax.all_gather(gain_a, "mp", axis=0, tiled=True),
        lax.all_gather(w_reduce_b, "mp", axis=1, tiled=True),
        lax.all_gather(taps_b, "mp", axis=1, tiled=True),
        lax.all_gather(w_expand_b, "mp", axis=0, tiled=True),
        lax.all_gather(gain_b, "mp", axis=0, tiled=True),
    )
    first_set = gathered[0:4]
    second_set = gathered[4:8]
    features = patches.shape[1]
    pictures = patches.reshape(-1, GRID * GRID, features)
    picture_count = pictures.shape[0]
    tables = jax.vmap(pool_table)(grid_sizes)

    def forward_one(element):
        pixels, grid_side, pool_weights = element
        result = lax.cond(
            grid_side == GRID,
            first_forward(first_set, GRID),
            first_forward(first_set, SMALL_GRID),
            pixels,
        )
        return jnp.einsum("ia,jb,abd->ijd", pool_weights, pool_weights, result, precision=highest)

    pooled = lax.map(forward_one, (pictures, grid_sizes, tables))
    pooled_rows = pooled.reshape(picture_count * POOL * POOL, features)
    pooled_low = pooled_rows.astype(jnp.bfloat16)
    mixed_rows, second_saved = block_forward(pooled_rows, pooled_low, second_set, POOL)
    queries = mixed_rows.astype(jnp.bfloat16)
    hidden = jnp.dot(
        lax.all_gather(queries, "mp", axis=0, tiled=True), w_in, preferred_element_type=jnp.float32
    )
    active = gelu_exact(hidden).astype(jnp.bfloat16)
    tokens = lax.psum_scatter(
        jnp.dot(active, w_out, preferred_element_type=jnp.float32).astype(jnp.bfloat16),
        "mp",
        scatter_dimension=0,
        tiled=True,
    )
    piece = lax.all_gather(d_tokens, "mp", axis=0, tiled=True)
    d_part = (times_trans(piece, w_out) * gelu_slope(hidden)).astype(jnp.bfloat16)
    grad_out_sum = outer_rows(active, piece)
    d_hidden = d_part
    d_part = d_hidden
    grad_in_part = outer_rows(lax.all_gather(queries, "mp", axis=0, tiled=True), d_part)
    d_part = d_hidden
    d_mixed = lax.psum_scatter(times_trans(d_part, w_in), "mp", scatter_dimension=0, tiled=True)
    d_pooled, second_grads = block_backward(d_mixed, pooled_low, second_set, second_saved)
    d_pooled = d_pooled.reshape(picture_count, POOL, POOL, features)

    def backward_one(totals, element):
        pixels, grid_side, pool_weights, upstream = element
        d_grid = jnp.einsum(
            "ia,jb,ijd->abd", pool_weights, pool_weights, upstream, precision=highest
        )
        d_pixels, grads = lax.cond(
            grid_side == GRID,
            first_backward(first_set, GRID),
            first_backward(first_set, SMALL_GRID),
            pixels,
            d_grid,
        )
        return (
            tuple((total_part + grad_part for total_part, grad_part in zip(totals, grads))),
            d_pixels,
        )

    zero_grads = tuple((jnp.zeros(weight.shape, jnp.float32) for weight in first_set))
    first_grads, d_pictures = lax.scan(
        backward_one, zero_grads, (pictures, grid_sizes, tables, d_pooled)
    )
    d_patches = d_pictures.reshape(-1, features)
    shards = (
        lax.psum_scatter(
            first_grads[0].astype(jnp.bfloat16), "mp", scatter_dimension=1, tiled=True
        ).astype(jnp.float32),
        lax.psum_scatter(
            first_grads[1].astype(jnp.bfloat16), "mp", scatter_dimension=1, tiled=True
        ).astype(jnp.float32),
        lax.psum_scatter(
            first_grads[2].astype(jnp.bfloat16), "mp", scatter_dimension=0, tiled=True
        ).astype(jnp.float32),
        lax.psum_scatter(
            first_grads[3].astype(jnp.bfloat16), "mp", scatter_dimension=0, tiled=True
        ).astype(jnp.float32),
        lax.psum_scatter(
            second_grads[0].astype(jnp.bfloat16), "mp", scatter_dimension=1, tiled=True
        ).astype(jnp.float32),
        lax.psum_scatter(
            second_grads[1].astype(jnp.bfloat16), "mp", scatter_dimension=1, tiled=True
        ).astype(jnp.float32),
        lax.psum_scatter(
            second_grads[2].astype(jnp.bfloat16), "mp", scatter_dimension=0, tiled=True
        ).astype(jnp.float32),
        lax.psum_scatter(
            second_grads[3].astype(jnp.bfloat16), "mp", scatter_dimension=0, tiled=True
        ).astype(jnp.float32),
    )
    summed = (
        lax.psum(shards[0].astype(jnp.bfloat16), "dp").astype(jnp.float32),
        lax.psum(shards[1].astype(jnp.bfloat16), "dp").astype(jnp.float32),
        lax.psum(shards[2].astype(jnp.bfloat16), "dp").astype(jnp.float32),
        lax.psum(shards[3].astype(jnp.bfloat16), "dp").astype(jnp.float32),
        lax.psum(shards[4].astype(jnp.bfloat16), "dp").astype(jnp.float32),
        lax.psum(shards[5].astype(jnp.bfloat16), "dp").astype(jnp.float32),
        lax.psum(shards[6].astype(jnp.bfloat16), "dp").astype(jnp.float32),
        lax.psum(shards[7].astype(jnp.bfloat16), "dp").astype(jnp.float32),
        lax.psum(grad_in_part.astype(jnp.bfloat16), "dp").astype(jnp.float32),
        lax.psum(grad_out_sum.astype(jnp.bfloat16), "dp").astype(jnp.float32),
    )
    return (
        tokens,
        d_patches,
        summed[0],
        summed[1],
        summed[2],
        summed[3],
        summed[4],
        summed[5],
        summed[6],
        summed[7],
        summed[8],
        summed[9],
    )


bf16 = jnp.bfloat16
f32 = jnp.float32
MESH = pl.DeviceIdType.MESH
CELLS = GRID * GRID
POOLED = POOL * POOL
TILE = 96
PIECES = 4
CHUNKS = 8


def dot(left, right, left_dim, right_dim):
    return lax.dot_general(
        left, right, (((left_dim,), (right_dim,)), ((), ())), preferred_element_type=f32
    )


def split_low(values):
    high = values.astype(bf16)
    return high, (values - high.astype(f32)).astype(bf16)


def edge_masks(extent, channels):
    cells = extent * extent
    index = lax.broadcasted_iota(jnp.int32, (cells, channels), 0).astype(f32)
    row = jnp.floor((index + 0.5) * (1.0 / extent))
    col = index - row * extent
    one = jnp.ones_like(index)
    zero = jnp.zeros_like(index)
    return (
        jnp.where(row >= 0.5, one, zero),
        jnp.where(row <= extent - 1.5, one, zero),
        jnp.where(col >= 0.5, one, zero),
        jnp.where(col <= extent - 1.5, one, zero),
    )


def conv_forward(act, taps, extent, masks):
    above, below, left, right = masks
    cells = extent * extent
    up = pltpu.roll(act, extent, 0) * above
    down = pltpu.roll(act, cells - extent, 0) * below
    sums = [up * taps[q] + act * taps[3 + q] + down * taps[6 + q] for q in range(3)]
    return (
        sums[1]
        + pltpu.roll(sums[0], 1, 0) * left
        + pltpu.roll(sums[2], cells - 1, 0) * right
    )


def conv_backward(upstream, act, taps, extent, masks):
    above, below, left, right = masks
    cells = extent * extent
    sides = [pltpu.roll(upstream, cells - 1, 0) * right, upstream, pltpu.roll(upstream, 1, 0) * left]
    sums = [
        sides[0] * taps[3 * r] + sides[1] * taps[3 * r + 1] + sides[2] * taps[3 * r + 2]
        for r in range(3)
    ]
    d_act = (
        sums[1]
        + pltpu.roll(sums[0], cells - extent, 0) * below
        + pltpu.roll(sums[2], extent, 0) * above
    )
    acts = [pltpu.roll(act, extent, 0) * above, act, pltpu.roll(act, cells - extent, 0) * below]
    d_taps = [
        jnp.sum(acts[r] * sides[q], axis=0, keepdims=True) for r in range(3) for q in range(3)
    ]
    return d_act, d_taps


def slot_rows(ref):
    slots, rows, columns = ref.shape
    return ref[...].reshape(slots * rows, columns)


def layer_kernel(
    patches_in, side_in, pack_in, w_in_in, w_out_in, cot_in,
    tok_out, dpat_out, gout_out, gin_out, gblk_out, gsml_out, cot_all, gx_land, gi_land,
    xp, gw, red_a, spa_a, nar_a, norm_a, inv_a, yhi, ylo, dy, dlow, pp,
    tw, poolv, red_b, spa_b, nar_b, norm_b, inv_b,
    wi, wo, qs, actv, slope, dpre, dtv, tp, cr, ps, rl, tstage,
    dr, dz, gos, gis, land,
    wgs, wgc, xs, xr, zs, zr, ys, yr, sm, smc, smx, smz, smy, gfin,
    loc, w_s, w_rz, w_rx, w_rc, sw_s, sw_r, q_s, q_rz, q_rc,
    dt_s, dt_r, dt_cs, dt_cr, t_cs, t_cr, t_s, t_r, credit,
    d_cs, d_cr, d_zs, d_zr, gx_s, gx_r, gy_s, gy_r, gc_s, gc_r, gl,
    gr_s, gr_r,
):
    dp_at = lax.axis_index("dp")
    mp_at = lax.axis_index("mp")
    y = lax.div(dp_at, 2)
    c = lax.rem(dp_at, 2)
    z = lax.div(mp_at, 2)
    x = lax.rem(mp_at, 2)
    zn = 4

    def device(x_at, y_at, z_at, c_at):
        return (2 * y_at + c_at, 2 * z_at + x_at)

    twin = device(x, y, z, 1 - c)
    x_peer = device(1 - x, y, z, c)
    cross = device(1 - x, y, z, 1 - c)
    y_peer = device(x, 1 - y, z, c)

    def z_at(step):
        return lax.rem(z + step + zn, zn)

    def z_dev(z_of):
        return device(x, y, z_of, c)

    def remote(src, dst, send, recv, to):
        return pltpu.make_async_remote_copy(
            src_ref=src, dst_ref=dst, send_sem=send, recv_sem=recv, device_id=to, device_id_type=MESH
        )

    def start(src, dst, send, recv, to):
        remote(src, dst, send, recv, to).start()

    def arrived(dst, recv):
        pltpu.make_async_copy(dst, dst, recv).wait()

    def left_here(src, send):
        pltpu.make_async_copy(src, src, send).wait()

    own = x == c

    load_patches = pltpu.make_async_copy(patches_in, xp, loc.at[0])
    load_pack = pltpu.make_async_copy(pack_in.at[c], gw.at[c, mp_at], loc.at[1])
    me = 2 * z + c
    load_cot = pltpu.make_async_copy(cot_in, cot_all.at[z, c], loc.at[2])
    load_patches.start()
    load_pack.start()
    load_cot.start()

    barrier = pltpu.get_barrier_semaphore()
    peers = [twin, x_peer, cross, y_peer] + [z_dev(z_at(k)) for k in range(1, zn)]
    for peer in peers:
        pl.semaphore_signal(barrier, inc=1, device_id=peer, device_id_type=MESH)
    pl.semaphore_wait(barrier, len(peers))

    load_pack.wait()
    spans = ((0, 48), (48, 32))

    def w_part(b, core, i):
        return gw.at[core, i, pl.ds(spans[b][0], spans[b][1])]

    def w_own(b):
        part = w_part(b, c, mp_at)
        for k in range(1, zn):
            start(part, part, w_s.at[b, k - 1], w_rz.at[b, k], z_dev(z_at(k)))
        start(part, part, w_s.at[b, 3], w_rx.at[b, z], x_peer)
        start(part, part, w_s.at[b, 7], w_rc.at[b, mp_at], twin)

    def w_forward(b):
        for k in range(1, zn):
            z_of = z_at(-k)
            i = 2 * z_of + x
            part = w_part(b, c, i)
            arrived(part, w_rz.at[b, k])
            start(part, part, w_s.at[b, 3 + k], w_rx.at[b, z_of], x_peer)
            start(part, part, w_s.at[b, 7 + k], w_rc.at[b, i], twin)
        for k in range(zn):
            z_of = z_at(-k)
            i = 2 * z_of + 1 - x
            part = w_part(b, c, i)
            arrived(part, w_rx.at[b, z_of])
            start(part, part, w_s.at[b, 11 + k], w_rc.at[b, i], twin)

    def w_finish(b):
        for i in range(8):
            arrived(w_part(b, 1 - c, i), w_rc.at[b, i])

    w_own(0)
    w_own(1)

    width = cot_in.shape[1] // PIECES

    def cot(z_of, c_of, p):
        return cot_all.at[z_of, c_of, :, pl.ds(pl.multiple_of(p * width, width), width)]

    def cot_right(z_of, p, hop):
        @pl.when(z < zn - 1)
        def _():
            part = cot(z_of, c, p)
            start(part, part, dt_s.at[p, 0, hop], dt_r.at[p, 0, hop], z_dev(z + 1))

    def cot_left(z_of, p, hop):
        @pl.when(z > 0)
        def _():
            part = cot(z_of, c, p)
            start(part, part, dt_s.at[p, 1, hop], dt_r.at[p, 1, hop], z_dev(z - 1))

    def cot_twin(z_of, p):
        part = cot(z_of, c, p)
        start(part, part, dt_cs.at[p, z_of], dt_cr.at[p, z_of], twin)

    def cot_own(p):
        cot_right(z, p, 0)
        cot_left(z, p, 0)
        cot_twin(z, p)

    def cot_hop(p, hop):
        @pl.when(z >= hop)
        def _():
            arrived(cot(z - hop, c, p), dt_r.at[p, 0, hop - 1])
            if hop < zn - 1:
                cot_right(z - hop, p, hop)
            cot_twin(z - hop, p)

        @pl.when(z + hop <= zn - 1)
        def _():
            arrived(cot(z + hop, c, p), dt_r.at[p, 1, hop - 1])
            if hop < zn - 1:
                cot_left(z + hop, p, hop)
            cot_twin(z + hop, p)

    w_forward(0)
    chunk = w_out_in.shape[1] // CHUNKS

    def columns(ref, j, span):
        return ref.at[:, pl.ds(j * span, span)]

    @pl.when(own)
    def _():
        pltpu.make_async_copy(w_in_in, wi, sw_r.at[0]).start()
        for j in range(CHUNKS):
            pltpu.make_async_copy(
                columns(w_out_in, j, chunk), columns(wo, j, chunk), sw_r.at[1 + j]
            ).start()

    @pl.when(jnp.logical_not(own))
    def _():
        start(w_in_in, wi, sw_s.at[0], sw_r.at[0], cross)
        for j in range(CHUNKS):
            start(
                columns(w_out_in, j, chunk), columns(wo, j, chunk),
                sw_s.at[1 + j], sw_r.at[1 + j], cross,
            )

    load_cot.wait()
    for p in range(2):
        cot_own(p)
    w_finish(0)

    def block_weights(b):
        rows = pl.ds(spans[b][0], 32)
        return (
            gw[0, :, rows, :].reshape(256, 1024),
            gw[1, :, rows, :].reshape(256, 1024),
        )

    def small_weights(b):
        total = gw[b, 0, 32:48, :].astype(f32)
        for i in range(1, 8):
            total = total + gw[b, i, 32:48, :].astype(f32)
        tw[b] = total
        return total[9:10, :]

    def lanes_of(h):
        return pl.ds(pl.multiple_of(h * 128, 128), 128)

    def tap_rows(b, lanes):
        return [tw[b, k : k + 1, lanes] for k in range(9)]

    gain_a = small_weights(0)
    side = side_in[0].astype(f32)
    def cell_mask():
        index = lax.broadcasted_iota(jnp.int32, (CELLS, 128), 0).astype(f32)
        row = jnp.floor((index + 0.5) * (1.0 / GRID))
        col = index - row * GRID
        return jnp.where((row < side - 0.5) & (col < side - 0.5), 1.0, 0.0).astype(f32)

    load_patches.wait()
    wr_a, we_a = block_weights(0)
    red_a[...] = dot(xp[...], wr_a, 1, 1)

    def conv_half_a(h, carry):
        lanes = lanes_of(h)
        reduced = red_a[:, lanes]
        activated = reduced * jax.nn.sigmoid(reduced) * cell_mask()
        spatial = conv_forward(activated, tap_rows(0, lanes), GRID, edge_masks(GRID, 128))
        spa_a[:, lanes] = spatial
        nar_a[:, lanes] = (spatial * jax.nn.sigmoid(spatial)).astype(bf16)
        return carry

    lax.fori_loop(0, 2, conv_half_a, 0)
    dy[...] = dot(nar_a[...], we_a, 1, 0)

    def normalise(wide_ref, ref, inv_ref, rows):
        widened = wide_ref[rows, :]
        centred = widened - jnp.mean(widened, axis=1, keepdims=True)
        inv = lax.rsqrt(jnp.mean(centred * centred, axis=1, keepdims=True) + epsilon)
        normed = centred * inv
        ref[rows, :] = normed.astype(ref.dtype)
        inv_ref[rows, :] = jnp.broadcast_to(inv, (normed.shape[0], 128))
        return normed

    def norm_tile(t, carry):
        rows = pl.ds(pl.multiple_of(t * TILE, TILE), TILE)
        normed = normalise(dy, norm_a, inv_a, rows)
        result = xp[rows, :].astype(f32) + normed * gain_a
        high, low = split_low(result)
        yhi[rows, :] = high
        ylo[rows, :] = low
        return carry

    lax.fori_loop(0, CELLS // TILE, norm_tile, 0)

    cell = lax.broadcasted_iota(jnp.int32, (POOLED, CELLS), 1).astype(f32)
    bin_of = lax.broadcasted_iota(jnp.int32, (POOLED, CELLS), 0).astype(f32)
    cell_row = jnp.floor((cell + 0.5) * (1.0 / GRID))
    cell_col = cell - cell_row * GRID
    bin_row = jnp.floor((bin_of + 0.5) * (1.0 / POOL))
    bin_col = bin_of - bin_row * POOL

    def table(bins, at):
        lower = jnp.floor((bins * side + 0.5) * (1.0 / POOL))
        upper = jnp.floor(((bins + 1.0) * side + (POOL - 0.5)) * (1.0 / POOL))
        return jnp.where((at > lower - 0.5) & (at < upper - 0.5), 1.0 / (upper - lower), 0.0)

    pp[...] = (table(bin_row, cell_row) * table(bin_col, cell_col)).astype(bf16)
    pooled = dot(pp[...], yhi[...], 1, 0) + dot(pp[...], ylo[...], 1, 0)
    poolv[...] = pooled

    w_forward(1)
    w_finish(1)

    gain_b = small_weights(1)
    wr_b, we_b = block_weights(1)
    reduced_b = dot(pooled.astype(bf16), wr_b, 1, 1)
    red_b[...] = reduced_b
    activated_b = reduced_b * jax.nn.sigmoid(reduced_b)
    spatial_b = conv_forward(activated_b, tap_rows(1, pl.ds(0, 256)), POOL, edge_masks(POOL, 256))
    spa_b[...] = spatial_b
    nar_b[...] = (spatial_b * jax.nn.sigmoid(spatial_b)).astype(bf16)
    norm_b[...] = dot(nar_b[...], we_b, 1, 0)
    normed_b = normalise(norm_b, norm_b, inv_b, pl.ds(0, POOLED))
    qs[me] = (pooled + normed_b * gain_b).astype(bf16)

    for k in range(1, zn):
        start(qs.at[me], qs.at[me], q_s.at[k - 1], q_rz.at[k], z_dev(z_at(k)))
    start(qs.at[me], qs.at[me], q_s.at[3], q_rc.at[z], twin)
    for p in range(2, PIECES):
        cot_own(p)
    for k in range(1, zn):
        z_of = z_at(-k)
        slot = qs.at[2 * z_of + c]
        arrived(slot, q_rz.at[k])
        start(slot, slot, q_s.at[3 + k], q_rc.at[z_of], twin)
    for p in range(PIECES):
        cot_hop(p, 1)
    for z_of in range(zn):
        arrived(qs.at[2 * z_of + 1 - c], q_rc.at[z_of])
    arrived(wi, sw_r.at[0])

    dpre[...] = dot(slot_rows(qs), wi[...], 1, 0)

    def gelu_tile(t, carry):
        rows = pl.ds(pl.multiple_of(t * POOLED, POOLED), POOLED)
        hidden = dpre[rows, :]
        phi = 0.5 * (1.0 + lax.erf(hidden * root_half))
        actv[rows, :] = (hidden * phi).astype(bf16)
        slope[rows, :] = (
            phi + hidden * jnp.exp(-0.5 * hidden * hidden) * inv_root_tau
        ).astype(bf16)
        return carry

    lax.fori_loop(0, 8, gelu_tile, 0)
    dpre[...] = jnp.zeros_like(dpre)

    def item_part(i):
        b = lax.rem(i, 2)

        @pl.when(i >= 2)
        def _():
            left_here(tp.at[b, :, 1 - c], t_cs.at[b])
            pl.semaphore_wait(credit, 1)

        weights = wo[:, pl.ds(pl.multiple_of(i * chunk, chunk), chunk)]
        partial = dot(actv[...], weights, 1, 0).astype(bf16)
        tp[b] = partial.reshape(zn, 2, POOLED, chunk)
        start(tp.at[b, :, 1 - c], cr.at[b], t_cs.at[b], t_cr.at[b], twin)

    def send_right(i, d):
        start(ps.at[i, d], rl.at[i, d + 1], t_s.at[i, d], t_r.at[i, d + 1], z_dev(z + 1))

    def send_left(i, d):
        start(ps.at[i, d], rl.at[i, d], t_s.at[i, d], t_r.at[i, d], z_dev(z - 1))

    def item_pair(i):
        b = lax.rem(i, 2)
        arrived(cr.at[b], t_cr.at[b])

        def add(d, carry):
            ps[i, d] = (tp[b, d, c].astype(f32) + cr[b, d].astype(f32)).astype(bf16)
            return carry

        lax.fori_loop(0, zn, add, 0)

        @pl.when(i < CHUNKS - 2)
        def _():
            pl.semaphore_signal(credit, inc=1, device_id=twin, device_id_type=MESH)

        @pl.when(z == 0)
        def _():
            for d in range(zn - 1, 0, -1):
                send_right(i, d)

        @pl.when(z == zn - 1)
        def _():
            for d in range(zn - 1):
                send_left(i, d)

    def item_right(i):
        def pass_on(step, carry):
            d = zn - 1 - step
            arrived(rl.at[i, d + 1], t_r.at[i, d + 1])
            ps[i, d] = (ps[i, d].astype(f32) + rl[i, d + 1].astype(f32)).astype(bf16)
            send_right(i, d)
            return carry

        lax.fori_loop(0, zn - 1 - z, pass_on, 0)
        arrived(rl.at[i, z + 1], t_r.at[i, z + 1])

    def item_left(i):
        def pass_on(d, carry):
            arrived(rl.at[i, d], t_r.at[i, d])
            ps[i, d] = (ps[i, d].astype(f32) + rl[i, d].astype(f32)).astype(bf16)
            send_left(i, d)
            return carry

        lax.fori_loop(0, z, pass_on, 0)
        arrived(rl.at[i, z], t_r.at[i, z])

    def tok_slice(i):
        return tok_out.at[:, pl.ds(pl.multiple_of(i * chunk, chunk), chunk)]

    def item_final(i):
        b = lax.rem(i, 2)

        @pl.when(i >= 2)
        def _():
            left_here(tstage.at[b], gl.at[8 + b])

        tstage[b] = ps[i, z]

        @pl.when(z > 0)
        def _():
            tstage[b] = (tstage[b].astype(f32) + rl[i, z + 1].astype(f32)).astype(bf16)

        @pl.when(z < zn - 1)
        def _():
            tstage[b] = (tstage[b].astype(f32) + rl[i, z].astype(f32)).astype(bf16)

        pltpu.make_async_copy(tstage.at[b], tok_slice(i), gl.at[8 + b]).start()

    def item_step(s):
        @pl.when(s < CHUNKS)
        def _():
            item_part(s)

        @pl.when((s >= 1) & (s < CHUNKS + 1))
        def _():
            item_pair(s - 1)

        right_at = s - 1 - z

        @pl.when((z > 0) & (right_at >= 0) & (right_at < CHUNKS))
        def _():
            item_right(right_at)

        left_at = s - zn + z

        @pl.when((z < zn - 1) & (left_at >= 0) & (left_at < CHUNKS))
        def _():
            item_left(left_at)

        @pl.when((s >= zn) & (s < CHUNKS + zn))
        def _():
            item_final(s - zn)

    def gx_part(p):
        return gx_land.at[p]

    def piece_work(p):
        for z_of in range(zn):
            arrived(cot(z_of, 1 - c, p), dt_cr.at[p, z_of])
        load = pltpu.make_async_copy(
            cot_all.at[:, :, :, pl.ds(pl.multiple_of(p * width, width), width)], dtv, loc.at[3]
        )
        load.start()

        @pl.when(p >= 1)
        def _():
            grad_pair(p - 1)

        load.wait()

        def out_half(h, carry):
            lanes = pl.ds(pl.multiple_of(h * chunk, chunk), chunk)
            rows = dtv[:, :, :, lanes].reshape(8 * POOLED, chunk)
            gos[p, :, lanes] = dot(actv[...], rows, 0, 0).astype(bf16)
            return carry

        def hidden_half(h, carry):
            lanes = pl.ds(pl.multiple_of(h * chunk, chunk), chunk)
            rows = dtv[:, :, :, lanes].reshape(8 * POOLED, chunk)
            weights = wo[:, pl.ds(pl.multiple_of(p * width + h * chunk, chunk), chunk)]
            dpre[...] += dot(rows, weights, 1, 1)
            return carry

        lax.fori_loop(0, 2, out_half, 0)

        @pl.when(jnp.logical_not(own))
        def _():
            start(gos.at[p], gx_land.at[p], gx_s.at[p], gx_r.at[p], x_peer)

        lax.fori_loop(0, 2, hidden_half, 0)

    def gout_slice(half, p):
        return gout_out.at[half, :, pl.ds(pl.multiple_of(p * width, width), width)]

    def grad_pair(p):
        @pl.when(own)
        def _():
            arrived(gx_land.at[p], gx_r.at[p])
            for h in range(2):
                half = pl.ds(h * width // 2, width // 2)
                load = pltpu.make_async_copy(gx_land.at[p, :, half], land, loc.at[4])
                load.start()
                load.wait()
                gos[p, :, half] = (gos[p, :, half].astype(f32) + land[...].astype(f32)).astype(bf16)
            mine = gout_slice(y, p)
            start(gos.at[p], mine, gy_s.at[p], gy_r.at[p], y_peer)
            start(gos.at[p], mine, gc_s.at[p, 0], gc_r.at[p, 0], twin)
            pltpu.make_async_copy(gos.at[p], mine, gl.at[p]).start()

    def grad_last(p):
        other = gout_slice(1 - y, p)
        mine = gout_slice(y, p)

        @pl.when(own)
        def _():
            arrived(other, gy_r.at[p])
            start(other, other, gc_s.at[p, 1], gc_r.at[p, 1], twin)

    def grad_done(p):
        other = gout_slice(1 - y, p)
        mine = gout_slice(y, p)

        @pl.when(own)
        def _():
            left_here(gos.at[p], gy_s.at[p])
            left_here(gos.at[p], gc_s.at[p, 0])
            left_here(other, gc_s.at[p, 1])
            pltpu.make_async_copy(gos.at[p], mine, gl.at[p]).wait()

        @pl.when(jnp.logical_not(own))
        def _():
            left_here(gos.at[p], gx_s.at[p])
            arrived(mine, gc_r.at[p, 0])
            arrived(other, gc_r.at[p, 1])

    def main_step(s, carry):
        @pl.when(s < CHUNKS // 2)
        def _():
            for half in range(2):
                j = 2 * s + half
                arrived(wo.at[:, pl.ds(pl.multiple_of(j * chunk, chunk), chunk)], sw_r.at[1 + j])

        item_step(s)

        @pl.when(s < PIECES)
        def _():
            cot_hop(s, 2)

        @pl.when((s >= 1) & (s < PIECES + 1))
        def _():
            cot_hop(s - 1, 3)

        @pl.when((s >= 2) & (s < PIECES + 2))
        def _():
            piece_work(s - 2)

        return carry

    main_steps = PIECES + 2
    lax.fori_loop(0, main_steps, main_step, 0)

    def dh_tile(t, carry):
        rows = pl.ds(pl.multiple_of(t * POOLED, POOLED), POOLED)
        half = lax.div(t, 4)
        place = pl.ds(pl.multiple_of((t - 4 * half) * POOLED, POOLED), POOLED)
        ylo[place, pl.ds(pl.multiple_of(half * 512, 512), 512)] = (
            dpre[rows, :] * slope[rows, :].astype(f32)
        ).astype(bf16)
        return carry

    lax.fori_loop(0, 8, dh_tile, 0)
    for h in range(2):
        d_part = dot(ylo[:, 512 * h : 512 * h + 512], wi[...], 1, 1).astype(bf16)
        dtv[2 * h : 2 * h + 2] = d_part.reshape(2, 2, POOLED, 1024)
    start(dtv.at[:, 1 - c], dr, d_cs.at[0], d_cr.at[0], twin)
    grad_pair(PIECES - 1)
    gis[...] = (
        dot(qs[0:4].reshape(4 * POOLED, 1024), ylo[:, 0:512], 0, 0)
        + dot(qs[4:8].reshape(4 * POOLED, 1024), ylo[:, 512:1024], 0, 0)
    ).astype(bf16)

    @pl.when(jnp.logical_not(own))
    def _():
        start(gis, gi_land, gx_s.at[PIECES], gx_r.at[PIECES], x_peer)

    arrived(dr, d_cr.at[0])

    def pair_rows(d, carry):
        dtv[d, c] = (dtv[d, c].astype(f32) + dr[d].astype(f32)).astype(bf16)
        return carry

    lax.fori_loop(0, zn, pair_rows, 0)
    for k in range(1, zn):
        d = z_at(k)
        start(dtv.at[d, c], dz.at[k - 1], d_zs.at[k - 1], d_zr.at[k - 1], z_dev(d))

    for p in range(PIECES):
        grad_last(p)
    total = dtv[z, c].astype(f32)
    for k in range(1, zn):
        arrived(dz.at[k - 1], d_zr.at[k - 1])
        total = total + dz[k - 1].astype(f32)

    def widened_back(d_rows, normed, gain, inv):
        dn = d_rows * gain
        return (
            inv
            * (
                dn
                - jnp.mean(dn, axis=1, keepdims=True)
                - normed * jnp.mean(dn * normed, axis=1, keepdims=True)
            )
        ).astype(bf16)

    def pack_small(t, d_gain):
        for k in range(4):
            sm[t, 9 + k : 10 + k, :] = d_gain[:, 256 * k : 256 * k + 256]
        sm[t, 13:16, :] = jnp.zeros((3, 256), f32)

    normed_b = norm_b[...]
    d_gain_b = jnp.sum(total * normed_b, axis=0, keepdims=True)
    gain_b = tw[1, 9:10, :]
    wr_b, we_b = block_weights(1)
    dw_b = widened_back(total, normed_b, gain_b, inv_b[:, 0:1])
    wgs[1, 1] = dot(nar_b[...], dw_b, 0, 0).astype(bf16)
    spatial_b = spa_b[...]
    d_spatial_b = dot(dw_b, we_b, 1, 1) * silu_slope(spatial_b)
    reduced_b = red_b[...]
    sig_b = jax.nn.sigmoid(reduced_b)
    d_act_b, d_taps_b = conv_backward(
        d_spatial_b, reduced_b * sig_b, tap_rows(1, pl.ds(0, 256)), POOL, edge_masks(POOL, 256)
    )
    d_red_b = (d_act_b * (sig_b * (1.0 + reduced_b * (1.0 - sig_b)))).astype(bf16)
    wgs[1, 0] = dot(d_red_b, poolv[...].astype(bf16), 0, 0).astype(bf16)
    for k in range(9):
        sm[1, k : k + 1, :] = d_taps_b[k]
    pack_small(1, d_gain_b)
    d_pool = total + dot(d_red_b, wr_b, 1, 0)

    def share_core(t):
        start(wgs.at[t, 1 - c], wgc.at[t], gr_s.at[t, 0], gr_r.at[t, 0], twin)
        start(sm.at[t], smc.at[t], gr_s.at[t, 1], gr_r.at[t, 1], twin)

    def share_x(t):
        arrived(wgc.at[t], gr_r.at[t, 0])
        arrived(smc.at[t], gr_r.at[t, 1])
        for i in range(8):
            rows = pl.ds(32 * i, 32)
            xs[t, i % 2, i // 2] = (
                wgs[t, c, rows, :].astype(f32) + wgc[t, rows, :].astype(f32)
            ).astype(bf16)
        left_here(sm.at[t], gr_s.at[t, 1])
        sm[t] = sm[t] + smc[t]
        start(xs.at[t, 1 - x], xr.at[t], gr_s.at[t, 2], gr_r.at[t, 2], x_peer)
        start(sm.at[t], smx.at[t], gr_s.at[t, 3], gr_r.at[t, 3], x_peer)

    def share_z(t):
        arrived(xr.at[t], gr_r.at[t, 2])
        arrived(smx.at[t], gr_r.at[t, 3])
        zs[t] = (xs[t, x].astype(f32) + xr[t].astype(f32)).astype(bf16)
        left_here(sm.at[t], gr_s.at[t, 3])
        smz[t, z] = sm[t] + smx[t]
        for k in range(1, zn):
            d = z_at(k)
            start(zs.at[t, d], zr.at[t, k - 1], gr_s.at[t, 3 + k], gr_r.at[t, 3 + k], z_dev(d))
            start(
                smz.at[t, z], smz.at[t, z], gr_s.at[t, 6 + k], gr_r.at[t, 6 + k], z_dev(d)
            )

    def share_y(t):
        total_rows = zs[t, z].astype(f32)
        for k in range(1, zn):
            arrived(zr.at[t, k - 1], gr_r.at[t, 3 + k])
            total_rows = total_rows + zr[t, k - 1].astype(f32)
            arrived(smz.at[t, z_at(-k)], gr_r.at[t, 6 + k])
        ys[t] = total_rows.astype(bf16)
        sm[t] = (smz[t, 0] + smz[t, 1]) + (smz[t, 2] + smz[t, 3])
        start(ys.at[t], yr.at[t], gr_s.at[t, 10], gr_r.at[t, 10], y_peer)
        start(sm.at[t], smy.at[t], gr_s.at[t, 11], gr_r.at[t, 11], y_peer)

    def share_twin(t):
        arrived(yr.at[t], gr_r.at[t, 10])
        arrived(smy.at[t], gr_r.at[t, 11])
        gfin[t, c] = ys[t].astype(f32) + yr[t].astype(f32)
        gsml_out[t] = sm[t] + smy[t]
        start(gfin.at[t, c], gfin.at[t, c], gr_s.at[t, 12], gr_r.at[t, 12], twin)

    def share_done(t):
        arrived(gfin.at[t, 1 - c], gr_r.at[t, 12])
        gblk_out[t] = gfin[t]
        left_here(wgs.at[t, 1 - c], gr_s.at[t, 0])
        left_here(xs.at[t, 1 - x], gr_s.at[t, 2])
        for k in range(1, zn):
            left_here(zs.at[t, 0], gr_s.at[t, 3 + k])
            left_here(smz.at[t, z], gr_s.at[t, 6 + k])
        left_here(ys.at[t], gr_s.at[t, 10])
        left_here(sm.at[t], gr_s.at[t, 11])
        left_here(gfin.at[t, c], gr_s.at[t, 12])

    share_core(1)

    high, low = split_low(d_pool)
    dy[...] = dot(pp[...], high, 0, 0) + dot(pp[...], low, 0, 0)
    gain_a = tw[0, 9:10, :]
    wr_a, we_a = block_weights(0)

    def back_tile(t, d_gain):
        rows = pl.ds(pl.multiple_of(t * TILE, TILE), TILE)
        d_rows = dy[rows, :]
        normed = norm_a[rows, :].astype(f32)
        yhi[rows, :] = widened_back(d_rows, normed, gain_a, inv_a[rows, 0:1])
        return d_gain + jnp.sum(d_rows * normed, axis=0, keepdims=True)

    d_gain_a = lax.fori_loop(0, CELLS // TILE, back_tile, jnp.zeros((1, 1024), f32))
    wgs[0, 1] = dot(nar_a[...], yhi[...], 0, 0).astype(bf16)
    share_x(1)
    spa_a[...] = dot(yhi[...], we_a, 1, 1) * silu_slope(spa_a[...])

    def conv_back_half_a(h, carry):
        lanes = lanes_of(h)
        reduced = red_a[:, lanes]
        sig = jax.nn.sigmoid(reduced)
        mask = cell_mask()
        d_act, d_taps = conv_backward(
            spa_a[:, lanes], reduced * sig * mask, tap_rows(0, lanes), GRID, edge_masks(GRID, 128)
        )
        dlow[:, lanes] = (d_act * mask * (sig * (1.0 + reduced * (1.0 - sig)))).astype(bf16)
        for k in range(9):
            sm[0, k : k + 1, lanes] = d_taps[k]
        return carry

    lax.fori_loop(0, 2, conv_back_half_a, 0)
    wgs[0, 0] = dot(dlow[...], xp[...], 0, 0).astype(bf16)
    pack_small(0, d_gain_a)
    share_core(0)
    share_z(1)
    dy[...] += dot(dlow[...], wr_a, 1, 0)
    store_dpat = pltpu.make_async_copy(dy, dpat_out, loc.at[5])
    store_dpat.start()
    share_x(0)
    share_y(1)

    def gin_slice(half):
        return gin_out.at[half]

    @pl.when(own)
    def _():
        arrived(gi_land, gx_r.at[PIECES])
        for h in range(2):
            rows = pl.ds(512 * h, 512)
            load = pltpu.make_async_copy(gi_land.at[rows], land, loc.at[4])
            load.start()
            load.wait()
            gis[rows, :] = (gis[rows, :].astype(f32) + land[...].astype(f32)).astype(bf16)
        start(gis, gin_slice(y), gy_s.at[PIECES], gy_r.at[PIECES], y_peer)
        start(gis, gin_slice(y), gc_s.at[PIECES, 0], gc_r.at[PIECES, 0], twin)
        pltpu.make_async_copy(gis, gin_slice(y), gl.at[PIECES]).start()

    share_z(0)
    share_twin(1)

    def tail_step(s, carry):
        item_step(s)
        return carry

    lax.fori_loop(main_steps, CHUNKS + zn, tail_step, 0)
    share_y(0)
    share_twin(0)

    @pl.when(own)
    def _():
        arrived(gin_slice(1 - y), gy_r.at[PIECES])
        start(gin_slice(1 - y), gin_slice(1 - y), gc_s.at[PIECES, 1], gc_r.at[PIECES, 1], twin)

    share_done(1)
    share_done(0)
    for p in range(PIECES):
        grad_done(p)

    @pl.when(own)
    def _():
        left_here(gis, gy_s.at[PIECES])
        left_here(gis, gc_s.at[PIECES, 0])
        left_here(gin_slice(1 - y), gc_s.at[PIECES, 1])
        pltpu.make_async_copy(gis, gin_slice(y), gl.at[PIECES]).wait()

    @pl.when(jnp.logical_not(own))
    def _():
        left_here(gis, gx_s.at[PIECES])
        arrived(gin_slice(y), gc_r.at[PIECES, 0])
        arrived(gin_slice(1 - y), gc_r.at[PIECES, 1])
        left_here(wi, sw_s.at[0])
        for j in range(CHUNKS):
            left_here(columns(wo, j, chunk), sw_s.at[1 + j])

    store_dpat.wait()
    for b in range(2):
        pltpu.make_async_copy(tstage.at[b], tok_slice(b), gl.at[8 + b]).wait()
        left_here(tp.at[b, :, 1 - c], t_cs.at[b])
        for k in range(15):
            left_here(w_part(b, c, 0), w_s.at[b, k])
    for k in range(7):
        left_here(qs.at[0], q_s.at[k])
    left_here(dtv.at[:, 0], d_cs.at[0])
    for k in range(zn - 1):
        left_here(dtv.at[0, 0], d_zs.at[k])
    for p in range(PIECES):
        for z_of in range(zn):
            left_here(cot(0, 0, p), dt_cs.at[p, z_of])
        for hop in range(zn - 1):
            @pl.when((z < zn - 1) & (z >= hop))
            def _():
                left_here(cot(0, 0, p), dt_s.at[p, 0, hop])

            @pl.when((z > 0) & (z + hop <= zn - 1))
            def _():
                left_here(cot(0, 0, p), dt_s.at[p, 1, hop])

    def drain_items(i, carry):
        for d in range(zn):
            @pl.when(z != d)
            def _():
                left_here(ps.at[0, 0], t_s.at[i, d])
        return carry

    lax.fori_loop(0, CHUNKS, drain_items, 0)


def layer_call(patches, grid_sizes, pack, w_in, w_out, d_tokens):
    any_space = pl.BlockSpec(memory_space=pl.ANY)
    vmem = pl.BlockSpec(memory_space=pltpu.VMEM)
    smem = pl.BlockSpec(memory_space=pltpu.SMEM)
    shape = jax.ShapeDtypeStruct
    width = w_out.shape[1] // PIECES
    chunk = w_out.shape[1] // CHUNKS
    out_shape = (
        shape((POOLED, 4096), bf16),
        shape((CELLS, 1024), f32),
        shape((2, 512, 4096), bf16),
        shape((2, 1024, 512), bf16),
        shape((2, 2, 32, 1024), f32),
        shape((2, 16, 256), f32),
        shape((4, 2, POOLED, 4096), bf16),
        shape((PIECES, 512, width), bf16),
        shape((1024, 512), bf16),
    )
    dma = pltpu.SemaphoreType.DMA
    scratch = [
        pltpu.VMEM((CELLS, 1024), bf16),
        pltpu.VMEM((2, 8, 80, 1024), bf16),
        pltpu.VMEM((CELLS, 256), f32),
        pltpu.VMEM((CELLS, 256), f32),
        pltpu.VMEM((CELLS, 256), bf16),
        pltpu.VMEM((CELLS, 1024), bf16),
        pltpu.VMEM((CELLS, 128), f32),
        pltpu.VMEM((CELLS, 1024), bf16),
        pltpu.VMEM((CELLS, 1024), bf16),
        pltpu.VMEM((CELLS, 1024), f32),
        pltpu.VMEM((CELLS, 256), bf16),
        pltpu.VMEM((POOLED, CELLS), bf16),
        pltpu.VMEM((2, 16, 1024), f32),
        pltpu.VMEM((POOLED, 1024), f32),
        pltpu.VMEM((POOLED, 256), f32),
        pltpu.VMEM((POOLED, 256), f32),
        pltpu.VMEM((POOLED, 256), bf16),
        pltpu.VMEM((POOLED, 1024), f32),
        pltpu.VMEM((POOLED, 128), f32),
        pltpu.VMEM((1024, 512), bf16),
        pltpu.VMEM((512, 4096), bf16),
        pltpu.VMEM((8, POOLED, 1024), bf16),
        pltpu.VMEM((8 * POOLED, 512), bf16),
        pltpu.VMEM((8 * POOLED, 512), bf16),
        pltpu.VMEM((8 * POOLED, 512), f32),
        pltpu.VMEM((4, 2, POOLED, width), bf16),
        pltpu.VMEM((2, 4, 2, POOLED, chunk), bf16),
        pltpu.VMEM((2, 4, POOLED, chunk), bf16),
        pltpu.VMEM((CHUNKS, 4, POOLED, chunk), bf16),
        pltpu.VMEM((CHUNKS, 5, POOLED, chunk), bf16),
        pltpu.VMEM((2, POOLED, chunk), bf16),
        pltpu.VMEM((4, POOLED, 1024), bf16),
        pltpu.VMEM((3, POOLED, 1024), bf16),
        pltpu.VMEM((PIECES, 512, width), bf16),
        pltpu.VMEM((1024, 512), bf16),
        pltpu.VMEM((512, width // 2), bf16),
        pltpu.VMEM((2, 2, 256, 1024), bf16),
        pltpu.VMEM((2, 256, 1024), bf16),
        pltpu.VMEM((2, 2, 4, 32, 1024), bf16),
        pltpu.VMEM((2, 4, 32, 1024), bf16),
        pltpu.VMEM((2, 4, 32, 1024), bf16),
        pltpu.VMEM((2, 3, 32, 1024), bf16),
        pltpu.VMEM((2, 32, 1024), bf16),
        pltpu.VMEM((2, 32, 1024), bf16),
        pltpu.VMEM((2, 16, 256), f32),
        pltpu.VMEM((2, 16, 256), f32),
        pltpu.VMEM((2, 16, 256), f32),
        pltpu.VMEM((2, 4, 16, 256), f32),
        pltpu.VMEM((2, 16, 256), f32),
        pltpu.VMEM((2, 2, 32, 1024), f32),
        dma((6,)),
        dma((2, 15)),
        dma((2, 4)),
        dma((2, 4)),
        dma((2, 8)),
        dma((1 + CHUNKS,)),
        dma((1 + CHUNKS,)),
        dma((7,)),
        dma((4,)),
        dma((4,)),
        dma((PIECES, 2, 3)),
        dma((PIECES, 2, 3)),
        dma((PIECES, 4)),
        dma((PIECES, 4)),
        dma((2,)),
        dma((2,)),
        dma((CHUNKS, 4)),
        dma((CHUNKS, 5)),
        pltpu.SemaphoreType.REGULAR,
        dma((1,)),
        dma((1,)),
        dma((3,)),
        dma((3,)),
        dma((PIECES + 1,)),
        dma((PIECES + 1,)),
        dma((PIECES + 1,)),
        dma((PIECES + 1,)),
        dma((PIECES + 1, 2)),
        dma((PIECES + 1, 2)),
        dma((10,)),
        dma((2, 13)),
        dma((2, 13)),
    ]
    return pl.pallas_call(
        layer_kernel,
        out_shape=out_shape,
        in_specs=[any_space, smem, any_space, any_space, any_space, any_space],
        out_specs=(any_space, any_space, any_space, any_space, vmem, vmem, any_space, any_space, any_space),
        scratch_shapes=scratch,
        compiler_params=pltpu.CompilerParams(
            collective_id=0, has_side_effects=True, vmem_limit_bytes=VMEM_BYTES
        ),
    )(patches, grid_sizes, pack, w_in, w_out, d_tokens)


VMEM_BYTES = 64 * 1024 * 1024


def small_pack(taps, gain, mp_at):
    shards = 8
    lane = lax.broadcasted_iota(jnp.int32, (9, 1024), 1)
    spread = jnp.tile(taps, (1, 1024 // taps.shape[1]))
    rows = jnp.where((lane // taps.shape[1]) == mp_at, spread, jnp.zeros_like(spread))
    lane = lax.broadcasted_iota(jnp.int32, (1, 1024), 1)
    spread = jnp.tile(gain[None, :], (1, shards))
    gain_row = jnp.where((lane // gain.shape[0]) == mp_at, spread, jnp.zeros_like(spread))
    return jnp.concatenate([rows, gain_row, jnp.zeros((6, 1024), taps.dtype)], axis=0)


def fast_body(
    patches, grid_sizes, w_reduce_a, taps_a, w_expand_a, gain_a,
    w_reduce_b, taps_b, w_expand_b, gain_b, w_in, w_out, d_tokens,
):
    mp_at = lax.axis_index("mp")
    pack = jnp.stack(
        [
            jnp.concatenate([w_reduce_a.T, small_pack(taps_a, gain_a, mp_at), w_reduce_b.T], axis=0),
            jnp.concatenate([w_expand_a, small_pack(taps_b, gain_b, mp_at), w_expand_b], axis=0),
        ]
    )
    results = layer_call(patches, grid_sizes, pack, w_in, w_out, d_tokens)
    tokens, d_patches, gout, gin, gblk, gsml = results[:6]
    taps_grads = lax.dynamic_slice(gsml, (0, 0, 32 * mp_at), (2, 9, 32))
    gain_grads = lax.dynamic_slice(gsml[:, 9:13].reshape(2, 1024), (0, 128 * mp_at), (2, 128))
    return (
        tokens,
        d_patches,
        gblk[0, 0].T,
        taps_grads[0],
        gblk[0, 1],
        gain_grads[0],
        gblk[1, 0].T,
        taps_grads[1],
        gblk[1, 1],
        gain_grads[1],
        gin[0].astype(f32) + gin[1].astype(f32),
        gout[0].astype(f32) + gout[1].astype(f32),
    )


def solution(mesh):
    in_specs = (
        P(("dp", "mp"), None),
        P(("dp", "mp")),
        P(None, "mp"),
        P(None, "mp"),
        P("mp", None),
        P("mp"),
        P(None, "mp"),
        P(None, "mp"),
        P("mp", None),
        P("mp"),
        P(None, "mp"),
        P("mp", None),
        P(("dp", "mp"), None),
    )
    out_specs = (
        P(("dp", "mp"), None),
        P(("dp", "mp"), None),
        P(None, "mp"),
        P(None, "mp"),
        P("mp", None),
        P("mp"),
        P(None, "mp"),
        P(None, "mp"),
        P("mp", None),
        P("mp"),
        P(None, "mp"),
        P("mp", None),
    )
    fits = mesh.shape["dp"] == 4 and mesh.shape["mp"] == 8
    return jax.shard_map(fast_body if fits else body, mesh=mesh, in_specs=in_specs, out_specs=out_specs, check_vma=False)
```

```python
import jax
import jax.numpy as jnp
from jax import lax
from jax.experimental import pallas as pl
from jax.experimental.pallas import tpu as pltpu
from jax.sharding import PartitionSpec as P

GRID = 24
SMALL_GRID = 16
POOL = 12


epsilon = 1e-05
highest = lax.Precision.HIGHEST
root_half = 0.7071067811865476
inv_root_tau = 0.3989422804014327


def silu_slope(values):
    sigmoid = jax.nn.sigmoid(values)
    return sigmoid * (1.0 + values * (1.0 - sigmoid))


def gelu_exact(values):
    return 0.5 * values * (1.0 + lax.erf(values * root_half))


def gelu_slope(values):
    return (
        0.5 * (1.0 + lax.erf(values * root_half))
        + values * jnp.exp(-0.5 * values * values) * inv_root_tau
    )


def outer_rows(left, right):
    return lax.dot_general(
        left, right, (((0,), (0,)), ((), ())), preferred_element_type=jnp.float32
    )


def times_trans(left, right):
    return lax.dot_general(
        left, right, (((1,), (1,)), ((), ())), preferred_element_type=jnp.float32
    )


def map_padding(ndims):
    return [(0, 0)] * (ndims - 3) + [(1, 1), (1, 1), (0, 0)]


def depthwise(feature_map, tap_weights):
    extent = feature_map.shape[-2]
    padded = jnp.pad(feature_map, map_padding(feature_map.ndim))
    result = jnp.zeros_like(feature_map)
    for tap_row in range(3):
        for tap_col in range(3):
            result = (
                result
                + padded[..., tap_row : tap_row + extent, tap_col : tap_col + extent, :]
                * tap_weights[3 * tap_row + tap_col]
            )
    return result


def depthwise_back(upstream, feature_map, tap_weights):
    extent = upstream.shape[-2]
    upstream_pad = jnp.pad(upstream, map_padding(upstream.ndim))
    feature_pad = jnp.pad(feature_map, map_padding(feature_map.ndim))
    d_feature = jnp.zeros_like(upstream)
    tap_grads = []
    leading = tuple(range(upstream.ndim - 1))
    for tap_row in range(3):
        for tap_col in range(3):
            d_feature = (
                d_feature
                + upstream_pad[
                    ..., 2 - tap_row : 2 - tap_row + extent, 2 - tap_col : 2 - tap_col + extent, :
                ]
                * tap_weights[3 * tap_row + tap_col]
            )
            shifted = feature_pad[..., tap_row : tap_row + extent, tap_col : tap_col + extent, :]
            tap_grads.append(jnp.sum(shifted * upstream, axis=leading))
    return (d_feature, jnp.stack(tap_grads))


def block_forward(feature_rows, low_rows, weights_set, extent):
    w_reduce, tap_weights, w_expand, norm_gain = weights_set
    channels = w_reduce.shape[1]
    row_count = feature_rows.shape[0]
    reduced = jnp.dot(low_rows, w_reduce, preferred_element_type=jnp.float32)
    activated = jax.nn.silu(reduced).reshape(-1, extent, extent, channels)
    spatial = depthwise(activated, tap_weights.astype(jnp.float32)).reshape(row_count, channels)
    narrow = jax.nn.silu(spatial).astype(jnp.bfloat16)
    widened = jnp.dot(narrow, w_expand, preferred_element_type=jnp.float32)
    centred = widened - jnp.mean(widened, axis=1, keepdims=True)
    inv_scale = lax.rsqrt(jnp.mean(centred * centred, axis=1, keepdims=True) + epsilon)
    normed = centred * inv_scale
    result = feature_rows + normed * norm_gain.astype(jnp.float32)
    return (result, (reduced, activated, spatial, narrow, normed, inv_scale))


def block_backward(d_result, low_rows, weights_set, saved):
    w_reduce, tap_weights, w_expand, norm_gain = weights_set
    reduced, activated, spatial, narrow, normed, inv_scale = saved
    d_gain = jnp.sum(d_result * normed, axis=0)
    d_normed = d_result * norm_gain.astype(jnp.float32)
    d_widened = inv_scale * (
        d_normed
        - jnp.mean(d_normed, axis=1, keepdims=True)
        - normed * jnp.mean(d_normed * normed, axis=1, keepdims=True)
    )
    d_widened = d_widened.astype(jnp.bfloat16)
    grad_expand = outer_rows(narrow, d_widened)
    d_spatial = times_trans(d_widened, w_expand) * silu_slope(spatial)
    d_activated, grad_taps = depthwise_back(
        d_spatial.reshape(activated.shape), activated, tap_weights.astype(jnp.float32)
    )
    d_reduced = (d_activated.reshape(reduced.shape) * silu_slope(reduced)).astype(jnp.bfloat16)
    grad_reduce = outer_rows(low_rows, d_reduced)
    d_rows = d_result + times_trans(d_reduced, w_reduce)
    return (d_rows, (grad_reduce, grad_taps, grad_expand, d_gain))


def crop_rows(pixels, extent):
    features = pixels.shape[-1]
    return pixels.reshape(GRID, GRID, features)[:extent, :extent].reshape(extent * extent, features)


def widen_grid(values, extent):
    features = values.shape[-1]
    return jnp.pad(
        values.reshape(extent, extent, features), ((0, GRID - extent), (0, GRID - extent), (0, 0))
    )


def first_forward(weights_set, extent):

    def compute(pixels):
        cropped = crop_rows(pixels, extent)
        result, unused = block_forward(cropped.astype(jnp.float32), cropped, weights_set, extent)
        return widen_grid(result, extent)

    return compute


def first_backward(weights_set, extent):

    def compute(pixels, upstream):
        cropped = crop_rows(pixels, extent)
        sliced = crop_rows(upstream, extent)
        unused, saved = block_forward(cropped.astype(jnp.float32), cropped, weights_set, extent)
        d_rows, grads = block_backward(sliced, cropped, weights_set, saved)
        return (widen_grid(d_rows, extent).reshape(GRID * GRID, -1), grads)

    return compute


def pool_table(grid_side):
    bin_index = lax.iota(jnp.int32, POOL)
    bin_lower = bin_index * grid_side // POOL
    bin_upper = ((bin_index + 1) * grid_side + POOL - 1) // POOL
    cell_index = lax.iota(jnp.int32, GRID)
    inside = (cell_index[None, :] >= bin_lower[:, None]) & (
        cell_index[None, :] < bin_upper[:, None]
    )
    weights = jnp.where(inside, 1.0, 0.0) / (bin_upper - bin_lower)[:, None]
    return weights.astype(jnp.float32)


def body(
    patches,
    grid_sizes,
    w_reduce_a,
    taps_a,
    w_expand_a,
    gain_a,
    w_reduce_b,
    taps_b,
    w_expand_b,
    gain_b,
    w_in,
    w_out,
    d_tokens,
):
    gathered = (
        lax.all_gather(w_reduce_a, "mp", axis=1, tiled=True),
        lax.all_gather(taps_a, "mp", axis=1, tiled=True),
        lax.all_gather(w_expand_a, "mp", axis=0, tiled=True),
        lax.all_gather(gain_a, "mp", axis=0, tiled=True),
        lax.all_gather(w_reduce_b, "mp", axis=1, tiled=True),
        lax.all_gather(taps_b, "mp", axis=1, tiled=True),
        lax.all_gather(w_expand_b, "mp", axis=0, tiled=True),
        lax.all_gather(gain_b, "mp", axis=0, tiled=True),
    )
    first_set = gathered[0:4]
    second_set = gathered[4:8]
    features = patches.shape[1]
    pictures = patches.reshape(-1, GRID * GRID, features)
    picture_count = pictures.shape[0]
    tables = jax.vmap(pool_table)(grid_sizes)

    def forward_one(element):
        pixels, grid_side, pool_weights = element
        result = lax.cond(
            grid_side == GRID,
            first_forward(first_set, GRID),
            first_forward(first_set, SMALL_GRID),
            pixels,
        )
        return jnp.einsum("ia,jb,abd->ijd", pool_weights, pool_weights, result, precision=highest)

    pooled = lax.map(forward_one, (pictures, grid_sizes, tables))
    pooled_rows = pooled.reshape(picture_count * POOL * POOL, features)
    pooled_low = pooled_rows.astype(jnp.bfloat16)
    mixed_rows, second_saved = block_forward(pooled_rows, pooled_low, second_set, POOL)
    queries = mixed_rows.astype(jnp.bfloat16)
    hidden = jnp.dot(
        lax.all_gather(queries, "mp", axis=0, tiled=True), w_in, preferred_element_type=jnp.float32
    )
    active = gelu_exact(hidden).astype(jnp.bfloat16)
    tokens = lax.psum_scatter(
        jnp.dot(active, w_out, preferred_element_type=jnp.float32).astype(jnp.bfloat16),
        "mp",
        scatter_dimension=0,
        tiled=True,
    )
    piece = lax.all_gather(d_tokens, "mp", axis=0, tiled=True)
    d_part = (times_trans(piece, w_out) * gelu_slope(hidden)).astype(jnp.bfloat16)
    grad_out_sum = outer_rows(active, piece)
    d_hidden = d_part
    d_part = d_hidden
    grad_in_part = outer_rows(lax.all_gather(queries, "mp", axis=0, tiled=True), d_part)
    d_part = d_hidden
    d_mixed = lax.psum_scatter(times_trans(d_part, w_in), "mp", scatter_dimension=0, tiled=True)
    d_pooled, second_grads = block_backward(d_mixed, pooled_low, second_set, second_saved)
    d_pooled = d_pooled.reshape(picture_count, POOL, POOL, features)

    def backward_one(totals, element):
        pixels, grid_side, pool_weights, upstream = element
        d_grid = jnp.einsum(
            "ia,jb,ijd->abd", pool_weights, pool_weights, upstream, precision=highest
        )
        d_pixels, grads = lax.cond(
            grid_side == GRID,
            first_backward(first_set, GRID),
            first_backward(first_set, SMALL_GRID),
            pixels,
            d_grid,
        )
        return (
            tuple((total_part + grad_part for total_part, grad_part in zip(totals, grads))),
            d_pixels,
        )

    zero_grads = tuple((jnp.zeros(weight.shape, jnp.float32) for weight in first_set))
    first_grads, d_pictures = lax.scan(
        backward_one, zero_grads, (pictures, grid_sizes, tables, d_pooled)
    )
    d_patches = d_pictures.reshape(-1, features)
    shards = (
        lax.psum_scatter(
            first_grads[0].astype(jnp.bfloat16), "mp", scatter_dimension=1, tiled=True
        ).astype(jnp.float32),
        lax.psum_scatter(
            first_grads[1].astype(jnp.bfloat16), "mp", scatter_dimension=1, tiled=True
        ).astype(jnp.float32),
        lax.psum_scatter(
            first_grads[2].astype(jnp.bfloat16), "mp", scatter_dimension=0, tiled=True
        ).astype(jnp.float32),
        lax.psum_scatter(
            first_grads[3].astype(jnp.bfloat16), "mp", scatter_dimension=0, tiled=True
        ).astype(jnp.float32),
        lax.psum_scatter(
            second_grads[0].astype(jnp.bfloat16), "mp", scatter_dimension=1, tiled=True
        ).astype(jnp.float32),
        lax.psum_scatter(
            second_grads[1].astype(jnp.bfloat16), "mp", scatter_dimension=1, tiled=True
        ).astype(jnp.float32),
        lax.psum_scatter(
            second_grads[2].astype(jnp.bfloat16), "mp", scatter_dimension=0, tiled=True
        ).astype(jnp.float32),
        lax.psum_scatter(
            second_grads[3].astype(jnp.bfloat16), "mp", scatter_dimension=0, tiled=True
        ).astype(jnp.float32),
    )
    summed = (
        lax.psum(shards[0].astype(jnp.bfloat16), "dp").astype(jnp.float32),
        lax.psum(shards[1].astype(jnp.bfloat16), "dp").astype(jnp.float32),
        lax.psum(shards[2].astype(jnp.bfloat16), "dp").astype(jnp.float32),
        lax.psum(shards[3].astype(jnp.bfloat16), "dp").astype(jnp.float32),
        lax.psum(shards[4].astype(jnp.bfloat16), "dp").astype(jnp.float32),
        lax.psum(shards[5].astype(jnp.bfloat16), "dp").astype(jnp.float32),
        lax.psum(shards[6].astype(jnp.bfloat16), "dp").astype(jnp.float32),
        lax.psum(shards[7].astype(jnp.bfloat16), "dp").astype(jnp.float32),
        lax.psum(grad_in_part.astype(jnp.bfloat16), "dp").astype(jnp.float32),
        lax.psum(grad_out_sum.astype(jnp.bfloat16), "dp").astype(jnp.float32),
    )
    return (
        tokens,
        d_patches,
        summed[0],
        summed[1],
        summed[2],
        summed[3],
        summed[4],
        summed[5],
        summed[6],
        summed[7],
        summed[8],
        summed[9],
    )


bf16 = jnp.bfloat16
f32 = jnp.float32
MESH = pl.DeviceIdType.MESH
CELLS = GRID * GRID
POOLED = POOL * POOL
TILE = 96
PIECES = 4
CHUNKS = 8


def dot(left, right, left_dim, right_dim):
    return lax.dot_general(
        left, right, (((left_dim,), (right_dim,)), ((), ())), preferred_element_type=f32
    )


def split_low(values):
    high = values.astype(bf16)
    return high, (values - high.astype(f32)).astype(bf16)


def edge_masks(extent, channels):
    cells = extent * extent
    index = lax.broadcasted_iota(jnp.int32, (cells, channels), 0).astype(f32)
    row = jnp.floor((index + 0.5) * (1.0 / extent))
    col = index - row * extent
    one = jnp.ones_like(index)
    zero = jnp.zeros_like(index)
    return (
        jnp.where(row >= 0.5, one, zero),
        jnp.where(row <= extent - 1.5, one, zero),
        jnp.where(col >= 0.5, one, zero),
        jnp.where(col <= extent - 1.5, one, zero),
    )


def conv_forward(act, taps, extent, masks):
    above, below, left, right = masks
    cells = extent * extent
    up = pltpu.roll(act, extent, 0) * above
    down = pltpu.roll(act, cells - extent, 0) * below
    sums = [up * taps[q] + act * taps[3 + q] + down * taps[6 + q] for q in range(3)]
    return (
        sums[1]
        + pltpu.roll(sums[0], 1, 0) * left
        + pltpu.roll(sums[2], cells - 1, 0) * right
    )


def conv_backward(upstream, act, taps, extent, masks):
    above, below, left, right = masks
    cells = extent * extent
    sides = [pltpu.roll(upstream, cells - 1, 0) * right, upstream, pltpu.roll(upstream, 1, 0) * left]
    sums = [
        sides[0] * taps[3 * r] + sides[1] * taps[3 * r + 1] + sides[2] * taps[3 * r + 2]
        for r in range(3)
    ]
    d_act = (
        sums[1]
        + pltpu.roll(sums[0], cells - extent, 0) * below
        + pltpu.roll(sums[2], extent, 0) * above
    )
    acts = [pltpu.roll(act, extent, 0) * above, act, pltpu.roll(act, cells - extent, 0) * below]
    d_taps = [
        jnp.sum(acts[r] * sides[q], axis=0, keepdims=True) for r in range(3) for q in range(3)
    ]
    return d_act, d_taps


def slot_rows(ref):
    slots, rows, columns = ref.shape
    return ref[...].reshape(slots * rows, columns)


def layer_kernel(
    patches_in, side_in, wr_a_in, taps_a_in, we_a_in, gain_a_in, wr_b_in, taps_b_in, we_b_in, gain_b_in,
    w_in_in, w_out_in, cot_in,
    tok_out, dpat_out, gout_out, gin_out, gblk_out, gsml_out, cot_all, gx_land, gi_land,
    xp, gw, gws, red_a, spa_a, nar_a, norm_a, inv_a, yhi, ylo, dy, dlow, pp,
    tw, poolv, red_b, spa_b, nar_b, norm_b, inv_b,
    wi, wo, qs, actv, slope, dpre, dtv, tp, cr, ps, rl, tstage,
    dps, dr, dz, gos, gis, land,
    wgs, wgc, xs, xr, zs, zr, ys, yr, sm, smc, smx, smz, smy, gfin,
    loc, w_s, w_rz, w_rx, w_rc, sw_s, sw_r, q_s, q_rz, q_rc,
    dt_s, dt_r, dt_cs, dt_cr, t_cs, t_cr, t_s, t_r, credit,
    d_cs, d_cr, d_zs, d_zr, gx_s, gx_r, gy_s, gy_r, gc_s, gc_r, gl,
    gr_s, gr_r,
):
    dp_at = lax.axis_index("dp")
    mp_at = lax.axis_index("mp")
    y = lax.div(dp_at, 2)
    c = lax.rem(dp_at, 2)
    z = lax.div(mp_at, 2)
    x = lax.rem(mp_at, 2)
    zn = 4

    def device(x_at, y_at, z_at, c_at):
        return (2 * y_at + c_at, 2 * z_at + x_at)

    twin = device(x, y, z, 1 - c)
    x_peer = device(1 - x, y, z, c)
    cross = device(1 - x, y, z, 1 - c)
    y_peer = device(x, 1 - y, z, c)

    def z_at(step):
        return lax.rem(z + step + zn, zn)

    def z_dev(z_of):
        return device(x, y, z_of, c)

    def remote(src, dst, send, recv, to):
        return pltpu.make_async_remote_copy(
            src_ref=src, dst_ref=dst, send_sem=send, recv_sem=recv, device_id=to, device_id_type=MESH
        )

    def start(src, dst, send, recv, to):
        remote(src, dst, send, recv, to).start()

    def arrived(dst, recv):
        pltpu.make_async_copy(dst, dst, recv).wait()

    def left_here(src, send):
        pltpu.make_async_copy(src, src, send).wait()

    own = x == c

    load_patches = pltpu.make_async_copy(patches_in, xp, loc.at[0])
    me = 2 * z + c
    load_patches.start()

    own_rows = pl.ds(pl.multiple_of(16 * c, 16), 16)
    gw[c, mp_at, 0:16, :] = wr_a_in[own_rows, :]
    gw[c, mp_at, 32:48, :] = wr_b_in[own_rows, :]
    gw[c, mp_at, 16:32, :] = we_a_in[own_rows, :]
    gw[c, mp_at, 48:64, :] = we_b_in[own_rows, :]
    unit = lax.broadcasted_iota(jnp.int32, (32, 256), 0)
    lane = lax.broadcasted_iota(jnp.int32, (32, 256), 1)
    place = 16 * mp_at + jnp.where(unit >= 16, unit + 112, unit)
    spread = jnp.where(lane == place, 1.0, 0.0).astype(bf16)
    gws[c, mp_at] = jnp.zeros((16, 256), f32)

    @pl.when(c == 0)
    def _():
        gws[0, mp_at, 0:9, :] = dot(taps_a_in[...], spread, 1, 0)
        gws[0, mp_at, 9:10, 0:128] = gain_a_in[...].astype(f32).reshape(1, 128)

    @pl.when(c == 1)
    def _():
        gws[1, mp_at, 0:9, :] = dot(taps_b_in[...], spread, 1, 0)
        gws[1, mp_at, 9:10, 0:128] = gain_b_in[...].astype(f32).reshape(1, 128)

    barrier = pltpu.get_barrier_semaphore()
    peers = [twin, x_peer, cross, y_peer] + [z_dev(z_at(k)) for k in range(1, zn)]
    for peer in peers:
        pl.semaphore_signal(barrier, inc=1, device_id=peer, device_id_type=MESH)
    pl.semaphore_wait(barrier, len(peers))

    spans = ((0, 16), (16, 16), (32, 32))

    def w_part(b, core, i):
        if b == 3:
            return gws.at[core, i]
        return gw.at[core, i, pl.ds(spans[b][0], spans[b][1])]

    def w_own(b):
        part = w_part(b, c, mp_at)
        for k in range(1, zn):
            start(part, part, w_s.at[b, k - 1], w_rz.at[b, k], z_dev(z_at(k)))
        start(part, part, w_s.at[b, 3], w_rx.at[b, z], x_peer)
        start(part, part, w_s.at[b, 7], w_rc.at[b, mp_at], twin)

    def w_forward(b):
        for k in range(1, zn):
            z_of = z_at(-k)
            i = 2 * z_of + x
            part = w_part(b, c, i)
            arrived(part, w_rz.at[b, k])
            start(part, part, w_s.at[b, 3 + k], w_rx.at[b, z_of], x_peer)
            start(part, part, w_s.at[b, 7 + k], w_rc.at[b, i], twin)

    def w_over(b):
        for k in range(zn):
            z_of = z_at(-k)
            i = 2 * z_of + 1 - x
            part = w_part(b, c, i)
            arrived(part, w_rx.at[b, z_of])
            start(part, part, w_s.at[b, 11 + k], w_rc.at[b, i], twin)

    def w_finish(b):
        for i in range(8):
            arrived(w_part(b, 1 - c, i), w_rc.at[b, i])

    w_own(0)
    w_own(3)
    w_own(1)
    w_own(2)

    width = cot_in.shape[1] // PIECES

    def cot(z_of, c_of, p):
        return cot_all.at[z_of, c_of, :, pl.ds(pl.multiple_of(p * width, width), width)]

    def cot_mine(p):
        return cot_in.at[:, pl.ds(pl.multiple_of(p * width, width), width)]

    def cot_right(z_of, p, hop):
        mine = cot_mine(p)

        @pl.when(z < zn - 1)
        def _():
            part = cot(z_of, c, p)
            start(mine if hop == 0 else part, part, dt_s.at[p, 0, hop], dt_r.at[p, 0, hop], z_dev(z + 1))

    def cot_left(z_of, p, hop):
        mine = cot_mine(p)

        @pl.when(z > 0)
        def _():
            part = cot(z_of, c, p)
            start(mine if hop == 0 else part, part, dt_s.at[p, 1, hop], dt_r.at[p, 1, hop], z_dev(z - 1))

    def cot_twin(z_of, p):
        part = cot(z_of, c, p)
        start(part, part, dt_cs.at[p, z_of], dt_cr.at[p, z_of], twin)

    def cot_own(p):
        cot_right(z, p, 0)
        cot_left(z, p, 0)
        start(cot_mine(p), cot(z, c, p), dt_cs.at[p, z], dt_cr.at[p, z], twin)

    def cot_hop(p, hop):
        @pl.when(z >= hop)
        def _():
            arrived(cot(z - hop, c, p), dt_r.at[p, 0, hop - 1])
            if hop < zn - 1:
                cot_right(z - hop, p, hop)
            cot_twin(z - hop, p)

        @pl.when(z + hop <= zn - 1)
        def _():
            arrived(cot(z + hop, c, p), dt_r.at[p, 1, hop - 1])
            if hop < zn - 1:
                cot_left(z + hop, p, hop)
            cot_twin(z + hop, p)

    chunk = w_out_in.shape[1] // CHUNKS

    def columns(ref, j, span):
        return ref.at[:, pl.ds(j * span, span)]

    def swap_weights():
        @pl.when(own)
        def _():
            pltpu.make_async_copy(w_in_in, wi, sw_r.at[0]).start()
            for j in range(CHUNKS):
                pltpu.make_async_copy(
                    columns(w_out_in, j, chunk), columns(wo, j, chunk), sw_r.at[1 + j]
                ).start()

        @pl.when(jnp.logical_not(own))
        def _():
            start(w_in_in, wi, sw_s.at[0], sw_r.at[0], cross)
            for j in range(CHUNKS):
                start(
                    columns(w_out_in, j, chunk), columns(wo, j, chunk),
                    sw_s.at[1 + j], sw_r.at[1 + j], cross,
                )

    w_forward(0)
    w_forward(3)
    w_forward(1)
    w_over(0)
    w_over(3)
    for p in range(3):
        cot_own(p)
    w_forward(2)
    w_over(1)
    w_finish(0)
    w_finish(3)

    def reduce_weights(b):
        return gw[:, :, 32 * b : 32 * b + 16, :].reshape(256, 1024)

    def expand_weights(b):
        return gw[:, :, 32 * b + 16 : 32 * b + 32, :].reshape(256, 1024)

    def small_weights(b):
        total = gws[b, 0, 0:9, :]
        for i in range(1, 8):
            total = total + gws[b, i, 0:9, :]
        tw[b, 0:9, 0:256] = total
        for i in range(8):
            tw[b, 9:10, 128 * i : 128 * i + 128] = gws[b, i, 9:10, 0:128]
        return tw[b, 9:10, :]

    def lanes_of(h):
        return pl.ds(pl.multiple_of(h * 128, 128), 128)

    def tap_rows(b, lanes):
        return [tw[b, k : k + 1, lanes] for k in range(9)]

    gain_a = small_weights(0)
    side = side_in[0].astype(f32)
    def cell_mask():
        index = lax.broadcasted_iota(jnp.int32, (CELLS, 128), 0).astype(f32)
        row = jnp.floor((index + 0.5) * (1.0 / GRID))
        col = index - row * GRID
        return jnp.where((row < side - 0.5) & (col < side - 0.5), 1.0, 0.0).astype(f32)

    load_patches.wait()
    red_a[...] = dot(xp[...], reduce_weights(0), 1, 1)

    def conv_half_a(h, carry):
        lanes = lanes_of(h)
        reduced = red_a[:, lanes]
        activated = reduced * jax.nn.sigmoid(reduced) * cell_mask()
        spatial = conv_forward(activated, tap_rows(0, lanes), GRID, edge_masks(GRID, 128))
        spa_a[:, lanes] = spatial
        nar_a[:, lanes] = (spatial * jax.nn.sigmoid(spatial)).astype(bf16)
        return carry

    lax.fori_loop(0, 2, conv_half_a, 0)
    w_over(2)
    swap_weights()
    w_finish(1)
    dy[...] = dot(nar_a[...], expand_weights(0), 1, 0)

    def normalise(wide_ref, ref, inv_ref, rows):
        widened = wide_ref[rows, :]
        centred = widened - jnp.mean(widened, axis=1, keepdims=True)
        inv = lax.rsqrt(jnp.mean(centred * centred, axis=1, keepdims=True) + epsilon)
        normed = centred * inv
        ref[rows, :] = normed.astype(ref.dtype)
        inv_ref[rows, :] = jnp.broadcast_to(inv, (normed.shape[0], 128))
        return normed

    def norm_tile(t, carry):
        rows = pl.ds(pl.multiple_of(t * TILE, TILE), TILE)
        normed = normalise(dy, norm_a, inv_a, rows)
        result = xp[rows, :].astype(f32) + normed * gain_a
        high, low = split_low(result)
        yhi[rows, :] = high
        ylo[rows, :] = low
        return carry

    lax.fori_loop(0, CELLS // TILE, norm_tile, 0)
    cot_hop(0, 1)

    cell = lax.broadcasted_iota(jnp.int32, (POOLED, CELLS), 1).astype(f32)
    bin_of = lax.broadcasted_iota(jnp.int32, (POOLED, CELLS), 0).astype(f32)
    cell_row = jnp.floor((cell + 0.5) * (1.0 / GRID))
    cell_col = cell - cell_row * GRID
    bin_row = jnp.floor((bin_of + 0.5) * (1.0 / POOL))
    bin_col = bin_of - bin_row * POOL

    def table(bins, at):
        lower = jnp.floor((bins * side + 0.5) * (1.0 / POOL))
        upper = jnp.floor(((bins + 1.0) * side + (POOL - 0.5)) * (1.0 / POOL))
        return jnp.where((at > lower - 0.5) & (at < upper - 0.5), 1.0 / (upper - lower), 0.0)

    pp[...] = (table(bin_row, cell_row) * table(bin_col, cell_col)).astype(bf16)
    pooled = dot(pp[...], yhi[...], 1, 0) + dot(pp[...], ylo[...], 1, 0)
    poolv[...] = pooled

    w_finish(2)

    gain_b = small_weights(1)
    reduced_b = dot(pooled.astype(bf16), reduce_weights(1), 1, 1)
    red_b[...] = reduced_b
    activated_b = reduced_b * jax.nn.sigmoid(reduced_b)
    spatial_b = conv_forward(activated_b, tap_rows(1, pl.ds(0, 256)), POOL, edge_masks(POOL, 256))
    spa_b[...] = spatial_b
    nar_b[...] = (spatial_b * jax.nn.sigmoid(spatial_b)).astype(bf16)
    norm_b[...] = dot(nar_b[...], expand_weights(1), 1, 0)
    normed_b = normalise(norm_b, norm_b, inv_b, pl.ds(0, POOLED))
    qs[me] = (pooled + normed_b * gain_b).astype(bf16)

    for k in range(1, zn):
        start(qs.at[me], qs.at[me], q_s.at[k - 1], q_rz.at[k], z_dev(z_at(k)))
    start(qs.at[me], qs.at[me], q_s.at[3], q_rc.at[z], twin)
    cot_own(3)
    cot_hop(1, 1)
    for k in range(1, zn):
        z_of = z_at(-k)
        slot = qs.at[2 * z_of + c]
        arrived(slot, q_rz.at[k])
        start(slot, slot, q_s.at[3 + k], q_rc.at[z_of], twin)
    cot_hop(0, 2)
    for z_of in range(zn):
        arrived(qs.at[2 * z_of + 1 - c], q_rc.at[z_of])
    arrived(wi, sw_r.at[0])

    dpre[...] = dot(slot_rows(qs), wi[...], 1, 0)

    def gelu_tile(t, carry):
        rows = pl.ds(pl.multiple_of(t * POOLED, POOLED), POOLED)
        hidden = dpre[rows, :]
        phi = 0.5 * (1.0 + lax.erf(hidden * root_half))
        actv[rows, :] = (hidden * phi).astype(bf16)
        slope[rows, :] = (
            phi + hidden * jnp.exp(-0.5 * hidden * hidden) * inv_root_tau
        ).astype(bf16)
        return carry

    lax.fori_loop(0, 8, gelu_tile, 0)
    dpre[...] = jnp.zeros_like(dpre)

    def item_part(i):
        b = lax.rem(i, 2)

        @pl.when(i >= 2)
        def _():
            left_here(tp.at[b], t_cs.at[b])
            pl.semaphore_wait(credit, 1)

        weights = wo[:, pl.ds(pl.multiple_of(i * chunk, chunk), chunk)]
        partial = dot(actv[...], weights, 1, 0).astype(bf16)
        partial = partial.reshape(zn, 2, POOLED, chunk)

        @pl.when(c == 0)
        def _():
            ps[i] = partial[:, 0]
            tp[b] = partial[:, 1]

        @pl.when(c == 1)
        def _():
            ps[i] = partial[:, 1]
            tp[b] = partial[:, 0]

        start(tp.at[b], cr.at[b], t_cs.at[b], t_cr.at[b], twin)

    def send_right(i, d):
        start(ps.at[i, d], rl.at[i, d + 1], t_s.at[i, d], t_r.at[i, d + 1], z_dev(z + 1))

    def send_left(i, d):
        start(ps.at[i, d], rl.at[i, d], t_s.at[i, d], t_r.at[i, d], z_dev(z - 1))

    def item_pair(i):
        b = lax.rem(i, 2)
        arrived(cr.at[b], t_cr.at[b])

        def add(d, carry):
            ps[i, d] = (ps[i, d].astype(f32) + cr[b, d].astype(f32)).astype(bf16)
            return carry

        lax.fori_loop(0, zn, add, 0)

        @pl.when(i < CHUNKS - 2)
        def _():
            pl.semaphore_signal(credit, inc=1, device_id=twin, device_id_type=MESH)

        @pl.when(z == 0)
        def _():
            for d in range(zn - 1, 0, -1):
                send_right(i, d)

        @pl.when(z == zn - 1)
        def _():
            for d in range(zn - 1):
                send_left(i, d)

    def item_right(i):
        def pass_on(step, carry):
            d = zn - 1 - step
            arrived(rl.at[i, d + 1], t_r.at[i, d + 1])
            ps[i, d] = (ps[i, d].astype(f32) + rl[i, d + 1].astype(f32)).astype(bf16)
            send_right(i, d)
            return carry

        lax.fori_loop(0, zn - 1 - z, pass_on, 0)
        arrived(rl.at[i, z + 1], t_r.at[i, z + 1])

    def item_left(i):
        def pass_on(d, carry):
            arrived(rl.at[i, d], t_r.at[i, d])
            ps[i, d] = (ps[i, d].astype(f32) + rl[i, d].astype(f32)).astype(bf16)
            send_left(i, d)
            return carry

        lax.fori_loop(0, z, pass_on, 0)
        arrived(rl.at[i, z], t_r.at[i, z])

    def tok_slice(i):
        return tok_out.at[:, pl.ds(pl.multiple_of(i * chunk, chunk), chunk)]

    def item_final(i):
        b = lax.rem(i, 2)

        @pl.when(i >= 2)
        def _():
            left_here(tstage.at[b], gl.at[8 + b])

        tstage[b] = ps[i, z]

        @pl.when(z > 0)
        def _():
            tstage[b] = (tstage[b].astype(f32) + rl[i, z + 1].astype(f32)).astype(bf16)

        @pl.when(z < zn - 1)
        def _():
            tstage[b] = (tstage[b].astype(f32) + rl[i, z].astype(f32)).astype(bf16)

        pltpu.make_async_copy(tstage.at[b], tok_slice(i), gl.at[8 + b]).start()

    def item_step(s):
        @pl.when(s < CHUNKS)
        def _():
            item_part(s)

        @pl.when((s >= 1) & (s < CHUNKS + 1))
        def _():
            item_pair(s - 1)

        right_at = s - 1 - z

        @pl.when((z > 0) & (right_at >= 0) & (right_at < CHUNKS))
        def _():
            item_right(right_at)

        left_at = s - zn + z

        @pl.when((z < zn - 1) & (left_at >= 0) & (left_at < CHUNKS))
        def _():
            item_left(left_at)

        @pl.when((s >= zn) & (s < CHUNKS + zn))
        def _():
            item_final(s - zn)

    def twin_rows(z_of, p):
        arrived(cot(z_of, 1 - c, p), dt_cr.at[p, z_of])

    def slot_span(z_of):
        return pl.ds(pl.multiple_of(z_of * (2 * POOLED), 2 * POOLED), 2 * POOLED)

    def load_rows(z_of, p, at):
        @pl.when(z_of != z)
        def _():
            part = cot_all.at[z_of, :, :, pl.ds(p * width, width)]
            pltpu.make_async_copy(part, dtv.at[pl.ds(at, 2)], loc.at[3]).start()

        @pl.when(z_of == z)
        def _():
            pltpu.make_async_copy(cot(z, 1 - c, p), dtv.at[at + 1 - c], loc.at[3]).start()
            pltpu.make_async_copy(cot_mine(p), dtv.at[at + c], loc.at[3]).start()

    def piece_rows(p):
        for z_of in range(zn):
            twin_rows(z_of, p)
            load_rows(z_of, p, 2 * z_of)
        pltpu.make_async_copy(dtv, dtv, loc.at[3]).wait()

    def piece_work(p):
        piece_rows(p)
        grad_part(p)

        def hidden_half(h, carry):
            lanes = pl.ds(pl.multiple_of(h * chunk, chunk), chunk)
            rows = dtv[:, :, lanes].reshape(8 * POOLED, chunk)
            weights = wo[:, pl.ds(pl.multiple_of(p * width + h * chunk, chunk), chunk)]
            dpre[...] += dot(rows, weights, 1, 1)
            return carry

        lax.fori_loop(0, 2, hidden_half, 0)

    last = PIECES - 1

    def source_last(z_of):
        twin_rows(z_of, last)
        load_rows(z_of, last, 2 * z_of)
        pair = dtv.at[pl.ds(2 * z_of, 2)]
        pltpu.make_async_copy(pair, pair, loc.at[3]).wait()
        rows = slot_span(z_of)
        left = dtv[pl.ds(2 * z_of, 2)].reshape(2 * POOLED, width)
        total = dpre[rows, :] + dot(left, wo[:, last * width :], 1, 1)
        d_hidden = (total * slope[rows, :].astype(f32)).astype(bf16)
        half = lax.div(z_of, 2)
        place = pl.ds(pl.multiple_of((z_of - 2 * half) * (2 * POOLED), 2 * POOLED), 2 * POOLED)
        ylo[place, pl.ds(pl.multiple_of(half * 512, 512), 512)] = d_hidden
        d_rows = dot(d_hidden, wi[...], 1, 1).astype(bf16)
        dps[z_of] = d_rows.reshape(2, POOLED, 1024)
        start(dps.at[z_of, 1 - c], dr.at[z_of], d_cs.at[z_of], d_cr.at[z_of], twin)

    def source_pair(z_of):
        arrived(dr.at[z_of], d_cr.at[z_of])
        dps[z_of, c] = (dps[z_of, c].astype(f32) + dr[z_of].astype(f32)).astype(bf16)

        @pl.when(z_of != z)
        def _():
            k = lax.rem(z_of - z + zn, zn)
            start(dps.at[z_of, c], dz.at[k - 1], d_zs.at[k - 1], d_zr.at[k - 1], z_dev(z_of))

    def around(hop, work):
        def one_side(side, carry):
            z_of = z + (2 * side - 1) * hop

            @pl.when((z_of >= 0) & (z_of <= zn - 1))
            def _():
                work(z_of)

            return carry

        lax.fori_loop(0, 2, one_side, 0)

    def grad_part(p):
        def out_half(h, carry):
            lanes = pl.ds(pl.multiple_of(h * chunk, chunk), chunk)
            rows = dtv[:, :, lanes].reshape(8 * POOLED, chunk)
            gos[p, :, lanes] = dot(actv[...], rows, 0, 0).astype(bf16)
            return carry

        lax.fori_loop(0, 2, out_half, 0)

        @pl.when(jnp.logical_not(own))
        def _():
            start(gos.at[p], gx_land.at[p], gx_s.at[p], gx_r.at[p], x_peer)

    def gout_slice(half, p):
        return gout_out.at[half, :, pl.ds(pl.multiple_of(p * width, width), width)]

    def grad_pair(p):
        @pl.when(own)
        def _():
            arrived(gx_land.at[p], gx_r.at[p])
            for h in range(2):
                half = pl.ds(h * width // 2, width // 2)
                load = pltpu.make_async_copy(gx_land.at[p, :, half], land, loc.at[4])
                load.start()
                load.wait()
                gos[p, :, half] = (gos[p, :, half].astype(f32) + land[...].astype(f32)).astype(bf16)
            mine = gout_slice(y, p)
            start(gos.at[p], mine, gy_s.at[p], gy_r.at[p], y_peer)
            start(gos.at[p], mine, gc_s.at[p, 0], gc_r.at[p, 0], twin)
            pltpu.make_async_copy(gos.at[p], mine, gl.at[p]).start()

    def grad_last(p):
        other = gout_slice(1 - y, p)
        mine = gout_slice(y, p)

        @pl.when(own)
        def _():
            arrived(other, gy_r.at[p])
            start(other, other, gc_s.at[p, 1], gc_r.at[p, 1], twin)

    def grad_done(p):
        other = gout_slice(1 - y, p)
        mine = gout_slice(y, p)

        @pl.when(own)
        def _():
            left_here(gos.at[p], gy_s.at[p])
            left_here(gos.at[p], gc_s.at[p, 0])
            left_here(other, gc_s.at[p, 1])
            pltpu.make_async_copy(gos.at[p], mine, gl.at[p]).wait()

        @pl.when(jnp.logical_not(own))
        def _():
            left_here(gos.at[p], gx_s.at[p])
            arrived(mine, gc_r.at[p, 0])
            arrived(other, gc_r.at[p, 1])

    def gin_slice(half):
        return gin_out.at[half]

    def widened_back(d_rows, normed, gain, inv):
        dn = d_rows * gain
        return (
            inv
            * (
                dn
                - jnp.mean(dn, axis=1, keepdims=True)
                - normed * jnp.mean(dn * normed, axis=1, keepdims=True)
            )
        ).astype(bf16)

    def pack_small(t, d_gain):
        for k in range(4):
            sm[t, 9 + k : 10 + k, :] = d_gain[:, 256 * k : 256 * k + 256]
        sm[t, 13:16, :] = jnp.zeros((3, 256), f32)

    def share_core(t):
        start(wgs.at[t, 1 - c], wgc.at[t], gr_s.at[t, 0], gr_r.at[t, 0], twin)
        start(sm.at[t], smc.at[t], gr_s.at[t, 1], gr_r.at[t, 1], twin)

    def share_x(t):
        arrived(wgc.at[t], gr_r.at[t, 0])
        arrived(smc.at[t], gr_r.at[t, 1])
        for i in range(8):
            for h in range(2):
                rows = pl.ds(128 * h + 16 * i, 16)
                xs[t, i % 2, i // 2, 16 * h : 16 * h + 16] = (
                    wgs[t, c, rows, :].astype(f32) + wgc[t, rows, :].astype(f32)
                ).astype(bf16)
        left_here(sm.at[t], gr_s.at[t, 1])
        sm[t] = sm[t] + smc[t]
        start(xs.at[t, 1 - x], xr.at[t], gr_s.at[t, 2], gr_r.at[t, 2], x_peer)
        start(sm.at[t], smx.at[t], gr_s.at[t, 3], gr_r.at[t, 3], x_peer)

    def share_z(t):
        arrived(xr.at[t], gr_r.at[t, 2])
        arrived(smx.at[t], gr_r.at[t, 3])
        zs[t] = (xs[t, x].astype(f32) + xr[t].astype(f32)).astype(bf16)
        left_here(sm.at[t], gr_s.at[t, 3])
        smz[t, z] = sm[t] + smx[t]
        for k in range(1, zn):
            d = z_at(k)
            start(zs.at[t, d], zr.at[t, k - 1], gr_s.at[t, 3 + k], gr_r.at[t, 3 + k], z_dev(d))
            start(
                smz.at[t, z], smz.at[t, z], gr_s.at[t, 6 + k], gr_r.at[t, 6 + k], z_dev(d)
            )

    def share_y(t):
        total_rows = zs[t, z].astype(f32)
        for k in range(1, zn):
            arrived(zr.at[t, k - 1], gr_r.at[t, 3 + k])
            total_rows = total_rows + zr[t, k - 1].astype(f32)
            arrived(smz.at[t, z_at(-k)], gr_r.at[t, 6 + k])
        ys[t] = total_rows.astype(bf16)
        sm[t] = (smz[t, 0] + smz[t, 1]) + (smz[t, 2] + smz[t, 3])
        start(ys.at[t], yr.at[t], gr_s.at[t, 10], gr_r.at[t, 10], y_peer)
        start(sm.at[t], smy.at[t], gr_s.at[t, 11], gr_r.at[t, 11], y_peer)

    def share_twin(t):
        arrived(yr.at[t], gr_r.at[t, 10])
        arrived(smy.at[t], gr_r.at[t, 11])
        gfin[t, c] = ys[t].astype(f32) + yr[t].astype(f32)
        gsml_out[t] = sm[t] + smy[t]
        start(gfin.at[t, c], gfin.at[t, c], gr_s.at[t, 12], gr_r.at[t, 12], twin)

    def share_done(t):
        arrived(gfin.at[t, 1 - c], gr_r.at[t, 12])
        gblk_out[t] = gfin[t]
        left_here(wgs.at[t, 1 - c], gr_s.at[t, 0])
        left_here(xs.at[t, 1 - x], gr_s.at[t, 2])
        for k in range(1, zn):
            left_here(zs.at[t, 0], gr_s.at[t, 3 + k])
            left_here(smz.at[t, z], gr_s.at[t, 6 + k])
        left_here(ys.at[t], gr_s.at[t, 10])
        left_here(sm.at[t], gr_s.at[t, 11])
        left_here(gfin.at[t, c], gr_s.at[t, 12])

    def back_second():
        total = dps[z, c].astype(f32)
        for k in range(1, zn):
            arrived(dz.at[k - 1], d_zr.at[k - 1])
            total = total + dz[k - 1].astype(f32)
        normed_b = norm_b[...]
        d_gain_b = jnp.sum(total * normed_b, axis=0, keepdims=True)
        gain_b = tw[1, 9:10, :]
        dw_b = widened_back(total, normed_b, gain_b, inv_b[:, 0:1])
        wgs[1, 1] = dot(nar_b[...], dw_b, 0, 0).astype(bf16)
        spatial_b = spa_b[...]
        d_spatial_b = dot(dw_b, expand_weights(1), 1, 1) * silu_slope(spatial_b)
        reduced_b = red_b[...]
        sig_b = jax.nn.sigmoid(reduced_b)
        d_act_b, d_taps_b = conv_backward(
            d_spatial_b, reduced_b * sig_b, tap_rows(1, pl.ds(0, 256)), POOL, edge_masks(POOL, 256)
        )
        d_red_b = (d_act_b * (sig_b * (1.0 + reduced_b * (1.0 - sig_b)))).astype(bf16)
        wgs[1, 0] = dot(d_red_b, poolv[...].astype(bf16), 0, 0).astype(bf16)
        for k in range(9):
            sm[1, k : k + 1, :] = d_taps_b[k]
        pack_small(1, d_gain_b)
        d_pool = total + dot(d_red_b, reduce_weights(1), 1, 0)
        high, low = split_low(d_pool)
        dy[...] = dot(pp[...], high, 0, 0) + dot(pp[...], low, 0, 0)

    def back_first_norm():
        gain_a = tw[0, 9:10, :]

        def back_tile(t, d_gain):
            rows = pl.ds(pl.multiple_of(t * TILE, TILE), TILE)
            d_rows = dy[rows, :]
            normed = norm_a[rows, :].astype(f32)
            yhi[rows, :] = widened_back(d_rows, normed, gain_a, inv_a[rows, 0:1])
            return d_gain + jnp.sum(d_rows * normed, axis=0, keepdims=True)

        d_gain_a = lax.fori_loop(0, CELLS // TILE, back_tile, jnp.zeros((1, 1024), f32))
        pack_small(0, d_gain_a)
        wgs[0, 1] = dot(nar_a[...], yhi[...], 0, 0).astype(bf16)

    def back_first_conv():
        spa_a[...] = dot(yhi[...], expand_weights(0), 1, 1) * silu_slope(spa_a[...])

        def conv_back_half_a(h, carry):
            lanes = lanes_of(h)
            reduced = red_a[:, lanes]
            sig = jax.nn.sigmoid(reduced)
            mask = cell_mask()
            d_act, d_taps = conv_backward(
                spa_a[:, lanes], reduced * sig * mask, tap_rows(0, lanes), GRID, edge_masks(GRID, 128)
            )
            dlow[:, lanes] = (d_act * mask * (sig * (1.0 + reduced * (1.0 - sig)))).astype(bf16)
            for k in range(9):
                sm[0, k : k + 1, lanes] = d_taps[k]
            return carry

        lax.fori_loop(0, 2, conv_back_half_a, 0)
        wgs[0, 0] = dot(dlow[...], xp[...], 0, 0).astype(bf16)

    store_dpat = pltpu.make_async_copy(dy, dpat_out, loc.at[5])

    def back_first_rows():
        dy[...] += dot(dlow[...], reduce_weights(0), 1, 0)
        store_dpat.start()

    def gin_part():
        gis[...] = (
            dot(qs[0:4].reshape(4 * POOLED, 1024), ylo[:, 0:512], 0, 0)
            + dot(qs[4:8].reshape(4 * POOLED, 1024), ylo[:, 512:1024], 0, 0)
        ).astype(bf16)

        @pl.when(jnp.logical_not(own))
        def _():
            start(gis, gi_land, gx_s.at[PIECES], gx_r.at[PIECES], x_peer)

    def gin_pair():
        @pl.when(own)
        def _():
            arrived(gi_land, gx_r.at[PIECES])
            for h in range(2):
                rows = pl.ds(512 * h, 512)
                load = pltpu.make_async_copy(gi_land.at[rows], land, loc.at[4])
                load.start()
                load.wait()
                gis[rows, :] = (gis[rows, :].astype(f32) + land[...].astype(f32)).astype(bf16)
            start(gis, gin_slice(y), gy_s.at[PIECES], gy_r.at[PIECES], y_peer)
            start(gis, gin_slice(y), gc_s.at[PIECES, 0], gc_r.at[PIECES, 0], twin)
            pltpu.make_async_copy(gis, gin_slice(y), gl.at[PIECES]).start()

    def gin_last():
        @pl.when(own)
        def _():
            arrived(gin_slice(1 - y), gy_r.at[PIECES])
            start(gin_slice(1 - y), gin_slice(1 - y), gc_s.at[PIECES, 1], gc_r.at[PIECES, 1], twin)

    def main_step(s, carry):
        def at(step):
            return pl.when(s == step)

        @pl.when(s < CHUNKS // 2)
        def _():
            for half in range(2):
                j = 2 * s + half
                arrived(wo.at[:, pl.ds(pl.multiple_of(j * chunk, chunk), chunk)], sw_r.at[1 + j])

        @at(0)
        def _():
            cot_hop(2, 1)
            cot_hop(1, 2)
            cot_hop(0, 3)

        @at(1)
        def _():
            cot_hop(3, 1)
            cot_hop(2, 2)
            piece_work(0)

        @at(2)
        def _():
            cot_hop(1, 3)

        @at(3)
        def _():
            cot_hop(3, 2)
            piece_work(1)
            grad_pair(0)

        @at(4)
        def _():
            cot_hop(2, 3)

        @at(5)
        def _():
            piece_work(2)
            grad_pair(1)
            grad_last(0)
            source_last(z)
            around(1, source_last)

        @at(6)
        def _():
            cot_hop(3, 3)
            source_pair(z)
            around(1, source_pair)
            around(2, source_last)

        @at(7)
        def _():
            around(3, source_last)
            around(2, source_pair)
            grad_part(3)
            around(3, source_pair)
            grad_pair(2)
            grad_last(1)

        @at(8)
        def _():
            gin_part()

        @at(9)
        def _():
            back_second()
            share_core(1)

        @at(10)
        def _():
            back_first_norm()
            share_x(1)
            grad_pair(3)
            grad_last(2)

        @at(11)
        def _():
            back_first_conv()
            share_core(0)
            share_z(1)
            back_first_rows()

        @at(12)
        def _():
            share_x(0)
            share_y(1)
            gin_pair()

        @at(13)
        def _():
            share_z(0)
            share_twin(1)
            grad_last(3)

        @at(14)
        def _():
            share_y(0)

        @at(15)
        def _():
            share_twin(0)
            gin_last()

        @pl.when((s >= CHUNKS) | (lax.rem(s, 2) == 0))
        def _():
            item_step(jnp.where(s < CHUNKS, lax.div(s, 2), s - CHUNKS // 2))

        return carry

    lax.fori_loop(0, 2 * CHUNKS, main_step, 0)

    share_done(1)
    share_done(0)
    for p in range(PIECES):
        grad_done(p)

    @pl.when(own)
    def _():
        left_here(gis, gy_s.at[PIECES])
        left_here(gis, gc_s.at[PIECES, 0])
        left_here(gin_slice(1 - y), gc_s.at[PIECES, 1])
        pltpu.make_async_copy(gis, gin_slice(y), gl.at[PIECES]).wait()

    @pl.when(jnp.logical_not(own))
    def _():
        left_here(gis, gx_s.at[PIECES])
        arrived(gin_slice(y), gc_r.at[PIECES, 0])
        arrived(gin_slice(1 - y), gc_r.at[PIECES, 1])
        left_here(wi, sw_s.at[0])
        for j in range(CHUNKS):
            left_here(columns(wo, j, chunk), sw_s.at[1 + j])

    store_dpat.wait()
    for b in range(2):
        pltpu.make_async_copy(tstage.at[b], tok_slice(b), gl.at[8 + b]).wait()
        left_here(tp.at[b], t_cs.at[b])
    for b in range(4):
        for k in range(15):
            left_here(w_part(b, c, 0), w_s.at[b, k])
    for k in range(7):
        left_here(qs.at[0], q_s.at[k])
    for k in range(zn):
        left_here(dps.at[0, 0], d_cs.at[k])
    for k in range(zn - 1):
        left_here(dps.at[0, 0], d_zs.at[k])
    for p in range(PIECES):
        for z_of in range(zn):
            left_here(cot(0, 0, p), dt_cs.at[p, z_of])
        for hop in range(zn - 1):
            @pl.when((z < zn - 1) & (z >= hop))
            def _():
                left_here(cot(0, 0, p), dt_s.at[p, 0, hop])

            @pl.when((z > 0) & (z + hop <= zn - 1))
            def _():
                left_here(cot(0, 0, p), dt_s.at[p, 1, hop])

    def drain_items(i, carry):
        for d in range(zn):
            @pl.when(z != d)
            def _():
                left_here(ps.at[0, 0], t_s.at[i, d])
        return carry

    lax.fori_loop(0, CHUNKS, drain_items, 0)


def layer_call(
    patches, grid_sizes, wr_a, taps_a, we_a, gain_a, wr_b, taps_b, we_b, gain_b, w_in, w_out, d_tokens
):
    any_space = pl.BlockSpec(memory_space=pl.ANY)
    vmem = pl.BlockSpec(memory_space=pltpu.VMEM)
    smem = pl.BlockSpec(memory_space=pltpu.SMEM)
    shape = jax.ShapeDtypeStruct
    width = w_out.shape[1] // PIECES
    chunk = w_out.shape[1] // CHUNKS
    out_shape = (
        shape((POOLED, 4096), bf16),
        shape((CELLS, 1024), f32),
        shape((2, 512, 4096), bf16),
        shape((2, 1024, 512), bf16),
        shape((2, 2, 32, 1024), f32),
        shape((2, 16, 256), f32),
        shape((4, 2, POOLED, 4096), bf16),
        shape((PIECES, 512, width), bf16),
        shape((1024, 512), bf16),
    )
    dma = pltpu.SemaphoreType.DMA
    scratch = [
        pltpu.VMEM((CELLS, 1024), bf16),
        pltpu.VMEM((2, 8, 64, 1024), bf16),
        pltpu.VMEM((2, 8, 16, 256), f32),
        pltpu.VMEM((CELLS, 256), f32),
        pltpu.VMEM((CELLS, 256), f32),
        pltpu.VMEM((CELLS, 256), bf16),
        pltpu.VMEM((CELLS, 1024), bf16),
        pltpu.VMEM((CELLS, 128), f32),
        pltpu.VMEM((CELLS, 1024), bf16),
        pltpu.VMEM((CELLS, 1024), bf16),
        pltpu.VMEM((CELLS, 1024), f32),
        pltpu.VMEM((CELLS, 256), bf16),
        pltpu.VMEM((POOLED, CELLS), bf16),
        pltpu.VMEM((2, 16, 1024), f32),
        pltpu.VMEM((POOLED, 1024), f32),
        pltpu.VMEM((POOLED, 256), f32),
        pltpu.VMEM((POOLED, 256), f32),
        pltpu.VMEM((POOLED, 256), bf16),
        pltpu.VMEM((POOLED, 1024), f32),
        pltpu.VMEM((POOLED, 128), f32),
        pltpu.VMEM((1024, 512), bf16),
        pltpu.VMEM((512, 4096), bf16),
        pltpu.VMEM((8, POOLED, 1024), bf16),
        pltpu.VMEM((8 * POOLED, 512), bf16),
        pltpu.VMEM((8 * POOLED, 512), bf16),
        pltpu.VMEM((8 * POOLED, 512), f32),
        pltpu.VMEM((8, POOLED, width), bf16),
        pltpu.VMEM((2, 4, POOLED, chunk), bf16),
        pltpu.VMEM((2, 4, POOLED, chunk), bf16),
        pltpu.VMEM((CHUNKS, 4, POOLED, chunk), bf16),
        pltpu.VMEM((CHUNKS, 5, POOLED, chunk), bf16),
        pltpu.VMEM((2, POOLED, chunk), bf16),
        pltpu.VMEM((4, 2, POOLED, 1024), bf16),
        pltpu.VMEM((4, POOLED, 1024), bf16),
        pltpu.VMEM((3, POOLED, 1024), bf16),
        pltpu.VMEM((PIECES, 512, width), bf16),
        pltpu.VMEM((1024, 512), bf16),
        pltpu.VMEM((512, width // 2), bf16),
        pltpu.VMEM((2, 2, 256, 1024), bf16),
        pltpu.VMEM((2, 256, 1024), bf16),
        pltpu.VMEM((2, 2, 4, 32, 1024), bf16),
        pltpu.VMEM((2, 4, 32, 1024), bf16),
        pltpu.VMEM((2, 4, 32, 1024), bf16),
        pltpu.VMEM((2, 3, 32, 1024), bf16),
        pltpu.VMEM((2, 32, 1024), bf16),
        pltpu.VMEM((2, 32, 1024), bf16),
        pltpu.VMEM((2, 16, 256), f32),
        pltpu.VMEM((2, 16, 256), f32),
        pltpu.VMEM((2, 16, 256), f32),
        pltpu.VMEM((2, 4, 16, 256), f32),
        pltpu.VMEM((2, 16, 256), f32),
        pltpu.VMEM((2, 2, 32, 1024), f32),
        dma((6,)),
        dma((4, 15)),
        dma((4, 4)),
        dma((4, 4)),
        dma((4, 8)),
        dma((1 + CHUNKS,)),
        dma((1 + CHUNKS,)),
        dma((7,)),
        dma((4,)),
        dma((4,)),
        dma((PIECES, 2, 3)),
        dma((PIECES, 2, 3)),
        dma((PIECES, 4)),
        dma((PIECES, 4)),
        dma((2,)),
        dma((2,)),
        dma((CHUNKS, 4)),
        dma((CHUNKS, 5)),
        pltpu.SemaphoreType.REGULAR,
        dma((4,)),
        dma((4,)),
        dma((3,)),
        dma((3,)),
        dma((PIECES + 1,)),
        dma((PIECES + 1,)),
        dma((PIECES + 1,)),
        dma((PIECES + 1,)),
        dma((PIECES + 1, 2)),
        dma((PIECES + 1, 2)),
        dma((10,)),
        dma((2, 13)),
        dma((2, 13)),
    ]
    return pl.pallas_call(
        layer_kernel,
        out_shape=out_shape,
        in_specs=[any_space, smem] + [vmem] * 8 + [any_space] * 3,
        out_specs=(any_space, any_space, any_space, any_space, vmem, vmem, any_space, any_space, any_space),
        scratch_shapes=scratch,
        compiler_params=pltpu.CompilerParams(
            collective_id=0, has_side_effects=True, vmem_limit_bytes=VMEM_BYTES
        ),
    )(
        patches, grid_sizes, wr_a, taps_a, we_a, gain_a, wr_b, taps_b, we_b, gain_b, w_in, w_out, d_tokens
    )


VMEM_BYTES = 64 * 1024 * 1024


FINISH = 8


def finish_kernel(
    tok_in, dpat_in, gout_in, gin_in, gblk_in, gsml_in,
    tok, dpat, gout, gin, gra, gta, gea, gga, grb, gtb, geb, ggb,
):
    tok[...] = tok_in[...]
    dpat[...] = dpat_in[...]
    gout[...] = gout_in[0].astype(f32) + gout_in[1].astype(f32)
    gin[...] = gin_in[0].astype(f32) + gin_in[1].astype(f32)

    @pl.when(pl.program_id(0) == 0)
    def _():
        mp_at = lax.axis_index("mp")
        for t, outs in enumerate(((gra, gta, gea, gga), (grb, gtb, geb, ggb))):
            reduce, taps, expand, gain = outs
            reduce[...] = gblk_in[t, 0]
            expand[...] = gblk_in[t, 1]
            turned = pltpu.roll(gsml_in[t], lax.rem(256 - 16 * mp_at, 256), 1)
            taps[:, 0:16] = turned[0:9, 0:16]
            taps[:, 16:32] = turned[0:9, 128:144]
            for i in range(8):
                @pl.when(mp_at == i)
                def _(t=t, i=i, gain=gain):
                    lanes = 128 * (i % 2)
                    gain[...] = gsml_in[t, 9 + i // 2 : 10 + i // 2, lanes : lanes + 128]


def finish_call(tokens, d_patches, gout, gin, gblk, gsml):
    shape = jax.ShapeDtypeStruct
    columns = tokens.shape[1] // FINISH

    def whole(*dims):
        return pl.BlockSpec(dims, lambda i: (0,) * len(dims))

    one = [whole(32, 1024), whole(9, 32), whole(32, 1024), whole(1, 128)]
    one_shape = [shape((32, 1024), f32), shape((9, 32), f32), shape((32, 1024), f32), shape((1, 128), f32)]
    return pl.pallas_call(
        finish_kernel,
        grid=(FINISH,),
        out_shape=[
            shape(tokens.shape, bf16),
            shape(d_patches.shape, f32),
            shape(gout.shape[1:], f32),
            shape(gin.shape[1:], f32),
        ]
        + one_shape * 2,
        in_specs=[
            pl.BlockSpec((POOLED, columns), lambda i: (0, i)),
            pl.BlockSpec((CELLS // FINISH, 1024), lambda i: (i, 0)),
            pl.BlockSpec((2, 512 // FINISH, 4096), lambda i: (0, i, 0)),
            pl.BlockSpec((2, 1024 // FINISH, 512), lambda i: (0, i, 0)),
            whole(2, 2, 32, 1024),
            whole(2, 16, 256),
        ],
        out_specs=[
            pl.BlockSpec((POOLED, columns), lambda i: (0, i)),
            pl.BlockSpec((CELLS // FINISH, 1024), lambda i: (i, 0)),
            pl.BlockSpec((512 // FINISH, 4096), lambda i: (i, 0)),
            pl.BlockSpec((1024 // FINISH, 512), lambda i: (i, 0)),
        ]
        + one * 2,
        compiler_params=pltpu.CompilerParams(vmem_limit_bytes=VMEM_BYTES),
    )(tokens, d_patches, gout, gin, gblk, gsml)


def fast_body(
    patches, grid_sizes, w_reduce_a, taps_a, w_expand_a, gain_a,
    w_reduce_b, taps_b, w_expand_b, gain_b, w_in, w_out, d_tokens,
):
    results = layer_call(
        patches, grid_sizes, w_reduce_a.T, taps_a, w_expand_a, gain_a,
        w_reduce_b.T, taps_b, w_expand_b, gain_b, w_in, w_out, d_tokens,
    )
    (
        tokens, d_patches, gout, gin, reduce_a, tap_a, expand_a, scale_a, reduce_b, tap_b, expand_b, scale_b
    ) = finish_call(*results[:6])
    return (
        tokens, d_patches,
        reduce_a.T, tap_a, expand_a, scale_a.reshape(-1),
        reduce_b.T, tap_b, expand_b, scale_b.reshape(-1),
        gin, gout,
    )


def solution(mesh):
    in_specs = (
        P(("dp", "mp"), None),
        P(("dp", "mp")),
        P(None, "mp"),
        P(None, "mp"),
        P("mp", None),
        P("mp"),
        P(None, "mp"),
        P(None, "mp"),
        P("mp", None),
        P("mp"),
        P(None, "mp"),
        P("mp", None),
        P(("dp", "mp"), None),
    )
    out_specs = (
        P(("dp", "mp"), None),
        P(("dp", "mp"), None),
        P(None, "mp"),
        P(None, "mp"),
        P("mp", None),
        P("mp"),
        P(None, "mp"),
        P(None, "mp"),
        P("mp", None),
        P("mp"),
        P(None, "mp"),
        P("mp", None),
    )
    fits = mesh.shape["dp"] == 4 and mesh.shape["mp"] == 8
    return jax.shard_map(fast_body if fits else body, mesh=mesh, in_specs=in_specs, out_specs=out_specs, check_vma=False)
```

```python
import jax
import jax.numpy as jnp
from jax import lax
from jax.experimental import pallas as pl
from jax.experimental.pallas import tpu as pltpu
from jax.sharding import PartitionSpec as P

GRID = 24
SMALL_GRID = 16
POOL = 12


epsilon = 1e-05
highest = lax.Precision.HIGHEST
root_half = 0.7071067811865476
inv_root_tau = 0.3989422804014327


def silu_slope(values):
    sigmoid = jax.nn.sigmoid(values)
    return sigmoid * (1.0 + values * (1.0 - sigmoid))


def gelu_exact(values):
    return 0.5 * values * (1.0 + lax.erf(values * root_half))


def gelu_slope(values):
    return (
        0.5 * (1.0 + lax.erf(values * root_half))
        + values * jnp.exp(-0.5 * values * values) * inv_root_tau
    )


def outer_rows(left, right):
    return lax.dot_general(
        left, right, (((0,), (0,)), ((), ())), preferred_element_type=jnp.float32
    )


def times_trans(left, right):
    return lax.dot_general(
        left, right, (((1,), (1,)), ((), ())), preferred_element_type=jnp.float32
    )


def map_padding(ndims):
    return [(0, 0)] * (ndims - 3) + [(1, 1), (1, 1), (0, 0)]


def depthwise(feature_map, tap_weights):
    extent = feature_map.shape[-2]
    padded = jnp.pad(feature_map, map_padding(feature_map.ndim))
    result = jnp.zeros_like(feature_map)
    for tap_row in range(3):
        for tap_col in range(3):
            result = (
                result
                + padded[..., tap_row : tap_row + extent, tap_col : tap_col + extent, :]
                * tap_weights[3 * tap_row + tap_col]
            )
    return result


def depthwise_back(upstream, feature_map, tap_weights):
    extent = upstream.shape[-2]
    upstream_pad = jnp.pad(upstream, map_padding(upstream.ndim))
    feature_pad = jnp.pad(feature_map, map_padding(feature_map.ndim))
    d_feature = jnp.zeros_like(upstream)
    tap_grads = []
    leading = tuple(range(upstream.ndim - 1))
    for tap_row in range(3):
        for tap_col in range(3):
            d_feature = (
                d_feature
                + upstream_pad[
                    ..., 2 - tap_row : 2 - tap_row + extent, 2 - tap_col : 2 - tap_col + extent, :
                ]
                * tap_weights[3 * tap_row + tap_col]
            )
            shifted = feature_pad[..., tap_row : tap_row + extent, tap_col : tap_col + extent, :]
            tap_grads.append(jnp.sum(shifted * upstream, axis=leading))
    return (d_feature, jnp.stack(tap_grads))


def block_forward(feature_rows, low_rows, weights_set, extent):
    w_reduce, tap_weights, w_expand, norm_gain = weights_set
    channels = w_reduce.shape[1]
    row_count = feature_rows.shape[0]
    reduced = jnp.dot(low_rows, w_reduce, preferred_element_type=jnp.float32)
    activated = jax.nn.silu(reduced).reshape(-1, extent, extent, channels)
    spatial = depthwise(activated, tap_weights.astype(jnp.float32)).reshape(row_count, channels)
    narrow = jax.nn.silu(spatial).astype(jnp.bfloat16)
    widened = jnp.dot(narrow, w_expand, preferred_element_type=jnp.float32)
    centred = widened - jnp.mean(widened, axis=1, keepdims=True)
    inv_scale = lax.rsqrt(jnp.mean(centred * centred, axis=1, keepdims=True) + epsilon)
    normed = centred * inv_scale
    result = feature_rows + normed * norm_gain.astype(jnp.float32)
    return (result, (reduced, activated, spatial, narrow, normed, inv_scale))


def block_backward(d_result, low_rows, weights_set, saved):
    w_reduce, tap_weights, w_expand, norm_gain = weights_set
    reduced, activated, spatial, narrow, normed, inv_scale = saved
    d_gain = jnp.sum(d_result * normed, axis=0)
    d_normed = d_result * norm_gain.astype(jnp.float32)
    d_widened = inv_scale * (
        d_normed
        - jnp.mean(d_normed, axis=1, keepdims=True)
        - normed * jnp.mean(d_normed * normed, axis=1, keepdims=True)
    )
    d_widened = d_widened.astype(jnp.bfloat16)
    grad_expand = outer_rows(narrow, d_widened)
    d_spatial = times_trans(d_widened, w_expand) * silu_slope(spatial)
    d_activated, grad_taps = depthwise_back(
        d_spatial.reshape(activated.shape), activated, tap_weights.astype(jnp.float32)
    )
    d_reduced = (d_activated.reshape(reduced.shape) * silu_slope(reduced)).astype(jnp.bfloat16)
    grad_reduce = outer_rows(low_rows, d_reduced)
    d_rows = d_result + times_trans(d_reduced, w_reduce)
    return (d_rows, (grad_reduce, grad_taps, grad_expand, d_gain))


def crop_rows(pixels, extent):
    features = pixels.shape[-1]
    return pixels.reshape(GRID, GRID, features)[:extent, :extent].reshape(extent * extent, features)


def widen_grid(values, extent):
    features = values.shape[-1]
    return jnp.pad(
        values.reshape(extent, extent, features), ((0, GRID - extent), (0, GRID - extent), (0, 0))
    )


def first_forward(weights_set, extent):

    def compute(pixels):
        cropped = crop_rows(pixels, extent)
        result, unused = block_forward(cropped.astype(jnp.float32), cropped, weights_set, extent)
        return widen_grid(result, extent)

    return compute


def first_backward(weights_set, extent):

    def compute(pixels, upstream):
        cropped = crop_rows(pixels, extent)
        sliced = crop_rows(upstream, extent)
        unused, saved = block_forward(cropped.astype(jnp.float32), cropped, weights_set, extent)
        d_rows, grads = block_backward(sliced, cropped, weights_set, saved)
        return (widen_grid(d_rows, extent).reshape(GRID * GRID, -1), grads)

    return compute


def pool_table(grid_side):
    bin_index = lax.iota(jnp.int32, POOL)
    bin_lower = bin_index * grid_side // POOL
    bin_upper = ((bin_index + 1) * grid_side + POOL - 1) // POOL
    cell_index = lax.iota(jnp.int32, GRID)
    inside = (cell_index[None, :] >= bin_lower[:, None]) & (
        cell_index[None, :] < bin_upper[:, None]
    )
    weights = jnp.where(inside, 1.0, 0.0) / (bin_upper - bin_lower)[:, None]
    return weights.astype(jnp.float32)


def body(
    patches,
    grid_sizes,
    w_reduce_a,
    taps_a,
    w_expand_a,
    gain_a,
    w_reduce_b,
    taps_b,
    w_expand_b,
    gain_b,
    w_in,
    w_out,
    d_tokens,
):
    gathered = (
        lax.all_gather(w_reduce_a, "mp", axis=1, tiled=True),
        lax.all_gather(taps_a, "mp", axis=1, tiled=True),
        lax.all_gather(w_expand_a, "mp", axis=0, tiled=True),
        lax.all_gather(gain_a, "mp", axis=0, tiled=True),
        lax.all_gather(w_reduce_b, "mp", axis=1, tiled=True),
        lax.all_gather(taps_b, "mp", axis=1, tiled=True),
        lax.all_gather(w_expand_b, "mp", axis=0, tiled=True),
        lax.all_gather(gain_b, "mp", axis=0, tiled=True),
    )
    first_set = gathered[0:4]
    second_set = gathered[4:8]
    features = patches.shape[1]
    pictures = patches.reshape(-1, GRID * GRID, features)
    picture_count = pictures.shape[0]
    tables = jax.vmap(pool_table)(grid_sizes)

    def forward_one(element):
        pixels, grid_side, pool_weights = element
        result = lax.cond(
            grid_side == GRID,
            first_forward(first_set, GRID),
            first_forward(first_set, SMALL_GRID),
            pixels,
        )
        return jnp.einsum("ia,jb,abd->ijd", pool_weights, pool_weights, result, precision=highest)

    pooled = lax.map(forward_one, (pictures, grid_sizes, tables))
    pooled_rows = pooled.reshape(picture_count * POOL * POOL, features)
    pooled_low = pooled_rows.astype(jnp.bfloat16)
    mixed_rows, second_saved = block_forward(pooled_rows, pooled_low, second_set, POOL)
    queries = mixed_rows.astype(jnp.bfloat16)
    hidden = jnp.dot(
        lax.all_gather(queries, "mp", axis=0, tiled=True), w_in, preferred_element_type=jnp.float32
    )
    active = gelu_exact(hidden).astype(jnp.bfloat16)
    tokens = lax.psum_scatter(
        jnp.dot(active, w_out, preferred_element_type=jnp.float32).astype(jnp.bfloat16),
        "mp",
        scatter_dimension=0,
        tiled=True,
    )
    piece = lax.all_gather(d_tokens, "mp", axis=0, tiled=True)
    d_part = (times_trans(piece, w_out) * gelu_slope(hidden)).astype(jnp.bfloat16)
    grad_out_sum = outer_rows(active, piece)
    d_hidden = d_part
    d_part = d_hidden
    grad_in_part = outer_rows(lax.all_gather(queries, "mp", axis=0, tiled=True), d_part)
    d_part = d_hidden
    d_mixed = lax.psum_scatter(times_trans(d_part, w_in), "mp", scatter_dimension=0, tiled=True)
    d_pooled, second_grads = block_backward(d_mixed, pooled_low, second_set, second_saved)
    d_pooled = d_pooled.reshape(picture_count, POOL, POOL, features)

    def backward_one(totals, element):
        pixels, grid_side, pool_weights, upstream = element
        d_grid = jnp.einsum(
            "ia,jb,ijd->abd", pool_weights, pool_weights, upstream, precision=highest
        )
        d_pixels, grads = lax.cond(
            grid_side == GRID,
            first_backward(first_set, GRID),
            first_backward(first_set, SMALL_GRID),
            pixels,
            d_grid,
        )
        return (
            tuple((total_part + grad_part for total_part, grad_part in zip(totals, grads))),
            d_pixels,
        )

    zero_grads = tuple((jnp.zeros(weight.shape, jnp.float32) for weight in first_set))
    first_grads, d_pictures = lax.scan(
        backward_one, zero_grads, (pictures, grid_sizes, tables, d_pooled)
    )
    d_patches = d_pictures.reshape(-1, features)
    shards = (
        lax.psum_scatter(
            first_grads[0].astype(jnp.bfloat16), "mp", scatter_dimension=1, tiled=True
        ).astype(jnp.float32),
        lax.psum_scatter(
            first_grads[1].astype(jnp.bfloat16), "mp", scatter_dimension=1, tiled=True
        ).astype(jnp.float32),
        lax.psum_scatter(
            first_grads[2].astype(jnp.bfloat16), "mp", scatter_dimension=0, tiled=True
        ).astype(jnp.float32),
        lax.psum_scatter(
            first_grads[3].astype(jnp.bfloat16), "mp", scatter_dimension=0, tiled=True
        ).astype(jnp.float32),
        lax.psum_scatter(
            second_grads[0].astype(jnp.bfloat16), "mp", scatter_dimension=1, tiled=True
        ).astype(jnp.float32),
        lax.psum_scatter(
            second_grads[1].astype(jnp.bfloat16), "mp", scatter_dimension=1, tiled=True
        ).astype(jnp.float32),
        lax.psum_scatter(
            second_grads[2].astype(jnp.bfloat16), "mp", scatter_dimension=0, tiled=True
        ).astype(jnp.float32),
        lax.psum_scatter(
            second_grads[3].astype(jnp.bfloat16), "mp", scatter_dimension=0, tiled=True
        ).astype(jnp.float32),
    )
    summed = (
        lax.psum(shards[0].astype(jnp.bfloat16), "dp").astype(jnp.float32),
        lax.psum(shards[1].astype(jnp.bfloat16), "dp").astype(jnp.float32),
        lax.psum(shards[2].astype(jnp.bfloat16), "dp").astype(jnp.float32),
        lax.psum(shards[3].astype(jnp.bfloat16), "dp").astype(jnp.float32),
        lax.psum(shards[4].astype(jnp.bfloat16), "dp").astype(jnp.float32),
        lax.psum(shards[5].astype(jnp.bfloat16), "dp").astype(jnp.float32),
        lax.psum(shards[6].astype(jnp.bfloat16), "dp").astype(jnp.float32),
        lax.psum(shards[7].astype(jnp.bfloat16), "dp").astype(jnp.float32),
        lax.psum(grad_in_part.astype(jnp.bfloat16), "dp").astype(jnp.float32),
        lax.psum(grad_out_sum.astype(jnp.bfloat16), "dp").astype(jnp.float32),
    )
    return (
        tokens,
        d_patches,
        summed[0],
        summed[1],
        summed[2],
        summed[3],
        summed[4],
        summed[5],
        summed[6],
        summed[7],
        summed[8],
        summed[9],
    )


bf16 = jnp.bfloat16
f32 = jnp.float32
MESH = pl.DeviceIdType.MESH
CELLS = GRID * GRID
POOLED = POOL * POOL
TILE = 96
PIECES = 4
CHUNKS = 8


def dot(left, right, left_dim, right_dim):
    return lax.dot_general(
        left, right, (((left_dim,), (right_dim,)), ((), ())), preferred_element_type=f32
    )


def split_low(values):
    high = values.astype(bf16)
    return high, (values - high.astype(f32)).astype(bf16)


def edge_masks(extent, channels):
    cells = extent * extent
    index = lax.broadcasted_iota(jnp.int32, (cells, channels), 0).astype(f32)
    row = jnp.floor((index + 0.5) * (1.0 / extent))
    col = index - row * extent
    one = jnp.ones_like(index)
    zero = jnp.zeros_like(index)
    return (
        jnp.where(row >= 0.5, one, zero),
        jnp.where(row <= extent - 1.5, one, zero),
        jnp.where(col >= 0.5, one, zero),
        jnp.where(col <= extent - 1.5, one, zero),
    )


def conv_forward(act, taps, extent, masks):
    above, below, left, right = masks
    cells = extent * extent
    up = pltpu.roll(act, extent, 0) * above
    down = pltpu.roll(act, cells - extent, 0) * below
    sums = [up * taps[q] + act * taps[3 + q] + down * taps[6 + q] for q in range(3)]
    return (
        sums[1]
        + pltpu.roll(sums[0], 1, 0) * left
        + pltpu.roll(sums[2], cells - 1, 0) * right
    )


def conv_backward(upstream, act, taps, extent, masks):
    above, below, left, right = masks
    cells = extent * extent
    sides = [pltpu.roll(upstream, cells - 1, 0) * right, upstream, pltpu.roll(upstream, 1, 0) * left]
    sums = [
        sides[0] * taps[3 * r] + sides[1] * taps[3 * r + 1] + sides[2] * taps[3 * r + 2]
        for r in range(3)
    ]
    d_act = (
        sums[1]
        + pltpu.roll(sums[0], cells - extent, 0) * below
        + pltpu.roll(sums[2], extent, 0) * above
    )
    acts = [pltpu.roll(act, extent, 0) * above, act, pltpu.roll(act, cells - extent, 0) * below]
    d_taps = [
        jnp.sum(acts[r] * sides[q], axis=0, keepdims=True) for r in range(3) for q in range(3)
    ]
    return d_act, d_taps


def slot_rows(ref):
    slots, rows, columns = ref.shape
    return ref[...].reshape(slots * rows, columns)


def layer_kernel(
    patches_in, side_in, wr_a_in, taps_a_in, we_a_in, gain_a_in, wr_b_in, taps_b_in, we_b_in, gain_b_in,
    w_in_in, w_out_in, cot_in,
    tok_out, dpat_out, gout_out, gin_out, gblk_out, gsml_out, cot_all, gfl,
    xp, gw, gws, red_a, spa_a, nar_a, norm_a, inv_a, yhi, ylo, dy, dlow, pp,
    tw, poolv, red_b, spa_b, nar_b, norm_b, inv_b,
    wi, wo, qs, actv, slope, dpre, dtv, tp, cr, ps, rl, tstage,
    dps, dr, dz, gos, gis, gyl, land,
    wgs, wgc, xs, xr, zs, zr, ys, yr, sm, smc, smx, smz, smy, gfin,
    loc, w_s, w_rz, w_rx, w_rc, sw_s, sw_r, sy_s, sy_r, q_s, q_r, q_cs, q_rc,
    dt_s, dt_r, dt_cs, dt_cr, t_cs, t_cr, t_s, t_r, credit,
    d_cs, d_cr, d_zs, d_zr, gy_s, gy_r, gx_s, gx_r, ga_s, ga_r, gc_s, gc_r, gl,
    gr_s, gr_r,
):
    dp_at = lax.axis_index("dp")
    mp_at = lax.axis_index("mp")
    y = lax.div(dp_at, 2)
    c = lax.rem(dp_at, 2)
    z = lax.div(mp_at, 2)
    x = lax.rem(mp_at, 2)
    zn = 4

    def device(x_at, y_at, z_at, c_at):
        return (2 * y_at + c_at, 2 * z_at + x_at)

    twin = device(x, y, z, 1 - c)
    x_peer = device(1 - x, y, z, c)
    y_peer = device(x, 1 - y, z, c)
    z_high = lax.div(z, 2)
    z_low = lax.rem(z, 2)
    z_near = z + 1 - 2 * z_low
    z_far = z + 2 - 4 * z_high
    z_peer = device(x, y, z_near, c)
    far_peer = device(x, y, z_far, c)
    cross = device(x, y, z_far, 1 - c)
    corner = device(1 - x, y, z_near, c)
    slot_own = 2 * z_low + x
    slot_x = 2 * z_low + 1 - x
    slot_z = 2 * (1 - z_low) + x
    slot_corner = 2 * (1 - z_low) + 1 - x

    def z_at(step):
        return lax.rem(z + step + zn, zn)

    def z_dev(z_of):
        return device(x, y, z_of, c)

    def remote(src, dst, send, recv, to):
        return pltpu.make_async_remote_copy(
            src_ref=src, dst_ref=dst, send_sem=send, recv_sem=recv, device_id=to, device_id_type=MESH
        )

    def start(src, dst, send, recv, to):
        remote(src, dst, send, recv, to).start()

    def arrived(dst, recv):
        pltpu.make_async_copy(dst, dst, recv).wait()

    def left_here(src, send):
        pltpu.make_async_copy(src, src, send).wait()

    own = z_high == c

    load_patches = pltpu.make_async_copy(patches_in, xp, loc.at[0])
    me = 2 * slot_own + c
    load_patches.start()

    own_rows = pl.ds(pl.multiple_of(16 * c, 16), 16)
    gw[c, mp_at, 0:16, :] = wr_a_in[own_rows, :]
    gw[c, mp_at, 32:48, :] = wr_b_in[own_rows, :]
    gw[c, mp_at, 16:32, :] = we_a_in[own_rows, :]
    gw[c, mp_at, 48:64, :] = we_b_in[own_rows, :]
    unit = lax.broadcasted_iota(jnp.int32, (32, 256), 0)
    lane = lax.broadcasted_iota(jnp.int32, (32, 256), 1)
    place = 16 * mp_at + jnp.where(unit >= 16, unit + 112, unit)
    spread = jnp.where(lane == place, 1.0, 0.0).astype(bf16)
    gws[c, mp_at] = jnp.zeros((16, 256), f32)

    @pl.when(c == 0)
    def _():
        gws[0, mp_at, 0:9, :] = dot(taps_a_in[...], spread, 1, 0)
        gws[0, mp_at, 9:10, 0:128] = gain_a_in[...].astype(f32).reshape(1, 128)

    @pl.when(c == 1)
    def _():
        gws[1, mp_at, 0:9, :] = dot(taps_b_in[...], spread, 1, 0)
        gws[1, mp_at, 9:10, 0:128] = gain_b_in[...].astype(f32).reshape(1, 128)

    barrier = pltpu.get_barrier_semaphore()
    peers = [twin, x_peer, cross, y_peer, corner] + [z_dev(z_at(k)) for k in range(1, zn)]
    for peer in peers:
        pl.semaphore_signal(barrier, inc=1, device_id=peer, device_id_type=MESH)
    pl.semaphore_wait(barrier, len(peers))

    spans = ((0, 16), (16, 16), (32, 32))

    def w_part(b, core, i):
        if b == 3:
            return gws.at[core, i]
        return gw.at[core, i, pl.ds(spans[b][0], spans[b][1])]

    def w_own(b):
        part = w_part(b, c, mp_at)
        for k in range(1, zn):
            start(part, part, w_s.at[b, k - 1], w_rz.at[b, k], z_dev(z_at(k)))
        start(part, part, w_s.at[b, 3], w_rx.at[b, z], x_peer)
        start(part, part, w_s.at[b, 7], w_rc.at[b, mp_at], twin)

    def w_forward(b):
        for k in range(1, zn):
            z_of = z_at(-k)
            i = 2 * z_of + x
            part = w_part(b, c, i)
            arrived(part, w_rz.at[b, k])
            start(part, part, w_s.at[b, 3 + k], w_rx.at[b, z_of], x_peer)
            start(part, part, w_s.at[b, 7 + k], w_rc.at[b, i], twin)

    def w_over(b):
        for k in range(zn):
            z_of = z_at(-k)
            i = 2 * z_of + 1 - x
            part = w_part(b, c, i)
            arrived(part, w_rx.at[b, z_of])
            start(part, part, w_s.at[b, 11 + k], w_rc.at[b, i], twin)

    def w_finish(b):
        for i in range(8):
            arrived(w_part(b, 1 - c, i), w_rc.at[b, i])

    width = cot_in.shape[1] // PIECES

    def cot(slot, c_of, p):
        return cot_all.at[slot, c_of, :, pl.ds(pl.multiple_of(p * width, width), width)]

    def cot_mine(p):
        return cot_in.at[:, pl.ds(pl.multiple_of(p * width, width), width)]

    def cot_twin(slot, p):
        part = cot(slot, c, p)
        start(part, part, dt_cs.at[p, slot], dt_cr.at[p, slot], twin)

    def cot_own_z(p):
        start(cot_mine(p), cot(slot_own, c, p), dt_s.at[p, 1], dt_r.at[p, 1], z_peer)

    def cot_own_x(p):
        start(cot_mine(p), cot(slot_own, c, p), dt_s.at[p, 0], dt_r.at[p, 0], x_peer)

    def cot_own_twin(p):
        start(cot_mine(p), cot(slot_own, c, p), dt_cs.at[p, slot_own], dt_cr.at[p, slot_own], twin)

    def cot_over_z(p):
        part = cot(slot_z, c, p)
        arrived(part, dt_r.at[p, 1])
        start(part, part, dt_s.at[p, 2], dt_r.at[p, 2], x_peer)
        cot_twin(slot_z, p)

    def cot_over_x(p):
        arrived(cot(slot_x, c, p), dt_r.at[p, 0])
        cot_twin(slot_x, p)

    def cot_corner(p):
        arrived(cot(slot_corner, c, p), dt_r.at[p, 2])
        cot_twin(slot_corner, p)

    chunk = w_out_in.shape[1] // CHUNKS

    def w_half(ref, j, half):
        if j == 0:
            return ref.at[pl.ds(pl.multiple_of(512 * half, 512), 512)]
        return ref.at[:, pl.ds(pl.multiple_of((j - 1) * width + half * chunk, chunk), chunk)]

    def swap_refs(j):
        return (w_in_in, wi) if j == 0 else (w_out_in, wo)

    def swap_send(j):
        src, dst = swap_refs(j)

        @pl.when(own)
        def _():
            pltpu.make_async_copy(w_half(src, j, y), w_half(dst, j, y), sw_r.at[j]).start()
            pltpu.make_async_copy(w_half(src, j, 1 - y), w_half(dst, j, 1 - y), sy_r.at[j]).start()

        @pl.when(jnp.logical_not(own))
        def _():
            start(w_half(src, j, y), w_half(dst, j, y), sw_s.at[j], sw_r.at[j], cross)

    def swap_forward(j):
        part = w_half(swap_refs(j)[1], j, y)
        arrived(part, sw_r.at[j])

        @pl.when(jnp.logical_not(own))
        def _():
            start(part, part, sy_s.at[j], sy_r.at[j], y_peer)

    def swap_ready(j):
        arrived(w_half(swap_refs(j)[1], j, 1 - y), sy_r.at[j])

    def reduce_weights(b):
        return gw[:, :, 32 * b : 32 * b + 16, :].reshape(256, 1024)

    def expand_weights(b):
        return gw[:, :, 32 * b + 16 : 32 * b + 32, :].reshape(256, 1024)

    def small_weights(b):
        total = gws[b, 0, 0:9, :]
        for i in range(1, 8):
            total = total + gws[b, i, 0:9, :]
        tw[b, 0:9, 0:256] = total
        for i in range(8):
            tw[b, 9:10, 128 * i : 128 * i + 128] = gws[b, i, 9:10, 0:128]
        return tw[b, 9:10, :]

    def lanes_of(h):
        return pl.ds(pl.multiple_of(h * 128, 128), 128)

    def tap_rows(b, lanes):
        return [tw[b, k : k + 1, lanes] for k in range(9)]

    def normalise(wide_ref, ref, inv_ref, rows):
        widened = wide_ref[rows, :]
        centred = widened - jnp.mean(widened, axis=1, keepdims=True)
        inv = lax.rsqrt(jnp.mean(centred * centred, axis=1, keepdims=True) + epsilon)
        normed = centred * inv
        ref[rows, :] = normed.astype(ref.dtype)
        inv_ref[rows, :] = jnp.broadcast_to(inv, (normed.shape[0], 128))
        return normed

    side = side_in[0].astype(f32)

    def cell_mask():
        index = lax.broadcasted_iota(jnp.int32, (CELLS, 128), 0).astype(f32)
        row = jnp.floor((index + 0.5) * (1.0 / GRID))
        col = index - row * GRID
        return jnp.where((row < side - 0.5) & (col < side - 0.5), 1.0, 0.0).astype(f32)


    def first_conv():
        small_weights(0)
        load_patches.wait()
        red_a[...] = dot(xp[...], reduce_weights(0), 1, 1)

        def conv_half_a(h, carry):
            lanes = lanes_of(h)
            reduced = red_a[:, lanes]
            activated = reduced * jax.nn.sigmoid(reduced) * cell_mask()
            spatial = conv_forward(activated, tap_rows(0, lanes), GRID, edge_masks(GRID, 128))
            spa_a[:, lanes] = spatial
            nar_a[:, lanes] = (spatial * jax.nn.sigmoid(spatial)).astype(bf16)
            return carry

        lax.fori_loop(0, 2, conv_half_a, 0)

    def first_norm():
        dy[...] = dot(nar_a[...], expand_weights(0), 1, 0)
        gain_a = tw[0, 9:10, :]

        def norm_tile(t, carry):
            rows = pl.ds(pl.multiple_of(t * TILE, TILE), TILE)
            normed = normalise(dy, norm_a, inv_a, rows)
            result = xp[rows, :].astype(f32) + normed * gain_a
            high, low = split_low(result)
            yhi[rows, :] = high
            ylo[rows, :] = low
            return carry

        lax.fori_loop(0, CELLS // TILE, norm_tile, 0)

    def first_pool():
        cell = lax.broadcasted_iota(jnp.int32, (POOLED, CELLS), 1).astype(f32)
        bin_of = lax.broadcasted_iota(jnp.int32, (POOLED, CELLS), 0).astype(f32)
        cell_row = jnp.floor((cell + 0.5) * (1.0 / GRID))
        cell_col = cell - cell_row * GRID
        bin_row = jnp.floor((bin_of + 0.5) * (1.0 / POOL))
        bin_col = bin_of - bin_row * POOL

        def table(bins, at):
            lower = jnp.floor((bins * side + 0.5) * (1.0 / POOL))
            upper = jnp.floor(((bins + 1.0) * side + (POOL - 0.5)) * (1.0 / POOL))
            return jnp.where((at > lower - 0.5) & (at < upper - 0.5), 1.0 / (upper - lower), 0.0)

        pp[...] = (table(bin_row, cell_row) * table(bin_col, cell_col)).astype(bf16)
        poolv[...] = dot(pp[...], yhi[...], 1, 0) + dot(pp[...], ylo[...], 1, 0)

    def second_forward():
        gain_b = small_weights(1)
        pooled = poolv[...]
        reduced_b = dot(pooled.astype(bf16), reduce_weights(1), 1, 1)
        red_b[...] = reduced_b
        activated_b = reduced_b * jax.nn.sigmoid(reduced_b)
        spatial_b = conv_forward(activated_b, tap_rows(1, pl.ds(0, 256)), POOL, edge_masks(POOL, 256))
        spa_b[...] = spatial_b
        nar_b[...] = (spatial_b * jax.nn.sigmoid(spatial_b)).astype(bf16)
        norm_b[...] = dot(nar_b[...], expand_weights(1), 1, 0)
        normed_b = normalise(norm_b, norm_b, inv_b, pl.ds(0, POOLED))
        qs[me] = (pooled + normed_b * gain_b).astype(bf16)

    def query_to(k, to):
        start(qs.at[me], qs.at[me], q_s.at[k], q_r.at[k], to)

    def query_twin():
        start(qs.at[me], qs.at[me], q_s.at[3], q_rc.at[slot_own], twin)

    def query_from(k):
        slot = (slot_x, slot_z, slot_corner)[k]
        part = qs.at[2 * slot + c]
        arrived(part, q_r.at[k])
        start(part, part, q_cs.at[k], q_rc.at[slot], twin)

    def query_all():
        for slot in (slot_own, slot_x, slot_z, slot_corner):
            arrived(qs.at[2 * slot + 1 - c], q_rc.at[slot])

    def hidden_units():
        dpre[...] = dot(slot_rows(qs), wi[...], 1, 0)

        def gelu_tile(t, carry):
            rows = pl.ds(pl.multiple_of(t * POOLED, POOLED), POOLED)
            hidden = dpre[rows, :]
            phi = 0.5 * (1.0 + lax.erf(hidden * root_half))
            actv[rows, :] = (hidden * phi).astype(bf16)
            slope[rows, :] = (
                phi + hidden * jnp.exp(-0.5 * hidden * hidden) * inv_root_tau
            ).astype(bf16)
            return carry

        lax.fori_loop(0, 8, gelu_tile, 0)
        dpre[...] = jnp.zeros_like(dpre)

    def item_part(i):
        b = lax.rem(i, 2)

        @pl.when(i >= 2)
        def _():
            left_here(tp.at[b], t_cs.at[b])
            pl.semaphore_wait(credit, 1)

        weights = wo[:, pl.ds(pl.multiple_of(i * chunk, chunk), chunk)]
        partial = dot(actv[...], weights, 1, 0).astype(bf16)
        partial = partial.reshape(4, 2, POOLED, chunk)

        @pl.when(c == 0)
        def _():
            ps[i] = partial[:, 0]
            tp[b] = partial[:, 1]

        @pl.when(c == 1)
        def _():
            ps[i] = partial[:, 1]
            tp[b] = partial[:, 0]

        start(tp.at[b], cr.at[b], t_cs.at[b], t_cr.at[b], twin)

    def item_pair(i):
        b = lax.rem(i, 2)
        arrived(cr.at[b], t_cr.at[b])

        def add(d, carry):
            ps[i, d] = (ps[i, d].astype(f32) + cr[b, d].astype(f32)).astype(bf16)
            return carry

        lax.fori_loop(0, 4, add, 0)

        @pl.when(i < CHUNKS - 2)
        def _():
            pl.semaphore_signal(credit, inc=1, device_id=twin, device_id_type=MESH)

        start(ps.at[i, slot_corner], rl.at[i, 0], t_s.at[i, 0], t_r.at[i, 0], x_peer)
        start(ps.at[i, slot_x], rl.at[i, 1], t_s.at[i, 1], t_r.at[i, 1], x_peer)

    def item_pass(i):
        arrived(rl.at[i, 0], t_r.at[i, 0])
        ps[i, slot_z] = (ps[i, slot_z].astype(f32) + rl[i, 0].astype(f32)).astype(bf16)
        start(ps.at[i, slot_z], rl.at[i, 2], t_s.at[i, 2], t_r.at[i, 2], z_peer)

    def tok_slice(i):
        return tok_out.at[:, pl.ds(pl.multiple_of(i * chunk, chunk), chunk)]

    def item_final(i):
        b = lax.rem(i, 2)

        @pl.when(i >= 2)
        def _():
            left_here(tstage.at[b], gl.at[8 + b])

        arrived(rl.at[i, 1], t_r.at[i, 1])
        arrived(rl.at[i, 2], t_r.at[i, 2])
        tstage[b] = (
            ps[i, slot_own].astype(f32) + rl[i, 1].astype(f32) + rl[i, 2].astype(f32)
        ).astype(bf16)
        pltpu.make_async_copy(tstage.at[b], tok_slice(i), gl.at[8 + b]).start()

    def piece_rows(p):
        for slot in range(4):
            arrived(cot(slot, 1 - c, p), dt_cr.at[p, slot])

            @pl.when(slot_own != slot)
            def _():
                part = cot_all.at[slot, :, :, pl.ds(p * width, width)]
                pltpu.make_async_copy(part, dtv.at[pl.ds(2 * slot, 2)], loc.at[3]).start()

        pltpu.make_async_copy(cot(slot_own, 1 - c, p), dtv.at[2 * slot_own + 1 - c], loc.at[3]).start()
        pltpu.make_async_copy(cot_mine(p), dtv.at[2 * slot_own + c], loc.at[3]).start()
        pltpu.make_async_copy(dtv, dtv, loc.at[3]).wait()

    def half_lanes(half):
        return pl.ds(pl.multiple_of(half * chunk, chunk), chunk)

    def piece_lanes(h):
        return dtv[:, :, half_lanes(h)].reshape(8 * POOLED, chunk)

    def hidden_part(p):
        def hidden_half(h, carry):
            weights = wo[:, pl.ds(pl.multiple_of(p * width + h * chunk, chunk), chunk)]
            dpre[...] += dot(piece_lanes(h), weights, 1, 1)
            return carry

        lax.fori_loop(0, 2, hidden_half, 0)

    def row_part(slot):
        rows = pl.ds(pl.multiple_of(slot * (2 * POOLED), 2 * POOLED), 2 * POOLED)
        d_hidden = (dpre[rows, :] * slope[rows, :].astype(f32)).astype(bf16)
        half = lax.div(slot, 2)
        place = pl.ds(pl.multiple_of((slot - 2 * half) * (2 * POOLED), 2 * POOLED), 2 * POOLED)
        ylo[place, pl.ds(pl.multiple_of(half * 512, 512), 512)] = d_hidden
        dps[slot] = dot(d_hidden, wi[...], 1, 1).astype(bf16).reshape(2, POOLED, 1024)
        start(dps.at[slot, 1 - c], dr.at[slot], d_cs.at[slot], d_cr.at[slot], twin)

    def in_turn(k):
        return jnp.where(k == 0, slot_corner, jnp.where(k == 1, slot_x, jnp.where(k == 2, slot_z, slot_own)))

    def row_gradients():
        def one(k, carry):
            @pl.when(k < 4)
            def _():
                row_part(in_turn(k))

            slot = in_turn(k - 1)

            @pl.when(k >= 1)
            def _():
                arrived(dr.at[slot], d_cr.at[slot])
                dps[slot, c] = (dps[slot, c].astype(f32) + dr[slot].astype(f32)).astype(bf16)

            @pl.when(k == 1)
            def _():
                start(dps.at[slot, c], dz.at[2], d_zs.at[2], d_zr.at[2], corner)

            @pl.when(k == 2)
            def _():
                start(dps.at[slot, c], dz.at[0], d_zs.at[0], d_zr.at[0], x_peer)

            @pl.when(k == 3)
            def _():
                start(dps.at[slot, c], dz.at[1], d_zs.at[1], d_zr.at[1], z_peer)

            return carry

        lax.fori_loop(0, 5, one, 0)

    def grad_half(j, half):
        if j == PIECES:
            return gis.at[pl.ds(pl.multiple_of(512 * half, 512), 512)]
        return gos.at[j, :, half_lanes(half)]

    def out_half(j, half):
        if j == PIECES:
            return gin_out.at[pl.ds(pl.multiple_of(512 * half, 512), 512)]
        return gout_out.at[:, pl.ds(pl.multiple_of(j * width + half * chunk, chunk), chunk)]

    def grad_send(j, h):
        rows = pl.ds(256 * h, 256)
        if j == PIECES:
            part = gis.at[pl.ds(pl.multiple_of(512 * (1 - y) + 256 * h, 256), 256)]
        else:
            part = gos.at[j, rows, half_lanes(1 - y)]
        start(part, gyl.at[j, rows], gy_s.at[j, h], gy_r.at[j, h], y_peer)

    def grad_part(p):
        def one_half(h, carry):
            gos[p, :, half_lanes(h)] = dot(actv[...], piece_lanes(h), 0, 0).astype(bf16)
            return carry

        lax.fori_loop(0, 2, one_half, 0)

    def gin_part():
        gis[...] = (
            dot(qs[0:4].reshape(4 * POOLED, 1024), ylo[:, 0:512], 0, 0)
            + dot(qs[4:8].reshape(4 * POOLED, 1024), ylo[:, 512:1024], 0, 0)
        ).astype(bf16)

    def grad_pair(j):
        mine = grad_half(j, y)
        for h in range(2):
            arrived(gyl.at[j, pl.ds(256 * h, 256)], gy_r.at[j, h])
        mine[...] = (mine[...].astype(f32) + gyl[j].astype(f32)).astype(bf16)

        @pl.when(jnp.logical_not(own))
        def _():
            start(mine, gfl.at[j], gx_s.at[j], gx_r.at[j], far_peer)

    def grad_sum(j):
        @pl.when(own)
        def _():
            mine = grad_half(j, y)
            arrived(gfl.at[j], gx_r.at[j])
            load = pltpu.make_async_copy(gfl.at[j], land, loc.at[4])
            load.start()
            load.wait()
            mine[...] = (mine[...].astype(f32) + land[...].astype(f32)).astype(bf16)
            start(mine, out_half(j, y), ga_s.at[j], ga_r.at[j], y_peer)
            start(mine, out_half(j, y), gc_s.at[j, 0], gc_r.at[j, 0], twin)
            pltpu.make_async_copy(mine, out_half(j, y), gl.at[j]).start()

    def grad_last(j):
        @pl.when(own)
        def _():
            other = out_half(j, 1 - y)
            arrived(other, ga_r.at[j])
            start(other, other, gc_s.at[j, 1], gc_r.at[j, 1], twin)

    def grad_done(j):
        for h in range(2):
            left_here(gyl.at[j, pl.ds(256 * h, 256)], gy_s.at[j, h])

        @pl.when(own)
        def _():
            left_here(grad_half(j, y), ga_s.at[j])
            left_here(grad_half(j, y), gc_s.at[j, 0])
            left_here(grad_half(j, y), gc_s.at[j, 1])
            pltpu.make_async_copy(grad_half(j, y), out_half(j, y), gl.at[j]).wait()

        @pl.when(jnp.logical_not(own))
        def _():
            left_here(grad_half(j, y), gx_s.at[j])
            arrived(out_half(j, y), gc_r.at[j, 0])
            arrived(out_half(j, 1 - y), gc_r.at[j, 1])

    def widened_back(d_rows, normed, gain, inv):
        dn = d_rows * gain
        return (
            inv
            * (
                dn
                - jnp.mean(dn, axis=1, keepdims=True)
                - normed * jnp.mean(dn * normed, axis=1, keepdims=True)
            )
        ).astype(bf16)

    def pack_small(t, d_gain):
        for k in range(4):
            sm[t, 9 + k : 10 + k, :] = d_gain[:, 256 * k : 256 * k + 256]
        sm[t, 13:16, :] = jnp.zeros((3, 256), f32)

    passes = ((1, 0, 2, 1), (0, 1, 1, None), (0, 0, 1, 0))

    def share_core(p):
        t, k0, n, small = passes[p]
        kinds = pl.ds(k0, n)
        start(
            wgs.at[t, kinds, pl.ds(pl.multiple_of(128 * (1 - c), 128), 128)], wgc.at[t, kinds],
            gr_s.at[p, 0], gr_r.at[p, 0], twin,
        )
        if small is not None:
            start(sm.at[t], smc.at[t], gr_s.at[p, 1], gr_r.at[p, 1], twin)

    def share_x(p):
        t, k0, n, small = passes[p]
        kinds = pl.ds(k0, n)
        arrived(wgc.at[t, kinds], gr_r.at[p, 0])
        for kind in range(k0, k0 + n):
            for i in range(8):
                rows = pl.ds(pl.multiple_of(128 * c + 16 * i, 16), 16)
                xs[t, kind, i % 2, i // 2] = (
                    wgs[t, kind, rows, :].astype(f32) + wgc[t, kind, 16 * i : 16 * i + 16, :].astype(f32)
                ).astype(bf16)
        start(xs.at[t, kinds, 1 - x], xr.at[t, kinds], gr_s.at[p, 2], gr_r.at[p, 2], x_peer)
        if small is not None:
            arrived(smc.at[t], gr_r.at[p, 1])
            left_here(sm.at[t], gr_s.at[p, 1])
            sm[t] = sm[t] + smc[t]
            start(sm.at[t], smx.at[t], gr_s.at[p, 3], gr_r.at[p, 3], x_peer)

    def share_z(p):
        t, k0, n, small = passes[p]
        kinds = pl.ds(k0, n)
        arrived(xr.at[t, kinds], gr_r.at[p, 2])
        for kind in range(k0, k0 + n):
            zs[t, kind] = (xs[t, kind, x].astype(f32) + xr[t, kind].astype(f32)).astype(bf16)
        for k in range(1, zn):
            d = z_at(k)
            start(
                zs.at[t, kinds, d], zr.at[t, kinds, k - 1], gr_s.at[p, 3 + k], gr_r.at[p, 3 + k], z_dev(d)
            )
        if small is not None:
            arrived(smx.at[t], gr_r.at[p, 3])
            left_here(sm.at[t], gr_s.at[p, 3])
            smz[t, z] = sm[t] + smx[t]
            for k in range(1, zn):
                start(
                    smz.at[t, z], smz.at[t, z], gr_s.at[p, 6 + k], gr_r.at[p, 6 + k], z_dev(z_at(k))
                )

    def share_y(p):
        t, k0, n, small = passes[p]
        kinds = pl.ds(k0, n)
        for k in range(1, zn):
            arrived(zr.at[t, kinds, k - 1], gr_r.at[p, 3 + k])
        for kind in range(k0, k0 + n):
            total_rows = zs[t, kind, z].astype(f32)
            for k in range(1, zn):
                total_rows = total_rows + zr[t, kind, k - 1].astype(f32)
            ys[t, kind] = total_rows.astype(bf16)
        start(ys.at[t, kinds], yr.at[t, kinds], gr_s.at[p, 10], gr_r.at[p, 10], y_peer)
        if small is not None:
            for k in range(1, zn):
                arrived(smz.at[t, z_at(-k)], gr_r.at[p, 6 + k])
            sm[t] = (smz[t, 0] + smz[t, 1]) + (smz[t, 2] + smz[t, 3])
            start(sm.at[t], smy.at[t], gr_s.at[p, 11], gr_r.at[p, 11], y_peer)

    def share_twin(p):
        t, k0, n, small = passes[p]
        kinds = pl.ds(k0, n)
        arrived(yr.at[t, kinds], gr_r.at[p, 10])
        for kind in range(k0, k0 + n):
            gfin[c, t, kind] = ys[t, kind].astype(f32) + yr[t, kind].astype(f32)
        part = gfin.at[c, t, kinds]
        start(part, part, gr_s.at[p, 12], gr_r.at[p, 12], twin)
        if small is not None:
            arrived(smy.at[t], gr_r.at[p, 11])
            gsml_out[t] = sm[t] + smy[t]

    def share_done(p):
        t, k0, n, small = passes[p]
        kinds = pl.ds(k0, n)
        arrived(gfin.at[1 - c, t, kinds], gr_r.at[p, 12])
        for kind in range(k0, k0 + n):
            for h in range(2):
                gblk_out[t, kind, 16 * h : 16 * h + 16, :] = gfin[h, t, kind]
        left_here(wgc.at[t, kinds], gr_s.at[p, 0])
        left_here(xr.at[t, kinds], gr_s.at[p, 2])
        for k in range(1, zn):
            left_here(ys.at[t, kinds], gr_s.at[p, 3 + k])
        left_here(ys.at[t, kinds], gr_s.at[p, 10])
        left_here(gfin.at[c, t, kinds], gr_s.at[p, 12])
        if small is not None:
            for k in range(1, zn):
                left_here(sm.at[t], gr_s.at[p, 6 + k])
            left_here(sm.at[t], gr_s.at[p, 11])

    def back_second():
        total = dps[slot_own, c].astype(f32)
        for k in range(3):
            arrived(dz.at[k], d_zr.at[k])
            total = total + dz[k].astype(f32)
        normed_b = norm_b[...]
        d_gain_b = jnp.sum(total * normed_b, axis=0, keepdims=True)
        gain_b = tw[1, 9:10, :]
        dw_b = widened_back(total, normed_b, gain_b, inv_b[:, 0:1])
        wgs[1, 1] = dot(nar_b[...], dw_b, 0, 0).astype(bf16)
        spatial_b = spa_b[...]
        d_spatial_b = dot(dw_b, expand_weights(1), 1, 1) * silu_slope(spatial_b)
        reduced_b = red_b[...]
        sig_b = jax.nn.sigmoid(reduced_b)
        d_act_b, d_taps_b = conv_backward(
            d_spatial_b, reduced_b * sig_b, tap_rows(1, pl.ds(0, 256)), POOL, edge_masks(POOL, 256)
        )
        d_red_b = (d_act_b * (sig_b * (1.0 + reduced_b * (1.0 - sig_b)))).astype(bf16)
        wgs[1, 0] = dot(d_red_b, poolv[...].astype(bf16), 0, 0).astype(bf16)
        for k in range(9):
            sm[1, k : k + 1, :] = d_taps_b[k]
        pack_small(1, d_gain_b)
        d_pool = total + dot(d_red_b, reduce_weights(1), 1, 0)
        high, low = split_low(d_pool)
        dy[...] = dot(pp[...], high, 0, 0) + dot(pp[...], low, 0, 0)

    def back_first_norm():
        gain_a = tw[0, 9:10, :]

        def back_tile(t, d_gain):
            rows = pl.ds(pl.multiple_of(t * TILE, TILE), TILE)
            d_rows = dy[rows, :]
            normed = norm_a[rows, :].astype(f32)
            yhi[rows, :] = widened_back(d_rows, normed, gain_a, inv_a[rows, 0:1])
            return d_gain + jnp.sum(d_rows * normed, axis=0, keepdims=True)

        d_gain_a = lax.fori_loop(0, CELLS // TILE, back_tile, jnp.zeros((1, 1024), f32))
        pack_small(0, d_gain_a)
        wgs[0, 1] = dot(nar_a[...], yhi[...], 0, 0).astype(bf16)

    def back_first_conv():
        spa_a[...] = dot(yhi[...], expand_weights(0), 1, 1) * silu_slope(spa_a[...])

        def conv_back_half_a(h, carry):
            lanes = lanes_of(h)
            reduced = red_a[:, lanes]
            sig = jax.nn.sigmoid(reduced)
            mask = cell_mask()
            d_act, d_taps = conv_backward(
                spa_a[:, lanes], reduced * sig * mask, tap_rows(0, lanes), GRID, edge_masks(GRID, 128)
            )
            dlow[:, lanes] = (d_act * mask * (sig * (1.0 + reduced * (1.0 - sig)))).astype(bf16)
            for k in range(9):
                sm[0, k : k + 1, lanes] = d_taps[k]
            return carry

        lax.fori_loop(0, 2, conv_back_half_a, 0)
        wgs[0, 0] = dot(dlow[...], xp[...], 0, 0).astype(bf16)

    store_dpat = pltpu.make_async_copy(dy, dpat_out, loc.at[5])

    def back_first_rows():
        dy[...] += dot(dlow[...], reduce_weights(0), 1, 0)
        store_dpat.start()

    w_own(0)
    w_own(1)
    cot_own_x(3)
    w_own(3)
    w_forward(0)
    w_own(2)
    w_forward(1)
    w_forward(3)
    w_over(0)
    cot_own_z(0)
    cot_own_z(1)
    w_over(1)
    cot_own_x(0)
    w_over(3)
    w_finish(3)
    swap_send(0)
    cot_own_twin(2)
    cot_over_x(3)
    w_finish(0)
    cot_own_twin(0)
    w_forward(2)
    first_conv()
    w_finish(1)
    first_norm()
    swap_send(1)
    w_over(2)
    cot_over_z(0)
    w_finish(2)
    first_pool()
    second_forward()
    query_to(1, z_peer)
    query_to(0, x_peer)
    query_to(2, corner)
    swap_forward(0)
    cot_own_x(2)
    query_twin()
    swap_send(2)
    cot_own_twin(1)
    query_from(0)
    cot_corner(0)
    cot_over_x(0)
    cot_own_z(2)
    piece_rows(0)
    query_from(1)
    swap_forward(1)
    swap_send(3)
    query_from(2)
    swap_ready(0)
    cot_own_x(1)
    query_all()
    swap_ready(1)
    cot_own_z(3)
    swap_forward(2)
    hidden_units()

    part_at = (0, 2, 3, 6, 8, 9, 13, 20)
    pair_at = (1, 4, 6, 7, 11, 15, 16, 21)
    pass_at = (5, 9, 10, 14, 16, 17, 19, 23)
    final_at = (12, 14, 17, 18, 20, 22, 24, 25)

    def item_of(s, places):
        number = jnp.int32(-1)
        for item, place in enumerate(places):
            number = jnp.where(s == place, item, number)
        return number

    def main_step(s, carry):
        def at(step):
            return pl.when(s == step)

        @at(1)
        def _():
            cot_own_twin(3)
            grad_part(0)
            cot_over_z(1)
            hidden_part(0)
            cot_over_x(2)
            swap_ready(2)
            grad_send(0, 1)
            cot_over_z(2)
            cot_over_x(1)

        @at(2)
        def _():
            grad_send(0, 0)
            swap_send(4)
            cot_corner(1)

        @at(3)
        def _():
            swap_forward(3)

        @at(4)
        def _():
            piece_rows(1)
            hidden_part(1)
            grad_pair(0)
            cot_over_z(3)
            grad_part(1)
            cot_corner(2)
            swap_forward(4)
            grad_send(1, 1)
            piece_rows(2)
            grad_send(1, 0)

        @at(5)
        def _():
            swap_ready(3)
            hidden_part(2)
            grad_part(2)
            grad_send(2, 0)
            cot_corner(3)

        @at(6)
        def _():
            piece_rows(3)
            swap_ready(4)
            hidden_part(3)
            row_gradients()

        @at(8)
        def _():
            grad_send(2, 1)
            grad_pair(1)

        @at(9)
        def _():
            gin_part()
            grad_sum(0)
            grad_pair(2)
            grad_part(3)
            grad_send(3, 1)
            grad_send(3, 0)
            back_second()

        @at(12)
        def _():
            grad_send(PIECES, 1)
            grad_send(PIECES, 0)
            back_first_norm()

        @at(13)
        def _():
            share_core(1)

        @at(14)
        def _():
            share_core(0)

        @at(15)
        def _():
            grad_pair(3)

        @at(16)
        def _():
            grad_sum(2)

        @at(17)
        def _():
            share_x(0)
            share_x(1)
            grad_sum(1)
            grad_pair(PIECES)
            grad_sum(3)

        @at(18)
        def _():
            back_first_conv()

        @at(19)
        def _():
            grad_last(0)

        @at(20)
        def _():
            share_z(0)
            share_core(2)

        @at(21)
        def _():
            share_z(1)
            share_x(2)
            grad_last(2)

        @at(22)
        def _():
            grad_sum(PIECES)
            grad_last(1)

        @at(23)
        def _():
            share_z(2)
            back_first_rows()

        @at(24)
        def _():
            share_y(0)
            share_y(1)
            grad_last(PIECES)
            grad_last(3)

        @at(25)
        def _():
            share_y(2)
            share_twin(0)
            share_twin(1)
            share_twin(2)

        for places, work in (
            (part_at, item_part), (pair_at, item_pair), (pass_at, item_pass), (final_at, item_final)
        ):
            number = item_of(s, places)

            @pl.when(number >= 0)
            def _(number=number, work=work):
                work(number)

        return carry

    lax.fori_loop(0, 26, main_step, 0)

    for p in range(3):
        share_done(p)
    for j in range(1 + PIECES):
        grad_done(j)

        @pl.when(jnp.logical_not(own))
        def _():
            part = w_half(swap_refs(j)[1], j, y)
            left_here(part, sw_s.at[j])
            left_here(part, sy_s.at[j])

    store_dpat.wait()
    for b in range(2):
        pltpu.make_async_copy(tstage.at[b], tok_slice(b), gl.at[8 + b]).wait()
        left_here(tp.at[b], t_cs.at[b])
    for b in range(4):
        for k in range(15):
            left_here(w_part(b, c, 0), w_s.at[b, k])
    for k in range(4):
        left_here(qs.at[0], q_s.at[k])
    for k in range(3):
        left_here(qs.at[0], q_cs.at[k])
    for k in range(4):
        left_here(dps.at[0, 0], d_cs.at[k])
    for k in range(3):
        left_here(dps.at[0, 0], d_zs.at[k])
    for p in range(PIECES):
        for slot in range(4):
            left_here(cot(0, 0, p), dt_cs.at[p, slot])
        for k in range(3):
            left_here(cot(0, 0, p), dt_s.at[p, k])

    def drain_items(i, carry):
        for k in range(3):
            left_here(ps.at[0, 0], t_s.at[i, k])
        return carry

    lax.fori_loop(0, CHUNKS, drain_items, 0)


def layer_call(
    patches, grid_sizes, wr_a, taps_a, we_a, gain_a, wr_b, taps_b, we_b, gain_b, w_in, w_out, d_tokens
):
    any_space = pl.BlockSpec(memory_space=pl.ANY)
    vmem = pl.BlockSpec(memory_space=pltpu.VMEM)
    smem = pl.BlockSpec(memory_space=pltpu.SMEM)
    shape = jax.ShapeDtypeStruct
    width = w_out.shape[1] // PIECES
    chunk = w_out.shape[1] // CHUNKS
    out_shape = (
        shape((POOLED, 4096), bf16),
        shape((CELLS, 1024), f32),
        shape((512, 4096), bf16),
        shape((1024, 512), bf16),
        shape((2, 2, 32, 1024), f32),
        shape((2, 16, 256), f32),
        shape((4, 2, POOLED, 4096), bf16),
        shape((1 + PIECES, 512, width // 2), bf16),
    )
    dma = pltpu.SemaphoreType.DMA
    scratch = [
        pltpu.VMEM((CELLS, 1024), bf16),
        pltpu.VMEM((2, 8, 64, 1024), bf16),
        pltpu.VMEM((2, 8, 16, 256), f32),
        pltpu.VMEM((CELLS, 256), f32),
        pltpu.VMEM((CELLS, 256), f32),
        pltpu.VMEM((CELLS, 256), bf16),
        pltpu.VMEM((CELLS, 1024), bf16),
        pltpu.VMEM((CELLS, 128), f32),
        pltpu.VMEM((CELLS, 1024), bf16),
        pltpu.VMEM((CELLS, 1024), bf16),
        pltpu.VMEM((CELLS, 1024), f32),
        pltpu.VMEM((CELLS, 256), bf16),
        pltpu.VMEM((POOLED, CELLS), bf16),
        pltpu.VMEM((2, 16, 1024), f32),
        pltpu.VMEM((POOLED, 1024), f32),
        pltpu.VMEM((POOLED, 256), f32),
        pltpu.VMEM((POOLED, 256), f32),
        pltpu.VMEM((POOLED, 256), bf16),
        pltpu.VMEM((POOLED, 1024), f32),
        pltpu.VMEM((POOLED, 128), f32),
        pltpu.VMEM((1024, 512), bf16),
        pltpu.VMEM((512, 4096), bf16),
        pltpu.VMEM((8, POOLED, 1024), bf16),
        pltpu.VMEM((8 * POOLED, 512), bf16),
        pltpu.VMEM((8 * POOLED, 512), bf16),
        pltpu.VMEM((8 * POOLED, 512), f32),
        pltpu.VMEM((8, POOLED, width), bf16),
        pltpu.VMEM((2, 4, POOLED, chunk), bf16),
        pltpu.VMEM((2, 4, POOLED, chunk), bf16),
        pltpu.VMEM((CHUNKS, 4, POOLED, chunk), bf16),
        pltpu.VMEM((CHUNKS, 3, POOLED, chunk), bf16),
        pltpu.VMEM((2, POOLED, chunk), bf16),
        pltpu.VMEM((4, 2, POOLED, 1024), bf16),
        pltpu.VMEM((4, POOLED, 1024), bf16),
        pltpu.VMEM((3, POOLED, 1024), bf16),
        pltpu.VMEM((PIECES, 512, width), bf16),
        pltpu.VMEM((1024, 512), bf16),
        pltpu.VMEM((1 + PIECES, 512, width // 2), bf16),
        pltpu.VMEM((512, width // 2), bf16),
        pltpu.VMEM((2, 2, 256, 1024), bf16),
        pltpu.VMEM((2, 2, 128, 1024), bf16),
        pltpu.VMEM((2, 2, 2, 4, 16, 1024), bf16),
        pltpu.VMEM((2, 2, 4, 16, 1024), bf16),
        pltpu.VMEM((2, 2, 4, 16, 1024), bf16),
        pltpu.VMEM((2, 2, 3, 16, 1024), bf16),
        pltpu.VMEM((2, 2, 16, 1024), bf16),
        pltpu.VMEM((2, 2, 16, 1024), bf16),
        pltpu.VMEM((2, 16, 256), f32),
        pltpu.VMEM((2, 16, 256), f32),
        pltpu.VMEM((2, 16, 256), f32),
        pltpu.VMEM((2, 4, 16, 256), f32),
        pltpu.VMEM((2, 16, 256), f32),
        pltpu.VMEM((2, 2, 2, 16, 1024), f32),
        dma((6,)),
        dma((4, 15)),
        dma((4, 4)),
        dma((4, 4)),
        dma((4, 8)),
        dma((1 + PIECES,)),
        dma((1 + PIECES,)),
        dma((1 + PIECES,)),
        dma((1 + PIECES,)),
        dma((4,)),
        dma((3,)),
        dma((3,)),
        dma((4,)),
        dma((PIECES, 3)),
        dma((PIECES, 3)),
        dma((PIECES, 4)),
        dma((PIECES, 4)),
        dma((2,)),
        dma((2,)),
        dma((CHUNKS, 3)),
        dma((CHUNKS, 3)),
        pltpu.SemaphoreType.REGULAR,
        dma((4,)),
        dma((4,)),
        dma((3,)),
        dma((3,)),
        dma((1 + PIECES, 2)),
        dma((1 + PIECES, 2)),
        dma((1 + PIECES,)),
        dma((1 + PIECES,)),
        dma((1 + PIECES,)),
        dma((1 + PIECES,)),
        dma((1 + PIECES, 2)),
        dma((1 + PIECES, 2)),
        dma((10,)),
        dma((3, 13)),
        dma((3, 13)),
    ]
    return pl.pallas_call(
        layer_kernel,
        out_shape=out_shape,
        in_specs=[any_space, smem] + [vmem] * 8 + [any_space] * 3,
        out_specs=(any_space, any_space, any_space, any_space, vmem, vmem, any_space, any_space),
        scratch_shapes=scratch,
        compiler_params=pltpu.CompilerParams(
            collective_id=0, has_side_effects=True, vmem_limit_bytes=VMEM_BYTES
        ),
    )(
        patches, grid_sizes, wr_a, taps_a, we_a, gain_a, wr_b, taps_b, we_b, gain_b, w_in, w_out, d_tokens
    )


VMEM_BYTES = 64 * 1024 * 1024


FINISH = 8


def finish_kernel(
    tok_in, dpat_in, gout_in, gin_in, gblk_in, gsml_in,
    tok, dpat, gout, gin, gra, gta, gea, gga, grb, gtb, geb, ggb,
):
    tok[...] = tok_in[...]
    dpat[...] = dpat_in[...]
    gout[...] = gout_in[...].astype(f32)
    gin[...] = gin_in[...].astype(f32)

    @pl.when(pl.program_id(0) == 0)
    def _():
        mp_at = lax.axis_index("mp")
        for t, outs in enumerate(((gra, gta, gea, gga), (grb, gtb, geb, ggb))):
            reduce, taps, expand, gain = outs
            reduce[...] = gblk_in[t, 0]
            expand[...] = gblk_in[t, 1]
            turned = pltpu.roll(gsml_in[t], lax.rem(256 - 16 * mp_at, 256), 1)
            taps[:, 0:16] = turned[0:9, 0:16]
            taps[:, 16:32] = turned[0:9, 128:144]
            for i in range(8):
                @pl.when(mp_at == i)
                def _(t=t, i=i, gain=gain):
                    lanes = 128 * (i % 2)
                    gain[...] = gsml_in[t, 9 + i // 2 : 10 + i // 2, lanes : lanes + 128]


def finish_call(tokens, d_patches, gout, gin, gblk, gsml):
    shape = jax.ShapeDtypeStruct
    columns = tokens.shape[1] // FINISH

    def whole(*dims):
        return pl.BlockSpec(dims, lambda i: (0,) * len(dims))

    one = [whole(32, 1024), whole(9, 32), whole(32, 1024), whole(1, 128)]
    one_shape = [shape((32, 1024), f32), shape((9, 32), f32), shape((32, 1024), f32), shape((1, 128), f32)]
    return pl.pallas_call(
        finish_kernel,
        grid=(FINISH,),
        out_shape=[
            shape(tokens.shape, bf16),
            shape(d_patches.shape, f32),
            shape(gout.shape, f32),
            shape(gin.shape, f32),
        ]
        + one_shape * 2,
        in_specs=[
            pl.BlockSpec((POOLED, columns), lambda i: (0, i)),
            pl.BlockSpec((CELLS // FINISH, 1024), lambda i: (i, 0)),
            pl.BlockSpec((512 // FINISH, 4096), lambda i: (i, 0)),
            pl.BlockSpec((1024 // FINISH, 512), lambda i: (i, 0)),
            whole(2, 2, 32, 1024),
            whole(2, 16, 256),
        ],
        out_specs=[
            pl.BlockSpec((POOLED, columns), lambda i: (0, i)),
            pl.BlockSpec((CELLS // FINISH, 1024), lambda i: (i, 0)),
            pl.BlockSpec((512 // FINISH, 4096), lambda i: (i, 0)),
            pl.BlockSpec((1024 // FINISH, 512), lambda i: (i, 0)),
        ]
        + one * 2,
        compiler_params=pltpu.CompilerParams(vmem_limit_bytes=VMEM_BYTES),
    )(tokens, d_patches, gout, gin, gblk, gsml)


def fast_body(
    patches, grid_sizes, w_reduce_a, taps_a, w_expand_a, gain_a,
    w_reduce_b, taps_b, w_expand_b, gain_b, w_in, w_out, d_tokens,
):
    results = layer_call(
        patches, grid_sizes, w_reduce_a.T, taps_a, w_expand_a, gain_a,
        w_reduce_b.T, taps_b, w_expand_b, gain_b, w_in, w_out, d_tokens,
    )
    (
        tokens, d_patches, gout, gin, reduce_a, tap_a, expand_a, scale_a, reduce_b, tap_b, expand_b, scale_b
    ) = finish_call(*results[:6])
    return (
        tokens, d_patches,
        reduce_a.T, tap_a, expand_a, scale_a.reshape(-1),
        reduce_b.T, tap_b, expand_b, scale_b.reshape(-1),
        gin, gout,
    )


def solution(mesh):
    in_specs = (
        P(("dp", "mp"), None),
        P(("dp", "mp")),
        P(None, "mp"),
        P(None, "mp"),
        P("mp", None),
        P("mp"),
        P(None, "mp"),
        P(None, "mp"),
        P("mp", None),
        P("mp"),
        P(None, "mp"),
        P("mp", None),
        P(("dp", "mp"), None),
    )
    out_specs = (
        P(("dp", "mp"), None),
        P(("dp", "mp"), None),
        P(None, "mp"),
        P(None, "mp"),
        P("mp", None),
        P("mp"),
        P(None, "mp"),
        P(None, "mp"),
        P("mp", None),
        P("mp"),
        P(None, "mp"),
        P("mp", None),
    )
    fits = mesh.shape["dp"] == 4 and mesh.shape["mp"] == 8
    return jax.shard_map(fast_body if fits else body, mesh=mesh, in_specs=in_specs, out_specs=out_specs, check_vma=False)
```

```python
import jax
import jax.numpy as jnp
from jax import lax
from jax.experimental import pallas as pl
from jax.experimental.pallas import tpu as pltpu
from jax.sharding import PartitionSpec as P

GRID = 24
SMALL_GRID = 16
POOL = 12


epsilon = 1e-05
highest = lax.Precision.HIGHEST
root_half = 0.7071067811865476
inv_root_tau = 0.3989422804014327


def silu_slope(values):
    sigmoid = jax.nn.sigmoid(values)
    return sigmoid * (1.0 + values * (1.0 - sigmoid))


def gelu_exact(values):
    return 0.5 * values * (1.0 + lax.erf(values * root_half))


def gelu_slope(values):
    return (
        0.5 * (1.0 + lax.erf(values * root_half))
        + values * jnp.exp(-0.5 * values * values) * inv_root_tau
    )


def outer_rows(left, right):
    return lax.dot_general(
        left, right, (((0,), (0,)), ((), ())), preferred_element_type=jnp.float32
    )


def times_trans(left, right):
    return lax.dot_general(
        left, right, (((1,), (1,)), ((), ())), preferred_element_type=jnp.float32
    )


def map_padding(ndims):
    return [(0, 0)] * (ndims - 3) + [(1, 1), (1, 1), (0, 0)]


def depthwise(feature_map, tap_weights):
    extent = feature_map.shape[-2]
    padded = jnp.pad(feature_map, map_padding(feature_map.ndim))
    result = jnp.zeros_like(feature_map)
    for tap_row in range(3):
        for tap_col in range(3):
            result = (
                result
                + padded[..., tap_row : tap_row + extent, tap_col : tap_col + extent, :]
                * tap_weights[3 * tap_row + tap_col]
            )
    return result


def depthwise_back(upstream, feature_map, tap_weights):
    extent = upstream.shape[-2]
    upstream_pad = jnp.pad(upstream, map_padding(upstream.ndim))
    feature_pad = jnp.pad(feature_map, map_padding(feature_map.ndim))
    d_feature = jnp.zeros_like(upstream)
    tap_grads = []
    leading = tuple(range(upstream.ndim - 1))
    for tap_row in range(3):
        for tap_col in range(3):
            d_feature = (
                d_feature
                + upstream_pad[
                    ..., 2 - tap_row : 2 - tap_row + extent, 2 - tap_col : 2 - tap_col + extent, :
                ]
                * tap_weights[3 * tap_row + tap_col]
            )
            shifted = feature_pad[..., tap_row : tap_row + extent, tap_col : tap_col + extent, :]
            tap_grads.append(jnp.sum(shifted * upstream, axis=leading))
    return (d_feature, jnp.stack(tap_grads))


def block_forward(feature_rows, low_rows, weights_set, extent):
    w_reduce, tap_weights, w_expand, norm_gain = weights_set
    channels = w_reduce.shape[1]
    row_count = feature_rows.shape[0]
    reduced = jnp.dot(low_rows, w_reduce, preferred_element_type=jnp.float32)
    activated = jax.nn.silu(reduced).reshape(-1, extent, extent, channels)
    spatial = depthwise(activated, tap_weights.astype(jnp.float32)).reshape(row_count, channels)
    narrow = jax.nn.silu(spatial).astype(jnp.bfloat16)
    widened = jnp.dot(narrow, w_expand, preferred_element_type=jnp.float32)
    centred = widened - jnp.mean(widened, axis=1, keepdims=True)
    inv_scale = lax.rsqrt(jnp.mean(centred * centred, axis=1, keepdims=True) + epsilon)
    normed = centred * inv_scale
    result = feature_rows + normed * norm_gain.astype(jnp.float32)
    return (result, (reduced, activated, spatial, narrow, normed, inv_scale))


def block_backward(d_result, low_rows, weights_set, saved):
    w_reduce, tap_weights, w_expand, norm_gain = weights_set
    reduced, activated, spatial, narrow, normed, inv_scale = saved
    d_gain = jnp.sum(d_result * normed, axis=0)
    d_normed = d_result * norm_gain.astype(jnp.float32)
    d_widened = inv_scale * (
        d_normed
        - jnp.mean(d_normed, axis=1, keepdims=True)
        - normed * jnp.mean(d_normed * normed, axis=1, keepdims=True)
    )
    d_widened = d_widened.astype(jnp.bfloat16)
    grad_expand = outer_rows(narrow, d_widened)
    d_spatial = times_trans(d_widened, w_expand) * silu_slope(spatial)
    d_activated, grad_taps = depthwise_back(
        d_spatial.reshape(activated.shape), activated, tap_weights.astype(jnp.float32)
    )
    d_reduced = (d_activated.reshape(reduced.shape) * silu_slope(reduced)).astype(jnp.bfloat16)
    grad_reduce = outer_rows(low_rows, d_reduced)
    d_rows = d_result + times_trans(d_reduced, w_reduce)
    return (d_rows, (grad_reduce, grad_taps, grad_expand, d_gain))


def crop_rows(pixels, extent):
    features = pixels.shape[-1]
    return pixels.reshape(GRID, GRID, features)[:extent, :extent].reshape(extent * extent, features)


def widen_grid(values, extent):
    features = values.shape[-1]
    return jnp.pad(
        values.reshape(extent, extent, features), ((0, GRID - extent), (0, GRID - extent), (0, 0))
    )


def first_forward(weights_set, extent):

    def compute(pixels):
        cropped = crop_rows(pixels, extent)
        result, unused = block_forward(cropped.astype(jnp.float32), cropped, weights_set, extent)
        return widen_grid(result, extent)

    return compute


def first_backward(weights_set, extent):

    def compute(pixels, upstream):
        cropped = crop_rows(pixels, extent)
        sliced = crop_rows(upstream, extent)
        unused, saved = block_forward(cropped.astype(jnp.float32), cropped, weights_set, extent)
        d_rows, grads = block_backward(sliced, cropped, weights_set, saved)
        return (widen_grid(d_rows, extent).reshape(GRID * GRID, -1), grads)

    return compute


def pool_table(grid_side):
    bin_index = lax.iota(jnp.int32, POOL)
    bin_lower = bin_index * grid_side // POOL
    bin_upper = ((bin_index + 1) * grid_side + POOL - 1) // POOL
    cell_index = lax.iota(jnp.int32, GRID)
    inside = (cell_index[None, :] >= bin_lower[:, None]) & (
        cell_index[None, :] < bin_upper[:, None]
    )
    weights = jnp.where(inside, 1.0, 0.0) / (bin_upper - bin_lower)[:, None]
    return weights.astype(jnp.float32)


def body(
    patches,
    grid_sizes,
    w_reduce_a,
    taps_a,
    w_expand_a,
    gain_a,
    w_reduce_b,
    taps_b,
    w_expand_b,
    gain_b,
    w_in,
    w_out,
    d_tokens,
):
    gathered = (
        lax.all_gather(w_reduce_a, "mp", axis=1, tiled=True),
        lax.all_gather(taps_a, "mp", axis=1, tiled=True),
        lax.all_gather(w_expand_a, "mp", axis=0, tiled=True),
        lax.all_gather(gain_a, "mp", axis=0, tiled=True),
        lax.all_gather(w_reduce_b, "mp", axis=1, tiled=True),
        lax.all_gather(taps_b, "mp", axis=1, tiled=True),
        lax.all_gather(w_expand_b, "mp", axis=0, tiled=True),
        lax.all_gather(gain_b, "mp", axis=0, tiled=True),
    )
    first_set = gathered[0:4]
    second_set = gathered[4:8]
    features = patches.shape[1]
    pictures = patches.reshape(-1, GRID * GRID, features)
    picture_count = pictures.shape[0]
    tables = jax.vmap(pool_table)(grid_sizes)

    def forward_one(element):
        pixels, grid_side, pool_weights = element
        result = lax.cond(
            grid_side == GRID,
            first_forward(first_set, GRID),
            first_forward(first_set, SMALL_GRID),
            pixels,
        )
        return jnp.einsum("ia,jb,abd->ijd", pool_weights, pool_weights, result, precision=highest)

    pooled = lax.map(forward_one, (pictures, grid_sizes, tables))
    pooled_rows = pooled.reshape(picture_count * POOL * POOL, features)
    pooled_low = pooled_rows.astype(jnp.bfloat16)
    mixed_rows, second_saved = block_forward(pooled_rows, pooled_low, second_set, POOL)
    queries = mixed_rows.astype(jnp.bfloat16)
    hidden = jnp.dot(
        lax.all_gather(queries, "mp", axis=0, tiled=True), w_in, preferred_element_type=jnp.float32
    )
    active = gelu_exact(hidden).astype(jnp.bfloat16)
    tokens = lax.psum_scatter(
        jnp.dot(active, w_out, preferred_element_type=jnp.float32).astype(jnp.bfloat16),
        "mp",
        scatter_dimension=0,
        tiled=True,
    )
    piece = lax.all_gather(d_tokens, "mp", axis=0, tiled=True)
    d_part = (times_trans(piece, w_out) * gelu_slope(hidden)).astype(jnp.bfloat16)
    grad_out_sum = outer_rows(active, piece)
    d_hidden = d_part
    d_part = d_hidden
    grad_in_part = outer_rows(lax.all_gather(queries, "mp", axis=0, tiled=True), d_part)
    d_part = d_hidden
    d_mixed = lax.psum_scatter(times_trans(d_part, w_in), "mp", scatter_dimension=0, tiled=True)
    d_pooled, second_grads = block_backward(d_mixed, pooled_low, second_set, second_saved)
    d_pooled = d_pooled.reshape(picture_count, POOL, POOL, features)

    def backward_one(totals, element):
        pixels, grid_side, pool_weights, upstream = element
        d_grid = jnp.einsum(
            "ia,jb,ijd->abd", pool_weights, pool_weights, upstream, precision=highest
        )
        d_pixels, grads = lax.cond(
            grid_side == GRID,
            first_backward(first_set, GRID),
            first_backward(first_set, SMALL_GRID),
            pixels,
            d_grid,
        )
        return (
            tuple((total_part + grad_part for total_part, grad_part in zip(totals, grads))),
            d_pixels,
        )

    zero_grads = tuple((jnp.zeros(weight.shape, jnp.float32) for weight in first_set))
    first_grads, d_pictures = lax.scan(
        backward_one, zero_grads, (pictures, grid_sizes, tables, d_pooled)
    )
    d_patches = d_pictures.reshape(-1, features)
    shards = (
        lax.psum_scatter(
            first_grads[0].astype(jnp.bfloat16), "mp", scatter_dimension=1, tiled=True
        ).astype(jnp.float32),
        lax.psum_scatter(
            first_grads[1].astype(jnp.bfloat16), "mp", scatter_dimension=1, tiled=True
        ).astype(jnp.float32),
        lax.psum_scatter(
            first_grads[2].astype(jnp.bfloat16), "mp", scatter_dimension=0, tiled=True
        ).astype(jnp.float32),
        lax.psum_scatter(
            first_grads[3].astype(jnp.bfloat16), "mp", scatter_dimension=0, tiled=True
        ).astype(jnp.float32),
        lax.psum_scatter(
            second_grads[0].astype(jnp.bfloat16), "mp", scatter_dimension=1, tiled=True
        ).astype(jnp.float32),
        lax.psum_scatter(
            second_grads[1].astype(jnp.bfloat16), "mp", scatter_dimension=1, tiled=True
        ).astype(jnp.float32),
        lax.psum_scatter(
            second_grads[2].astype(jnp.bfloat16), "mp", scatter_dimension=0, tiled=True
        ).astype(jnp.float32),
        lax.psum_scatter(
            second_grads[3].astype(jnp.bfloat16), "mp", scatter_dimension=0, tiled=True
        ).astype(jnp.float32),
    )
    summed = (
        lax.psum(shards[0].astype(jnp.bfloat16), "dp").astype(jnp.float32),
        lax.psum(shards[1].astype(jnp.bfloat16), "dp").astype(jnp.float32),
        lax.psum(shards[2].astype(jnp.bfloat16), "dp").astype(jnp.float32),
        lax.psum(shards[3].astype(jnp.bfloat16), "dp").astype(jnp.float32),
        lax.psum(shards[4].astype(jnp.bfloat16), "dp").astype(jnp.float32),
        lax.psum(shards[5].astype(jnp.bfloat16), "dp").astype(jnp.float32),
        lax.psum(shards[6].astype(jnp.bfloat16), "dp").astype(jnp.float32),
        lax.psum(shards[7].astype(jnp.bfloat16), "dp").astype(jnp.float32),
        lax.psum(grad_in_part.astype(jnp.bfloat16), "dp").astype(jnp.float32),
        lax.psum(grad_out_sum.astype(jnp.bfloat16), "dp").astype(jnp.float32),
    )
    return (
        tokens,
        d_patches,
        summed[0],
        summed[1],
        summed[2],
        summed[3],
        summed[4],
        summed[5],
        summed[6],
        summed[7],
        summed[8],
        summed[9],
    )


bf16 = jnp.bfloat16
f32 = jnp.float32
MESH = pl.DeviceIdType.MESH
CELLS = GRID * GRID
POOLED = POOL * POOL
TILE = 96
PIECES = 4
CHUNKS = 8


def dot(left, right, left_dim, right_dim):
    return lax.dot_general(
        left, right, (((left_dim,), (right_dim,)), ((), ())), preferred_element_type=f32
    )


def split_low(values):
    high = values.astype(bf16)
    return high, (values - high.astype(f32)).astype(bf16)


def edge_masks(extent, channels):
    cells = extent * extent
    index = lax.broadcasted_iota(jnp.int32, (cells, channels), 0).astype(f32)
    row = jnp.floor((index + 0.5) * (1.0 / extent))
    col = index - row * extent
    one = jnp.ones_like(index)
    zero = jnp.zeros_like(index)
    return (
        jnp.where(row >= 0.5, one, zero),
        jnp.where(row <= extent - 1.5, one, zero),
        jnp.where(col >= 0.5, one, zero),
        jnp.where(col <= extent - 1.5, one, zero),
    )


def conv_forward(act, taps, extent, masks):
    above, below, left, right = masks
    cells = extent * extent
    up = pltpu.roll(act, extent, 0) * above
    down = pltpu.roll(act, cells - extent, 0) * below
    sums = [up * taps[q] + act * taps[3 + q] + down * taps[6 + q] for q in range(3)]
    return (
        sums[1]
        + pltpu.roll(sums[0], 1, 0) * left
        + pltpu.roll(sums[2], cells - 1, 0) * right
    )


def conv_backward(upstream, act, taps, extent, masks):
    above, below, left, right = masks
    cells = extent * extent
    sides = [pltpu.roll(upstream, cells - 1, 0) * right, upstream, pltpu.roll(upstream, 1, 0) * left]
    sums = [
        sides[0] * taps[3 * r] + sides[1] * taps[3 * r + 1] + sides[2] * taps[3 * r + 2]
        for r in range(3)
    ]
    d_act = (
        sums[1]
        + pltpu.roll(sums[0], cells - extent, 0) * below
        + pltpu.roll(sums[2], extent, 0) * above
    )
    acts = [pltpu.roll(act, extent, 0) * above, act, pltpu.roll(act, cells - extent, 0) * below]
    d_taps = [
        jnp.sum(acts[r] * sides[q], axis=0, keepdims=True) for r in range(3) for q in range(3)
    ]
    return d_act, d_taps


def slot_rows(ref):
    slots, rows, columns = ref.shape
    return ref[...].reshape(slots * rows, columns)


def layer_kernel(
    patches_in, side_in, wr_a_in, taps_a_in, we_a_in, gain_a_in, wr_b_in, taps_b_in, we_b_in, gain_b_in,
    w_in_in, w_out_in, cot_in,
    tok_out, dpat_out, gout_out, gin_out, gblk_out, gsml_out, cot_all, gfl,
    xp, gw, gws, red_a, spa_a, nar_a, norm_a, inv_a, yhi, ylo, dy, dlow, pp,
    tw, poolv, red_b, spa_b, nar_b, norm_b, inv_b,
    wi, wo, qs, actv, slope, dpre, dtv, tp, cr, ps, rl, tstage,
    dps, dr, dz, gos, gis, gyl, land,
    wgs, wgc, xs, xr, zs, zr, ys, yr, sm, smc, smx, smz, smy, gfin,
    loc, w_s, w_rz, w_rx, w_rc, sw_s, sw_r, sy_s, sy_r, q_s, q_r, q_cs, q_rc,
    dt_s, dt_r, dt_cs, dt_cr, t_cs, t_cr, t_s, t_r, credit,
    d_cs, d_cr, d_zs, d_zr, gy_s, gy_r, gx_s, gx_r, ga_s, ga_r, gc_s, gc_r, gl,
    gr_s, gr_r,
):
    dp_at = lax.axis_index("dp")
    mp_at = lax.axis_index("mp")
    y = lax.div(dp_at, 2)
    c = lax.rem(dp_at, 2)
    z = lax.div(mp_at, 2)
    x = lax.rem(mp_at, 2)
    zn = 4

    def device(x_at, y_at, z_at, c_at):
        return (2 * y_at + c_at, 2 * z_at + x_at)

    twin = device(x, y, z, 1 - c)
    x_peer = device(1 - x, y, z, c)
    y_peer = device(x, 1 - y, z, c)
    z_high = lax.div(z, 2)
    z_low = lax.rem(z, 2)
    z_near = z + 1 - 2 * z_low
    z_far = z + 2 - 4 * z_high
    z_peer = device(x, y, z_near, c)
    far_peer = device(x, y, z_far, c)
    cross = device(x, y, z_far, 1 - c)
    corner = device(1 - x, y, z_near, c)
    slot_own = 2 * z_low + x
    slot_x = 2 * z_low + 1 - x
    slot_z = 2 * (1 - z_low) + x
    slot_corner = 2 * (1 - z_low) + 1 - x

    def z_at(step):
        return lax.rem(z + step + zn, zn)

    def z_dev(z_of):
        return device(x, y, z_of, c)

    def remote(src, dst, send, recv, to):
        return pltpu.make_async_remote_copy(
            src_ref=src, dst_ref=dst, send_sem=send, recv_sem=recv, device_id=to, device_id_type=MESH
        )

    def start(src, dst, send, recv, to):
        remote(src, dst, send, recv, to).start()

    def arrived(dst, recv):
        pltpu.make_async_copy(dst, dst, recv).wait()

    def left_here(src, send):
        pltpu.make_async_copy(src, src, send).wait()

    own = z_high == c

    load_patches = pltpu.make_async_copy(patches_in, xp, loc.at[0])
    me = 2 * slot_own + c
    load_patches.start()

    own_rows = pl.ds(pl.multiple_of(16 * c, 16), 16)
    gw[c, mp_at, 0:16, :] = wr_a_in[own_rows, :]
    gw[c, mp_at, 32:48, :] = wr_b_in[own_rows, :]
    gw[c, mp_at, 16:32, :] = we_a_in[own_rows, :]
    gw[c, mp_at, 48:64, :] = we_b_in[own_rows, :]
    unit = lax.broadcasted_iota(jnp.int32, (32, 256), 0)
    lane = lax.broadcasted_iota(jnp.int32, (32, 256), 1)
    place = 16 * mp_at + jnp.where(unit >= 16, unit + 112, unit)
    spread = jnp.where(lane == place, 1.0, 0.0).astype(bf16)
    gws[c, mp_at] = jnp.zeros((16, 256), f32)

    @pl.when(c == 0)
    def _():
        gws[0, mp_at, 0:9, :] = dot(taps_a_in[...], spread, 1, 0)
        gws[0, mp_at, 9:10, 0:128] = gain_a_in[...].astype(f32).reshape(1, 128)

    @pl.when(c == 1)
    def _():
        gws[1, mp_at, 0:9, :] = dot(taps_b_in[...], spread, 1, 0)
        gws[1, mp_at, 9:10, 0:128] = gain_b_in[...].astype(f32).reshape(1, 128)

    barrier = pltpu.get_barrier_semaphore()
    peers = [twin, x_peer, cross, y_peer, corner] + [z_dev(z_at(k)) for k in range(1, zn)]
    for peer in peers:
        pl.semaphore_signal(barrier, inc=1, device_id=peer, device_id_type=MESH)
    pl.semaphore_wait(barrier, len(peers))

    spans = ((0, 16), (16, 16), (32, 32))

    def w_part(b, core, i):
        if b == 3:
            return gws.at[core, i]
        return gw.at[core, i, pl.ds(spans[b][0], spans[b][1])]

    def w_own(b):
        part = w_part(b, c, mp_at)
        for k in range(1, zn):
            start(part, part, w_s.at[b, k - 1], w_rz.at[b, k], z_dev(z_at(k)))
        start(part, part, w_s.at[b, 3], w_rx.at[b, z], x_peer)
        start(part, part, w_s.at[b, 7], w_rc.at[b, mp_at], twin)

    def w_forward(b):
        for k in range(1, zn):
            z_of = z_at(-k)
            i = 2 * z_of + x
            part = w_part(b, c, i)
            arrived(part, w_rz.at[b, k])
            start(part, part, w_s.at[b, 3 + k], w_rx.at[b, z_of], x_peer)
            start(part, part, w_s.at[b, 7 + k], w_rc.at[b, i], twin)

    def w_over(b):
        for k in range(zn):
            z_of = z_at(-k)
            i = 2 * z_of + 1 - x
            part = w_part(b, c, i)
            arrived(part, w_rx.at[b, z_of])
            start(part, part, w_s.at[b, 11 + k], w_rc.at[b, i], twin)

    def w_finish(b):
        for i in range(8):
            arrived(w_part(b, 1 - c, i), w_rc.at[b, i])

    width = cot_in.shape[1] // PIECES

    def cot(slot, c_of, p):
        return cot_all.at[slot, c_of, :, pl.ds(pl.multiple_of(p * width, width), width)]

    def cot_mine(p):
        return cot_in.at[:, pl.ds(pl.multiple_of(p * width, width), width)]

    def cot_twin(slot, p):
        part = cot(slot, c, p)
        start(part, part, dt_cs.at[p, slot], dt_cr.at[p, slot], twin)

    def cot_own_z(p):
        start(cot_mine(p), cot(slot_own, c, p), dt_s.at[p, 1], dt_r.at[p, 1], z_peer)

    def cot_own_x(p):
        start(cot_mine(p), cot(slot_own, c, p), dt_s.at[p, 0], dt_r.at[p, 0], x_peer)

    def cot_own_twin(p):
        start(cot_mine(p), cot(slot_own, c, p), dt_cs.at[p, slot_own], dt_cr.at[p, slot_own], twin)

    def cot_over_z(p):
        part = cot(slot_z, c, p)
        arrived(part, dt_r.at[p, 1])
        start(part, part, dt_s.at[p, 2], dt_r.at[p, 2], x_peer)
        cot_twin(slot_z, p)

    def cot_over_x(p):
        arrived(cot(slot_x, c, p), dt_r.at[p, 0])
        cot_twin(slot_x, p)

    def cot_corner(p):
        arrived(cot(slot_corner, c, p), dt_r.at[p, 2])
        cot_twin(slot_corner, p)

    chunk = w_out_in.shape[1] // CHUNKS

    def w_half(ref, j, half):
        if j == 0:
            return ref.at[pl.ds(pl.multiple_of(512 * half, 512), 512)]
        return ref.at[:, pl.ds(pl.multiple_of((j - 1) * width + half * chunk, chunk), chunk)]

    def swap_refs(j):
        return (w_in_in, wi) if j == 0 else (w_out_in, wo)

    def swap_send(j):
        src, dst = swap_refs(j)

        @pl.when(own)
        def _():
            pltpu.make_async_copy(w_half(src, j, y), w_half(dst, j, y), sw_r.at[j]).start()
            pltpu.make_async_copy(w_half(src, j, 1 - y), w_half(dst, j, 1 - y), sy_r.at[j]).start()

        @pl.when(jnp.logical_not(own))
        def _():
            start(w_half(src, j, y), w_half(dst, j, y), sw_s.at[j], sw_r.at[j], cross)

    def swap_forward(j):
        part = w_half(swap_refs(j)[1], j, y)
        arrived(part, sw_r.at[j])

        @pl.when(jnp.logical_not(own))
        def _():
            start(part, part, sy_s.at[j], sy_r.at[j], y_peer)

    def swap_ready(j):
        arrived(w_half(swap_refs(j)[1], j, 1 - y), sy_r.at[j])

    def reduce_weights(b):
        return gw[:, :, 32 * b : 32 * b + 16, :].reshape(256, 1024)

    def expand_weights(b):
        return gw[:, :, 32 * b + 16 : 32 * b + 32, :].reshape(256, 1024)

    def small_weights(b):
        total = gws[b, 0, 0:9, :]
        for i in range(1, 8):
            total = total + gws[b, i, 0:9, :]
        tw[b, 0:9, 0:256] = total
        for i in range(8):
            tw[b, 9:10, 128 * i : 128 * i + 128] = gws[b, i, 9:10, 0:128]
        return tw[b, 9:10, :]

    def lanes_of(h):
        return pl.ds(pl.multiple_of(h * 128, 128), 128)

    def tap_rows(b, lanes):
        return [tw[b, k : k + 1, lanes] for k in range(9)]

    def normalise(wide_ref, ref, inv_ref, rows):
        widened = wide_ref[rows, :]
        centred = widened - jnp.mean(widened, axis=1, keepdims=True)
        inv = lax.rsqrt(jnp.mean(centred * centred, axis=1, keepdims=True) + epsilon)
        normed = centred * inv
        ref[rows, :] = normed.astype(ref.dtype)
        inv_ref[rows, :] = jnp.broadcast_to(inv, (normed.shape[0], 128))
        return normed

    side = side_in[0].astype(f32)

    def cell_mask():
        index = lax.broadcasted_iota(jnp.int32, (CELLS, 128), 0).astype(f32)
        row = jnp.floor((index + 0.5) * (1.0 / GRID))
        col = index - row * GRID
        return jnp.where((row < side - 0.5) & (col < side - 0.5), 1.0, 0.0).astype(f32)


    def first_conv():
        small_weights(0)
        load_patches.wait()
        red_a[...] = dot(xp[...], reduce_weights(0), 1, 1)

        def conv_half_a(h, carry):
            lanes = lanes_of(h)
            reduced = red_a[:, lanes]
            activated = reduced * jax.nn.sigmoid(reduced) * cell_mask()
            spatial = conv_forward(activated, tap_rows(0, lanes), GRID, edge_masks(GRID, 128))
            spa_a[:, lanes] = spatial
            nar_a[:, lanes] = (spatial * jax.nn.sigmoid(spatial)).astype(bf16)
            return carry

        lax.fori_loop(0, 2, conv_half_a, 0)

    def first_norm():
        dy[...] = dot(nar_a[...], expand_weights(0), 1, 0)
        gain_a = tw[0, 9:10, :]

        def norm_tile(t, carry):
            rows = pl.ds(pl.multiple_of(t * TILE, TILE), TILE)
            normed = normalise(dy, norm_a, inv_a, rows)
            result = xp[rows, :].astype(f32) + normed * gain_a
            high, low = split_low(result)
            yhi[rows, :] = high
            ylo[rows, :] = low
            return carry

        lax.fori_loop(0, CELLS // TILE, norm_tile, 0)

    def first_pool():
        cell = lax.broadcasted_iota(jnp.int32, (POOLED, CELLS), 1).astype(f32)
        bin_of = lax.broadcasted_iota(jnp.int32, (POOLED, CELLS), 0).astype(f32)
        cell_row = jnp.floor((cell + 0.5) * (1.0 / GRID))
        cell_col = cell - cell_row * GRID
        bin_row = jnp.floor((bin_of + 0.5) * (1.0 / POOL))
        bin_col = bin_of - bin_row * POOL

        def table(bins, at):
            lower = jnp.floor((bins * side + 0.5) * (1.0 / POOL))
            upper = jnp.floor(((bins + 1.0) * side + (POOL - 0.5)) * (1.0 / POOL))
            return jnp.where((at > lower - 0.5) & (at < upper - 0.5), 1.0 / (upper - lower), 0.0)

        pp[...] = (table(bin_row, cell_row) * table(bin_col, cell_col)).astype(bf16)
        poolv[...] = dot(pp[...], yhi[...], 1, 0) + dot(pp[...], ylo[...], 1, 0)

    def second_forward():
        gain_b = small_weights(1)
        pooled = poolv[...]
        reduced_b = dot(pooled.astype(bf16), reduce_weights(1), 1, 1)
        red_b[...] = reduced_b
        activated_b = reduced_b * jax.nn.sigmoid(reduced_b)
        spatial_b = conv_forward(activated_b, tap_rows(1, pl.ds(0, 256)), POOL, edge_masks(POOL, 256))
        spa_b[...] = spatial_b
        nar_b[...] = (spatial_b * jax.nn.sigmoid(spatial_b)).astype(bf16)
        norm_b[...] = dot(nar_b[...], expand_weights(1), 1, 0)
        normed_b = normalise(norm_b, norm_b, inv_b, pl.ds(0, POOLED))
        qs[me] = (pooled + normed_b * gain_b).astype(bf16)

    def query_to(k, to):
        start(qs.at[me], qs.at[me], q_s.at[k], q_r.at[k], to)

    def query_twin():
        start(qs.at[me], qs.at[me], q_s.at[3], q_rc.at[slot_own], twin)

    def query_from(k):
        slot = (slot_x, slot_z, slot_corner)[k]
        part = qs.at[2 * slot + c]
        arrived(part, q_r.at[k])
        start(part, part, q_cs.at[k], q_rc.at[slot], twin)

    def query_all():
        for slot in (slot_own, slot_x, slot_z, slot_corner):
            arrived(qs.at[2 * slot + 1 - c], q_rc.at[slot])

    def hidden_units():
        dpre[...] = dot(slot_rows(qs), wi[...], 1, 0)

        def gelu_tile(t, carry):
            rows = pl.ds(pl.multiple_of(t * POOLED, POOLED), POOLED)
            hidden = dpre[rows, :]
            phi = 0.5 * (1.0 + lax.erf(hidden * root_half))
            actv[rows, :] = (hidden * phi).astype(bf16)
            slope[rows, :] = (
                phi + hidden * jnp.exp(-0.5 * hidden * hidden) * inv_root_tau
            ).astype(bf16)
            return carry

        lax.fori_loop(0, 8, gelu_tile, 0)
        dpre[...] = jnp.zeros_like(dpre)

    def item_part(i):
        b = i % 2

        if i >= 2:
            left_here(tp.at[b], t_cs.at[b])
            pl.semaphore_wait(credit, 1)


        weights = wo[:, i * chunk : (i + 1) * chunk]
        partial = dot(actv[...], weights, 1, 0).astype(bf16)
        partial = partial.reshape(4, 2, POOLED, chunk)

        @pl.when(c == 0)
        def _():
            ps[i] = partial[:, 0]
            tp[b] = partial[:, 1]

        @pl.when(c == 1)
        def _():
            ps[i] = partial[:, 1]
            tp[b] = partial[:, 0]

        start(tp.at[b], cr.at[b], t_cs.at[b], t_cr.at[b], twin)

    def item_pair(i):
        b = i % 2
        arrived(cr.at[b], t_cr.at[b])

        def add(d, carry):
            ps[i, d] = (ps[i, d].astype(f32) + cr[b, d].astype(f32)).astype(bf16)
            return carry

        lax.fori_loop(0, 4, add, 0)

        if i < CHUNKS - 2:
            pl.semaphore_signal(credit, inc=1, device_id=twin, device_id_type=MESH)

        start(ps.at[i, slot_corner], rl.at[i, 0], t_s.at[i, 0], t_r.at[i, 0], x_peer)
        start(ps.at[i, slot_x], rl.at[i, 1], t_s.at[i, 1], t_r.at[i, 1], x_peer)

    def item_pass(i):
        arrived(rl.at[i, 0], t_r.at[i, 0])
        ps[i, slot_z] = (ps[i, slot_z].astype(f32) + rl[i, 0].astype(f32)).astype(bf16)
        start(ps.at[i, slot_z], rl.at[i, 2], t_s.at[i, 2], t_r.at[i, 2], z_peer)

    def tok_slice(i):
        return tok_out.at[:, pl.ds(i * chunk, chunk)]

    def item_final(i):
        b = i % 2

        if i >= 2:
            left_here(tstage.at[b], gl.at[8 + b])

        arrived(rl.at[i, 1], t_r.at[i, 1])
        arrived(rl.at[i, 2], t_r.at[i, 2])
        tstage[b] = (
            ps[i, slot_own].astype(f32) + rl[i, 1].astype(f32) + rl[i, 2].astype(f32)
        ).astype(bf16)
        pltpu.make_async_copy(tstage.at[b], tok_slice(i), gl.at[8 + b]).start()

    def piece_rows(p):
        for slot in range(4):
            arrived(cot(slot, 1 - c, p), dt_cr.at[p, slot])

            @pl.when(slot_own != slot)
            def _():
                part = cot_all.at[slot, :, :, pl.ds(p * width, width)]
                pltpu.make_async_copy(part, dtv.at[pl.ds(2 * slot, 2)], loc.at[3]).start()

        pltpu.make_async_copy(cot(slot_own, 1 - c, p), dtv.at[2 * slot_own + 1 - c], loc.at[3]).start()
        pltpu.make_async_copy(cot_mine(p), dtv.at[2 * slot_own + c], loc.at[3]).start()
        pltpu.make_async_copy(dtv, dtv, loc.at[3]).wait()

    def half_lanes(half):
        return pl.ds(pl.multiple_of(half * chunk, chunk), chunk)

    def piece_lanes(h):
        return dtv[:, :, half_lanes(h)].reshape(8 * POOLED, chunk)

    def hidden_part(p):
        def hidden_half(h, carry):
            weights = wo[:, pl.ds(pl.multiple_of(p * width + h * chunk, chunk), chunk)]
            dpre[...] += dot(piece_lanes(h), weights, 1, 1)
            return carry

        lax.fori_loop(0, 2, hidden_half, 0)

    def row_part(slot):
        rows = pl.ds(pl.multiple_of(slot * (2 * POOLED), 2 * POOLED), 2 * POOLED)
        d_hidden = (dpre[rows, :] * slope[rows, :].astype(f32)).astype(bf16)
        half = lax.div(slot, 2)
        place = pl.ds(pl.multiple_of((slot - 2 * half) * (2 * POOLED), 2 * POOLED), 2 * POOLED)
        ylo[place, pl.ds(pl.multiple_of(half * 512, 512), 512)] = d_hidden
        dps[slot] = dot(d_hidden, wi[...], 1, 1).astype(bf16).reshape(2, POOLED, 1024)
        start(dps.at[slot, 1 - c], dr.at[slot], d_cs.at[slot], d_cr.at[slot], twin)

    def in_turn(k):
        return jnp.where(k == 0, slot_corner, jnp.where(k == 1, slot_x, jnp.where(k == 2, slot_z, slot_own)))

    def row_gradients():
        def one(k, carry):
            @pl.when(k < 4)
            def _():
                row_part(in_turn(k))

            slot = in_turn(k - 1)

            @pl.when(k >= 1)
            def _():
                arrived(dr.at[slot], d_cr.at[slot])
                dps[slot, c] = (dps[slot, c].astype(f32) + dr[slot].astype(f32)).astype(bf16)

            @pl.when(k == 1)
            def _():
                start(dps.at[slot, c], dz.at[2], d_zs.at[2], d_zr.at[2], corner)

            @pl.when(k == 2)
            def _():
                start(dps.at[slot, c], dz.at[0], d_zs.at[0], d_zr.at[0], x_peer)

            @pl.when(k == 3)
            def _():
                start(dps.at[slot, c], dz.at[1], d_zs.at[1], d_zr.at[1], z_peer)

            return carry

        lax.fori_loop(0, 5, one, 0)

    def grad_half(j, half):
        if j == PIECES:
            return gis.at[pl.ds(pl.multiple_of(512 * half, 512), 512)]
        return gos.at[j, :, half_lanes(half)]

    def out_half(j, half):
        if j == PIECES:
            return gin_out.at[pl.ds(pl.multiple_of(512 * half, 512), 512)]
        return gout_out.at[:, pl.ds(pl.multiple_of(j * width + half * chunk, chunk), chunk)]

    def grad_send(j, h):
        rows = pl.ds(256 * h, 256)
        if j == PIECES:
            part = gis.at[pl.ds(pl.multiple_of(512 * (1 - y) + 256 * h, 256), 256)]
        else:
            part = gos.at[j, rows, half_lanes(1 - y)]
        start(part, gyl.at[j, rows], gy_s.at[j, h], gy_r.at[j, h], y_peer)

    def grad_part(p):
        def one_half(h, carry):
            gos[p, :, half_lanes(h)] = dot(actv[...], piece_lanes(h), 0, 0).astype(bf16)
            return carry

        lax.fori_loop(0, 2, one_half, 0)

    def gin_part():
        gis[...] = (
            dot(qs[0:4].reshape(4 * POOLED, 1024), ylo[:, 0:512], 0, 0)
            + dot(qs[4:8].reshape(4 * POOLED, 1024), ylo[:, 512:1024], 0, 0)
        ).astype(bf16)

    def grad_pair(j):
        mine = grad_half(j, y)
        for h in range(2):
            arrived(gyl.at[j, pl.ds(256 * h, 256)], gy_r.at[j, h])
        mine[...] = (mine[...].astype(f32) + gyl[j].astype(f32)).astype(bf16)

        @pl.when(jnp.logical_not(own))
        def _():
            start(mine, gfl.at[j], gx_s.at[j], gx_r.at[j], far_peer)

    def grad_sum(j):
        @pl.when(own)
        def _():
            mine = grad_half(j, y)
            arrived(gfl.at[j], gx_r.at[j])
            load = pltpu.make_async_copy(gfl.at[j], land, loc.at[4])
            load.start()
            load.wait()
            mine[...] = (mine[...].astype(f32) + land[...].astype(f32)).astype(bf16)
            start(mine, out_half(j, y), ga_s.at[j], ga_r.at[j], y_peer)
            start(mine, out_half(j, y), gc_s.at[j, 0], gc_r.at[j, 0], twin)
            pltpu.make_async_copy(mine, out_half(j, y), gl.at[j]).start()

    def grad_last(j):
        @pl.when(own)
        def _():
            other = out_half(j, 1 - y)
            arrived(other, ga_r.at[j])
            start(other, other, gc_s.at[j, 1], gc_r.at[j, 1], twin)

    def grad_done(j):
        for h in range(2):
            left_here(gyl.at[j, pl.ds(256 * h, 256)], gy_s.at[j, h])

        @pl.when(own)
        def _():
            left_here(grad_half(j, y), ga_s.at[j])
            left_here(grad_half(j, y), gc_s.at[j, 0])
            left_here(grad_half(j, y), gc_s.at[j, 1])
            pltpu.make_async_copy(grad_half(j, y), out_half(j, y), gl.at[j]).wait()

        @pl.when(jnp.logical_not(own))
        def _():
            left_here(grad_half(j, y), gx_s.at[j])
            arrived(out_half(j, y), gc_r.at[j, 0])
            arrived(out_half(j, 1 - y), gc_r.at[j, 1])

    def widened_back(d_rows, normed, gain, inv):
        dn = d_rows * gain
        return (
            inv
            * (
                dn
                - jnp.mean(dn, axis=1, keepdims=True)
                - normed * jnp.mean(dn * normed, axis=1, keepdims=True)
            )
        ).astype(bf16)

    def pack_small(t, d_gain):
        for k in range(4):
            sm[t, 9 + k : 10 + k, :] = d_gain[:, 256 * k : 256 * k + 256]
        sm[t, 13:16, :] = jnp.zeros((3, 256), f32)

    passes = ((1, 0, 2, 1), (0, 1, 1, None), (0, 0, 1, 0))

    def share_core(p):
        t, k0, n, small = passes[p]
        kinds = pl.ds(k0, n)
        start(
            wgs.at[t, kinds, pl.ds(pl.multiple_of(128 * (1 - c), 128), 128)], wgc.at[t, kinds],
            gr_s.at[p, 0], gr_r.at[p, 0], twin,
        )
        if small is not None:
            start(sm.at[t], smc.at[t], gr_s.at[p, 1], gr_r.at[p, 1], twin)

    def share_x(p):
        t, k0, n, small = passes[p]
        kinds = pl.ds(k0, n)
        arrived(wgc.at[t, kinds], gr_r.at[p, 0])
        for kind in range(k0, k0 + n):
            for i in range(8):
                rows = pl.ds(pl.multiple_of(128 * c + 16 * i, 16), 16)
                xs[t, kind, i % 2, i // 2] = (
                    wgs[t, kind, rows, :].astype(f32) + wgc[t, kind, 16 * i : 16 * i + 16, :].astype(f32)
                ).astype(bf16)
        start(xs.at[t, kinds, 1 - x], xr.at[t, kinds], gr_s.at[p, 2], gr_r.at[p, 2], x_peer)
        if small is not None:
            arrived(smc.at[t], gr_r.at[p, 1])
            left_here(sm.at[t], gr_s.at[p, 1])
            sm[t] = sm[t] + smc[t]
            start(sm.at[t], smx.at[t], gr_s.at[p, 3], gr_r.at[p, 3], x_peer)

    def share_z(p):
        t, k0, n, small = passes[p]
        kinds = pl.ds(k0, n)
        arrived(xr.at[t, kinds], gr_r.at[p, 2])
        for kind in range(k0, k0 + n):
            zs[t, kind] = (xs[t, kind, x].astype(f32) + xr[t, kind].astype(f32)).astype(bf16)
        for k in range(1, zn):
            d = z_at(k)
            start(
                zs.at[t, kinds, d], zr.at[t, kinds, k - 1], gr_s.at[p, 3 + k], gr_r.at[p, 3 + k], z_dev(d)
            )
        if small is not None:
            arrived(smx.at[t], gr_r.at[p, 3])
            left_here(sm.at[t], gr_s.at[p, 3])
            smz[t, z] = sm[t] + smx[t]
            for k in range(1, zn):
                start(
                    smz.at[t, z], smz.at[t, z], gr_s.at[p, 6 + k], gr_r.at[p, 6 + k], z_dev(z_at(k))
                )

    def share_y(p):
        t, k0, n, small = passes[p]
        kinds = pl.ds(k0, n)
        for k in range(1, zn):
            arrived(zr.at[t, kinds, k - 1], gr_r.at[p, 3 + k])
        for kind in range(k0, k0 + n):
            total_rows = zs[t, kind, z].astype(f32)
            for k in range(1, zn):
                total_rows = total_rows + zr[t, kind, k - 1].astype(f32)
            ys[t, kind] = total_rows.astype(bf16)
        start(ys.at[t, kinds], yr.at[t, kinds], gr_s.at[p, 10], gr_r.at[p, 10], y_peer)
        if small is not None:
            for k in range(1, zn):
                arrived(smz.at[t, z_at(-k)], gr_r.at[p, 6 + k])
            sm[t] = (smz[t, 0] + smz[t, 1]) + (smz[t, 2] + smz[t, 3])
            start(sm.at[t], smy.at[t], gr_s.at[p, 11], gr_r.at[p, 11], y_peer)

    def share_twin(p):
        t, k0, n, small = passes[p]
        kinds = pl.ds(k0, n)
        arrived(yr.at[t, kinds], gr_r.at[p, 10])
        for kind in range(k0, k0 + n):
            gfin[c, t, kind] = ys[t, kind].astype(f32) + yr[t, kind].astype(f32)
        part = gfin.at[c, t, kinds]
        start(part, part, gr_s.at[p, 12], gr_r.at[p, 12], twin)
        if small is not None:
            arrived(smy.at[t], gr_r.at[p, 11])
            gsml_out[t] = sm[t] + smy[t]

    def share_done(p):
        t, k0, n, small = passes[p]
        kinds = pl.ds(k0, n)
        arrived(gfin.at[1 - c, t, kinds], gr_r.at[p, 12])
        for kind in range(k0, k0 + n):
            for h in range(2):
                gblk_out[t, kind, 16 * h : 16 * h + 16, :] = gfin[h, t, kind]
        left_here(wgc.at[t, kinds], gr_s.at[p, 0])
        left_here(xr.at[t, kinds], gr_s.at[p, 2])
        for k in range(1, zn):
            left_here(ys.at[t, kinds], gr_s.at[p, 3 + k])
        left_here(ys.at[t, kinds], gr_s.at[p, 10])
        left_here(gfin.at[c, t, kinds], gr_s.at[p, 12])
        if small is not None:
            for k in range(1, zn):
                left_here(sm.at[t], gr_s.at[p, 6 + k])
            left_here(sm.at[t], gr_s.at[p, 11])

    def back_second():
        total = dps[slot_own, c].astype(f32)
        for k in range(3):
            arrived(dz.at[k], d_zr.at[k])
            total = total + dz[k].astype(f32)
        normed_b = norm_b[...]
        d_gain_b = jnp.sum(total * normed_b, axis=0, keepdims=True)
        gain_b = tw[1, 9:10, :]
        dw_b = widened_back(total, normed_b, gain_b, inv_b[:, 0:1])
        wgs[1, 1] = dot(nar_b[...], dw_b, 0, 0).astype(bf16)
        spatial_b = spa_b[...]
        d_spatial_b = dot(dw_b, expand_weights(1), 1, 1) * silu_slope(spatial_b)
        reduced_b = red_b[...]
        sig_b = jax.nn.sigmoid(reduced_b)
        d_act_b, d_taps_b = conv_backward(
            d_spatial_b, reduced_b * sig_b, tap_rows(1, pl.ds(0, 256)), POOL, edge_masks(POOL, 256)
        )
        d_red_b = (d_act_b * (sig_b * (1.0 + reduced_b * (1.0 - sig_b)))).astype(bf16)
        wgs[1, 0] = dot(d_red_b, poolv[...].astype(bf16), 0, 0).astype(bf16)
        for k in range(9):
            sm[1, k : k + 1, :] = d_taps_b[k]
        pack_small(1, d_gain_b)
        d_pool = total + dot(d_red_b, reduce_weights(1), 1, 0)
        high, low = split_low(d_pool)
        dy[...] = dot(pp[...], high, 0, 0) + dot(pp[...], low, 0, 0)

    def back_first_norm():
        gain_a = tw[0, 9:10, :]

        def back_tile(t, d_gain):
            rows = pl.ds(pl.multiple_of(t * TILE, TILE), TILE)
            d_rows = dy[rows, :]
            normed = norm_a[rows, :].astype(f32)
            yhi[rows, :] = widened_back(d_rows, normed, gain_a, inv_a[rows, 0:1])
            return d_gain + jnp.sum(d_rows * normed, axis=0, keepdims=True)

        d_gain_a = lax.fori_loop(0, CELLS // TILE, back_tile, jnp.zeros((1, 1024), f32))
        pack_small(0, d_gain_a)
        wgs[0, 1] = dot(nar_a[...], yhi[...], 0, 0).astype(bf16)

    def back_first_conv():
        spa_a[...] = dot(yhi[...], expand_weights(0), 1, 1) * silu_slope(spa_a[...])

        def conv_back_half_a(h, carry):
            lanes = lanes_of(h)
            reduced = red_a[:, lanes]
            sig = jax.nn.sigmoid(reduced)
            mask = cell_mask()
            d_act, d_taps = conv_backward(
                spa_a[:, lanes], reduced * sig * mask, tap_rows(0, lanes), GRID, edge_masks(GRID, 128)
            )
            dlow[:, lanes] = (d_act * mask * (sig * (1.0 + reduced * (1.0 - sig)))).astype(bf16)
            for k in range(9):
                sm[0, k : k + 1, lanes] = d_taps[k]
            return carry

        lax.fori_loop(0, 2, conv_back_half_a, 0)
        wgs[0, 0] = dot(dlow[...], xp[...], 0, 0).astype(bf16)

    store_dpat = pltpu.make_async_copy(dy, dpat_out, loc.at[5])

    def back_first_rows():
        dy[...] += dot(dlow[...], reduce_weights(0), 1, 0)
        store_dpat.start()

    w_own(3)
    cot_own_x(0)
    w_own(0)
    w_own(2)
    cot_own_z(0)
    w_own(1)
    w_forward(3)
    cot_own_x(2)
    cot_own_z(1)
    w_over(3)
    w_forward(2)
    cot_own_twin(1)
    swap_send(0)
    swap_send(1)
    w_forward(0)
    swap_send(2)
    w_forward(1)
    w_over(2)
    w_finish(3)
    cot_over_z(0)
    cot_own_x(3)
    w_over(1)
    w_finish(1)
    w_over(0)
    w_finish(0)
    cot_over_x(2)
    w_finish(2)
    first_conv()
    first_norm()
    first_pool()
    cot_own_twin(2)
    second_forward()
    cot_corner(0)
    swap_forward(0)
    query_to(0, x_peer)
    query_twin()
    query_to(2, corner)
    swap_ready(0)
    query_to(1, z_peer)
    cot_over_x(0)
    swap_forward(1)
    cot_own_twin(0)
    piece_rows(0)
    swap_ready(1)
    cot_own_z(2)
    swap_send(3)
    swap_forward(2)
    query_from(1)
    query_from(2)
    query_from(0)
    cot_over_z(1)
    query_all()
    hidden_units()

    cot_own_x(1)
    grad_part(0)
    grad_send(0, 0)
    item_part(0)
    hidden_part(0)
    grad_send(0, 1)
    cot_corner(1)
    cot_over_x(3)
    cot_own_z(3)
    cot_over_z(2)
    swap_send(4)
    item_pair(0)
    cot_over_x(1)
    cot_own_twin(3)
    piece_rows(1)
    item_part(1)
    swap_forward(3)
    swap_ready(2)
    item_part(2)
    cot_over_z(3)
    grad_part(1)
    swap_forward(4)
    grad_send(1, 0)
    item_pass(0)
    hidden_part(1)
    cot_corner(2)
    item_pair(1)
    grad_send(1, 1)
    grad_pair(0)
    item_part(3)
    piece_rows(2)
    item_pair(2)
    grad_part(2)
    swap_ready(3)
    hidden_part(2)
    cot_corner(3)
    piece_rows(3)
    item_pass(1)
    grad_send(2, 1)
    swap_ready(4)
    grad_send(2, 0)
    hidden_part(3)
    row_gradients()
    grad_pair(1)
    item_pair(3)
    grad_part(3)
    grad_send(3, 1)
    grad_pair(2)
    item_pass(2)
    grad_send(3, 0)
    item_part(4)
    item_pair(4)
    grad_sum(1)
    gin_part()
    item_part(5)
    grad_send(PIECES, 0)
    item_part(6)
    grad_send(PIECES, 1)
    grad_pair(3)
    back_second()
    share_core(0)
    item_pair(5)
    item_part(7)
    back_first_norm()
    item_final(0)
    item_pass(3)
    share_x(0)
    back_first_conv()
    item_pass(4)
    share_core(1)
    grad_sum(0)
    item_final(1)
    grad_pair(PIECES)
    item_pass(5)
    share_core(2)
    grad_sum(3)
    item_final(2)
    item_final(3)
    grad_last(1)
    share_x(1)
    back_first_rows()
    grad_last(0)
    grad_sum(2)
    share_z(0)
    item_final(4)
    item_pair(6)
    grad_last(3)
    share_x(2)
    grad_sum(PIECES)
    item_pass(6)
    share_z(2)
    item_final(5)
    item_pair(7)
    share_z(1)
    grad_last(2)
    share_y(0)
    item_pass(7)
    share_y(2)
    share_y(1)
    share_twin(0)
    item_final(6)
    grad_last(PIECES)
    share_twin(2)
    item_final(7)
    share_twin(1)

    for p in range(3):
        share_done(p)
    for j in range(1 + PIECES):
        grad_done(j)

        @pl.when(jnp.logical_not(own))
        def _():
            part = w_half(swap_refs(j)[1], j, y)
            left_here(part, sw_s.at[j])
            left_here(part, sy_s.at[j])

    store_dpat.wait()
    for b in range(2):
        pltpu.make_async_copy(tstage.at[b], tok_slice(b), gl.at[8 + b]).wait()
        left_here(tp.at[b], t_cs.at[b])
    for b in range(4):
        for k in range(15):
            left_here(w_part(b, c, 0), w_s.at[b, k])
    for k in range(4):
        left_here(qs.at[0], q_s.at[k])
    for k in range(3):
        left_here(qs.at[0], q_cs.at[k])
    for k in range(4):
        left_here(dps.at[0, 0], d_cs.at[k])
    for k in range(3):
        left_here(dps.at[0, 0], d_zs.at[k])
    for p in range(PIECES):
        for slot in range(4):
            left_here(cot(0, 0, p), dt_cs.at[p, slot])
        for k in range(3):
            left_here(cot(0, 0, p), dt_s.at[p, k])

    def drain_items(i, carry):
        for k in range(3):
            left_here(ps.at[0, 0], t_s.at[i, k])
        return carry

    lax.fori_loop(0, CHUNKS, drain_items, 0)


def layer_call(
    patches, grid_sizes, wr_a, taps_a, we_a, gain_a, wr_b, taps_b, we_b, gain_b, w_in, w_out, d_tokens
):
    any_space = pl.BlockSpec(memory_space=pl.ANY)
    vmem = pl.BlockSpec(memory_space=pltpu.VMEM)
    smem = pl.BlockSpec(memory_space=pltpu.SMEM)
    shape = jax.ShapeDtypeStruct
    width = w_out.shape[1] // PIECES
    chunk = w_out.shape[1] // CHUNKS
    out_shape = (
        shape((POOLED, 4096), bf16),
        shape((CELLS, 1024), f32),
        shape((512, 4096), bf16),
        shape((1024, 512), bf16),
        shape((2, 2, 32, 1024), f32),
        shape((2, 16, 256), f32),
        shape((4, 2, POOLED, 4096), bf16),
        shape((1 + PIECES, 512, width // 2), bf16),
    )
    dma = pltpu.SemaphoreType.DMA
    scratch = [
        pltpu.VMEM((CELLS, 1024), bf16),
        pltpu.VMEM((2, 8, 64, 1024), bf16),
        pltpu.VMEM((2, 8, 16, 256), f32),
        pltpu.VMEM((CELLS, 256), f32),
        pltpu.VMEM((CELLS, 256), f32),
        pltpu.VMEM((CELLS, 256), bf16),
        pltpu.VMEM((CELLS, 1024), bf16),
        pltpu.VMEM((CELLS, 128), f32),
        pltpu.VMEM((CELLS, 1024), bf16),
        pltpu.VMEM((CELLS, 1024), bf16),
        pltpu.VMEM((CELLS, 1024), f32),
        pltpu.VMEM((CELLS, 256), bf16),
        pltpu.VMEM((POOLED, CELLS), bf16),
        pltpu.VMEM((2, 16, 1024), f32),
        pltpu.VMEM((POOLED, 1024), f32),
        pltpu.VMEM((POOLED, 256), f32),
        pltpu.VMEM((POOLED, 256), f32),
        pltpu.VMEM((POOLED, 256), bf16),
        pltpu.VMEM((POOLED, 1024), f32),
        pltpu.VMEM((POOLED, 128), f32),
        pltpu.VMEM((1024, 512), bf16),
        pltpu.VMEM((512, 4096), bf16),
        pltpu.VMEM((8, POOLED, 1024), bf16),
        pltpu.VMEM((8 * POOLED, 512), bf16),
        pltpu.VMEM((8 * POOLED, 512), bf16),
        pltpu.VMEM((8 * POOLED, 512), f32),
        pltpu.VMEM((8, POOLED, width), bf16),
        pltpu.VMEM((2, 4, POOLED, chunk), bf16),
        pltpu.VMEM((2, 4, POOLED, chunk), bf16),
        pltpu.VMEM((CHUNKS, 4, POOLED, chunk), bf16),
        pltpu.VMEM((CHUNKS, 3, POOLED, chunk), bf16),
        pltpu.VMEM((2, POOLED, chunk), bf16),
        pltpu.VMEM((4, 2, POOLED, 1024), bf16),
        pltpu.VMEM((4, POOLED, 1024), bf16),
        pltpu.VMEM((3, POOLED, 1024), bf16),
        pltpu.VMEM((PIECES, 512, width), bf16),
        pltpu.VMEM((1024, 512), bf16),
        pltpu.VMEM((1 + PIECES, 512, width // 2), bf16),
        pltpu.VMEM((512, width // 2), bf16),
        pltpu.VMEM((2, 2, 256, 1024), bf16),
        pltpu.VMEM((2, 2, 128, 1024), bf16),
        pltpu.VMEM((2, 2, 2, 4, 16, 1024), bf16),
        pltpu.VMEM((2, 2, 4, 16, 1024), bf16),
        pltpu.VMEM((2, 2, 4, 16, 1024), bf16),
        pltpu.VMEM((2, 2, 3, 16, 1024), bf16),
        pltpu.VMEM((2, 2, 16, 1024), bf16),
        pltpu.VMEM((2, 2, 16, 1024), bf16),
        pltpu.VMEM((2, 16, 256), f32),
        pltpu.VMEM((2, 16, 256), f32),
        pltpu.VMEM((2, 16, 256), f32),
        pltpu.VMEM((2, 4, 16, 256), f32),
        pltpu.VMEM((2, 16, 256), f32),
        pltpu.VMEM((2, 2, 2, 16, 1024), f32),
        dma((6,)),
        dma((4, 15)),
        dma((4, 4)),
        dma((4, 4)),
        dma((4, 8)),
        dma((1 + PIECES,)),
        dma((1 + PIECES,)),
        dma((1 + PIECES,)),
        dma((1 + PIECES,)),
        dma((4,)),
        dma((3,)),
        dma((3,)),
        dma((4,)),
        dma((PIECES, 3)),
        dma((PIECES, 3)),
        dma((PIECES, 4)),
        dma((PIECES, 4)),
        dma((2,)),
        dma((2,)),
        dma((CHUNKS, 3)),
        dma((CHUNKS, 3)),
        pltpu.SemaphoreType.REGULAR,
        dma((4,)),
        dma((4,)),
        dma((3,)),
        dma((3,)),
        dma((1 + PIECES, 2)),
        dma((1 + PIECES, 2)),
        dma((1 + PIECES,)),
        dma((1 + PIECES,)),
        dma((1 + PIECES,)),
        dma((1 + PIECES,)),
        dma((1 + PIECES, 2)),
        dma((1 + PIECES, 2)),
        dma((10,)),
        dma((3, 13)),
        dma((3, 13)),
    ]
    return pl.pallas_call(
        layer_kernel,
        out_shape=out_shape,
        in_specs=[any_space, smem] + [vmem] * 8 + [any_space] * 3,
        out_specs=(any_space, any_space, any_space, any_space, vmem, vmem, any_space, any_space),
        scratch_shapes=scratch,
        compiler_params=pltpu.CompilerParams(
            collective_id=0, has_side_effects=True, vmem_limit_bytes=VMEM_BYTES
        ),
    )(
        patches, grid_sizes, wr_a, taps_a, we_a, gain_a, wr_b, taps_b, we_b, gain_b, w_in, w_out, d_tokens
    )


VMEM_BYTES = 64 * 1024 * 1024


FINISH = 2


def finish_kernel(
    tok_in, dpat_in, gout_in, gin_in, gblk_in, gsml_in,
    tok, dpat, gout, gin, gra, gta, gea, gga, grb, gtb, geb, ggb,
):
    tok[...] = tok_in[...]
    dpat[...] = dpat_in[...]
    gout[...] = gout_in[...].astype(f32)
    gin[...] = gin_in[...].astype(f32)

    @pl.when(pl.program_id(0) == 0)
    def _():
        mp_at = lax.axis_index("mp")
        for t, outs in enumerate(((gra, gta, gea, gga), (grb, gtb, geb, ggb))):
            reduce, taps, expand, gain = outs
            reduce[...] = gblk_in[t, 0]
            expand[...] = gblk_in[t, 1]
            turned = pltpu.roll(gsml_in[t], lax.rem(256 - 16 * mp_at, 256), 1)
            taps[:, 0:16] = turned[0:9, 0:16]
            taps[:, 16:32] = turned[0:9, 128:144]
            for i in range(8):
                @pl.when(mp_at == i)
                def _(t=t, i=i, gain=gain):
                    lanes = 128 * (i % 2)
                    gain[...] = gsml_in[t, 9 + i // 2 : 10 + i // 2, lanes : lanes + 128]


def finish_call(tokens, d_patches, gout, gin, gblk, gsml):
    shape = jax.ShapeDtypeStruct
    columns = tokens.shape[1] // FINISH

    def whole(*dims):
        return pl.BlockSpec(dims, lambda i: (0,) * len(dims))

    one = [whole(32, 1024), whole(9, 32), whole(32, 1024), whole(1, 128)]
    one_shape = [shape((32, 1024), f32), shape((9, 32), f32), shape((32, 1024), f32), shape((1, 128), f32)]
    return pl.pallas_call(
        finish_kernel,
        grid=(FINISH,),
        out_shape=[
            shape(tokens.shape, bf16),
            shape(d_patches.shape, f32),
            shape(gout.shape, f32),
            shape(gin.shape, f32),
        ]
        + one_shape * 2,
        in_specs=[
            pl.BlockSpec((POOLED, columns), lambda i: (0, i)),
            pl.BlockSpec((CELLS // FINISH, 1024), lambda i: (i, 0)),
            pl.BlockSpec((512 // FINISH, 4096), lambda i: (i, 0)),
            pl.BlockSpec((1024 // FINISH, 512), lambda i: (i, 0)),
            whole(2, 2, 32, 1024),
            whole(2, 16, 256),
        ],
        out_specs=[
            pl.BlockSpec((POOLED, columns), lambda i: (0, i)),
            pl.BlockSpec((CELLS // FINISH, 1024), lambda i: (i, 0)),
            pl.BlockSpec((512 // FINISH, 4096), lambda i: (i, 0)),
            pl.BlockSpec((1024 // FINISH, 512), lambda i: (i, 0)),
        ]
        + one * 2,
        compiler_params=pltpu.CompilerParams(vmem_limit_bytes=VMEM_BYTES),
    )(tokens, d_patches, gout, gin, gblk, gsml)


def fast_body(
    patches, grid_sizes, w_reduce_a, taps_a, w_expand_a, gain_a,
    w_reduce_b, taps_b, w_expand_b, gain_b, w_in, w_out, d_tokens,
):
    results = layer_call(
        patches, grid_sizes, w_reduce_a.T, taps_a, w_expand_a, gain_a,
        w_reduce_b.T, taps_b, w_expand_b, gain_b, w_in, w_out, d_tokens,
    )
    (
        tokens, d_patches, gout, gin, reduce_a, tap_a, expand_a, scale_a, reduce_b, tap_b, expand_b, scale_b
    ) = finish_call(*results[:6])
    return (
        tokens, d_patches,
        reduce_a.T, tap_a, expand_a, scale_a.reshape(-1),
        reduce_b.T, tap_b, expand_b, scale_b.reshape(-1),
        gin, gout,
    )


def solution(mesh):
    in_specs = (
        P(("dp", "mp"), None),
        P(("dp", "mp")),
        P(None, "mp"),
        P(None, "mp"),
        P("mp", None),
        P("mp"),
        P(None, "mp"),
        P(None, "mp"),
        P("mp", None),
        P("mp"),
        P(None, "mp"),
        P("mp", None),
        P(("dp", "mp"), None),
    )
    out_specs = (
        P(("dp", "mp"), None),
        P(("dp", "mp"), None),
        P(None, "mp"),
        P(None, "mp"),
        P("mp", None),
        P("mp"),
        P(None, "mp"),
        P(None, "mp"),
        P("mp", None),
        P("mp"),
        P(None, "mp"),
        P("mp", None),
    )
    fits = mesh.shape["dp"] == 4 and mesh.shape["mp"] == 8
    return jax.shard_map(fast_body if fits else body, mesh=mesh, in_specs=in_specs, out_specs=out_specs, check_vma=False)
```

```python
import jax
import jax.numpy as jnp
from jax import lax
from jax.experimental import pallas as pl
from jax.experimental.pallas import tpu as pltpu
from jax.sharding import PartitionSpec as P

GRID = 24
SMALL_GRID = 16
POOL = 12


epsilon = 1e-05
highest = lax.Precision.HIGHEST
root_half = 0.7071067811865476
inv_root_tau = 0.3989422804014327


def silu_slope(values):
    sigmoid = jax.nn.sigmoid(values)
    return sigmoid * (1.0 + values * (1.0 - sigmoid))


def gelu_exact(values):
    return 0.5 * values * (1.0 + lax.erf(values * root_half))


def gelu_slope(values):
    return (
        0.5 * (1.0 + lax.erf(values * root_half))
        + values * jnp.exp(-0.5 * values * values) * inv_root_tau
    )


def outer_rows(left, right):
    return lax.dot_general(
        left, right, (((0,), (0,)), ((), ())), preferred_element_type=jnp.float32
    )


def times_trans(left, right):
    return lax.dot_general(
        left, right, (((1,), (1,)), ((), ())), preferred_element_type=jnp.float32
    )


def map_padding(ndims):
    return [(0, 0)] * (ndims - 3) + [(1, 1), (1, 1), (0, 0)]


def depthwise(feature_map, tap_weights):
    extent = feature_map.shape[-2]
    padded = jnp.pad(feature_map, map_padding(feature_map.ndim))
    result = jnp.zeros_like(feature_map)
    for tap_row in range(3):
        for tap_col in range(3):
            result = (
                result
                + padded[..., tap_row : tap_row + extent, tap_col : tap_col + extent, :]
                * tap_weights[3 * tap_row + tap_col]
            )
    return result


def depthwise_back(upstream, feature_map, tap_weights):
    extent = upstream.shape[-2]
    upstream_pad = jnp.pad(upstream, map_padding(upstream.ndim))
    feature_pad = jnp.pad(feature_map, map_padding(feature_map.ndim))
    d_feature = jnp.zeros_like(upstream)
    tap_grads = []
    leading = tuple(range(upstream.ndim - 1))
    for tap_row in range(3):
        for tap_col in range(3):
            d_feature = (
                d_feature
                + upstream_pad[
                    ..., 2 - tap_row : 2 - tap_row + extent, 2 - tap_col : 2 - tap_col + extent, :
                ]
                * tap_weights[3 * tap_row + tap_col]
            )
            shifted = feature_pad[..., tap_row : tap_row + extent, tap_col : tap_col + extent, :]
            tap_grads.append(jnp.sum(shifted * upstream, axis=leading))
    return (d_feature, jnp.stack(tap_grads))


def block_forward(feature_rows, low_rows, weights_set, extent):
    w_reduce, tap_weights, w_expand, norm_gain = weights_set
    channels = w_reduce.shape[1]
    row_count = feature_rows.shape[0]
    reduced = jnp.dot(low_rows, w_reduce, preferred_element_type=jnp.float32)
    activated = jax.nn.silu(reduced).reshape(-1, extent, extent, channels)
    spatial = depthwise(activated, tap_weights.astype(jnp.float32)).reshape(row_count, channels)
    narrow = jax.nn.silu(spatial).astype(jnp.bfloat16)
    widened = jnp.dot(narrow, w_expand, preferred_element_type=jnp.float32)
    centred = widened - jnp.mean(widened, axis=1, keepdims=True)
    inv_scale = lax.rsqrt(jnp.mean(centred * centred, axis=1, keepdims=True) + epsilon)
    normed = centred * inv_scale
    result = feature_rows + normed * norm_gain.astype(jnp.float32)
    return (result, (reduced, activated, spatial, narrow, normed, inv_scale))


def block_backward(d_result, low_rows, weights_set, saved):
    w_reduce, tap_weights, w_expand, norm_gain = weights_set
    reduced, activated, spatial, narrow, normed, inv_scale = saved
    d_gain = jnp.sum(d_result * normed, axis=0)
    d_normed = d_result * norm_gain.astype(jnp.float32)
    d_widened = inv_scale * (
        d_normed
        - jnp.mean(d_normed, axis=1, keepdims=True)
        - normed * jnp.mean(d_normed * normed, axis=1, keepdims=True)
    )
    d_widened = d_widened.astype(jnp.bfloat16)
    grad_expand = outer_rows(narrow, d_widened)
    d_spatial = times_trans(d_widened, w_expand) * silu_slope(spatial)
    d_activated, grad_taps = depthwise_back(
        d_spatial.reshape(activated.shape), activated, tap_weights.astype(jnp.float32)
    )
    d_reduced = (d_activated.reshape(reduced.shape) * silu_slope(reduced)).astype(jnp.bfloat16)
    grad_reduce = outer_rows(low_rows, d_reduced)
    d_rows = d_result + times_trans(d_reduced, w_reduce)
    return (d_rows, (grad_reduce, grad_taps, grad_expand, d_gain))


def crop_rows(pixels, extent):
    features = pixels.shape[-1]
    return pixels.reshape(GRID, GRID, features)[:extent, :extent].reshape(extent * extent, features)


def widen_grid(values, extent):
    features = values.shape[-1]
    return jnp.pad(
        values.reshape(extent, extent, features), ((0, GRID - extent), (0, GRID - extent), (0, 0))
    )


def first_forward(weights_set, extent):

    def compute(pixels):
        cropped = crop_rows(pixels, extent)
        result, unused = block_forward(cropped.astype(jnp.float32), cropped, weights_set, extent)
        return widen_grid(result, extent)

    return compute


def first_backward(weights_set, extent):

    def compute(pixels, upstream):
        cropped = crop_rows(pixels, extent)
        sliced = crop_rows(upstream, extent)
        unused, saved = block_forward(cropped.astype(jnp.float32), cropped, weights_set, extent)
        d_rows, grads = block_backward(sliced, cropped, weights_set, saved)
        return (widen_grid(d_rows, extent).reshape(GRID * GRID, -1), grads)

    return compute


def pool_table(grid_side):
    bin_index = lax.iota(jnp.int32, POOL)
    bin_lower = bin_index * grid_side // POOL
    bin_upper = ((bin_index + 1) * grid_side + POOL - 1) // POOL
    cell_index = lax.iota(jnp.int32, GRID)
    inside = (cell_index[None, :] >= bin_lower[:, None]) & (
        cell_index[None, :] < bin_upper[:, None]
    )
    weights = jnp.where(inside, 1.0, 0.0) / (bin_upper - bin_lower)[:, None]
    return weights.astype(jnp.float32)


def body(
    patches,
    grid_sizes,
    w_reduce_a,
    taps_a,
    w_expand_a,
    gain_a,
    w_reduce_b,
    taps_b,
    w_expand_b,
    gain_b,
    w_in,
    w_out,
    d_tokens,
):
    gathered = (
        lax.all_gather(w_reduce_a, "mp", axis=1, tiled=True),
        lax.all_gather(taps_a, "mp", axis=1, tiled=True),
        lax.all_gather(w_expand_a, "mp", axis=0, tiled=True),
        lax.all_gather(gain_a, "mp", axis=0, tiled=True),
        lax.all_gather(w_reduce_b, "mp", axis=1, tiled=True),
        lax.all_gather(taps_b, "mp", axis=1, tiled=True),
        lax.all_gather(w_expand_b, "mp", axis=0, tiled=True),
        lax.all_gather(gain_b, "mp", axis=0, tiled=True),
    )
    first_set = gathered[0:4]
    second_set = gathered[4:8]
    features = patches.shape[1]
    pictures = patches.reshape(-1, GRID * GRID, features)
    picture_count = pictures.shape[0]
    tables = jax.vmap(pool_table)(grid_sizes)

    def forward_one(element):
        pixels, grid_side, pool_weights = element
        result = lax.cond(
            grid_side == GRID,
            first_forward(first_set, GRID),
            first_forward(first_set, SMALL_GRID),
            pixels,
        )
        return jnp.einsum("ia,jb,abd->ijd", pool_weights, pool_weights, result, precision=highest)

    pooled = lax.map(forward_one, (pictures, grid_sizes, tables))
    pooled_rows = pooled.reshape(picture_count * POOL * POOL, features)
    pooled_low = pooled_rows.astype(jnp.bfloat16)
    mixed_rows, second_saved = block_forward(pooled_rows, pooled_low, second_set, POOL)
    queries = mixed_rows.astype(jnp.bfloat16)
    hidden = jnp.dot(
        lax.all_gather(queries, "mp", axis=0, tiled=True), w_in, preferred_element_type=jnp.float32
    )
    active = gelu_exact(hidden).astype(jnp.bfloat16)
    tokens = lax.psum_scatter(
        jnp.dot(active, w_out, preferred_element_type=jnp.float32).astype(jnp.bfloat16),
        "mp",
        scatter_dimension=0,
        tiled=True,
    )
    piece = lax.all_gather(d_tokens, "mp", axis=0, tiled=True)
    d_part = (times_trans(piece, w_out) * gelu_slope(hidden)).astype(jnp.bfloat16)
    grad_out_sum = outer_rows(active, piece)
    d_hidden = d_part
    d_part = d_hidden
    grad_in_part = outer_rows(lax.all_gather(queries, "mp", axis=0, tiled=True), d_part)
    d_part = d_hidden
    d_mixed = lax.psum_scatter(times_trans(d_part, w_in), "mp", scatter_dimension=0, tiled=True)
    d_pooled, second_grads = block_backward(d_mixed, pooled_low, second_set, second_saved)
    d_pooled = d_pooled.reshape(picture_count, POOL, POOL, features)

    def backward_one(totals, element):
        pixels, grid_side, pool_weights, upstream = element
        d_grid = jnp.einsum(
            "ia,jb,ijd->abd", pool_weights, pool_weights, upstream, precision=highest
        )
        d_pixels, grads = lax.cond(
            grid_side == GRID,
            first_backward(first_set, GRID),
            first_backward(first_set, SMALL_GRID),
            pixels,
            d_grid,
        )
        return (
            tuple((total_part + grad_part for total_part, grad_part in zip(totals, grads))),
            d_pixels,
        )

    zero_grads = tuple((jnp.zeros(weight.shape, jnp.float32) for weight in first_set))
    first_grads, d_pictures = lax.scan(
        backward_one, zero_grads, (pictures, grid_sizes, tables, d_pooled)
    )
    d_patches = d_pictures.reshape(-1, features)
    shards = (
        lax.psum_scatter(
            first_grads[0].astype(jnp.bfloat16), "mp", scatter_dimension=1, tiled=True
        ).astype(jnp.float32),
        lax.psum_scatter(
            first_grads[1].astype(jnp.bfloat16), "mp", scatter_dimension=1, tiled=True
        ).astype(jnp.float32),
        lax.psum_scatter(
            first_grads[2].astype(jnp.bfloat16), "mp", scatter_dimension=0, tiled=True
        ).astype(jnp.float32),
        lax.psum_scatter(
            first_grads[3].astype(jnp.bfloat16), "mp", scatter_dimension=0, tiled=True
        ).astype(jnp.float32),
        lax.psum_scatter(
            second_grads[0].astype(jnp.bfloat16), "mp", scatter_dimension=1, tiled=True
        ).astype(jnp.float32),
        lax.psum_scatter(
            second_grads[1].astype(jnp.bfloat16), "mp", scatter_dimension=1, tiled=True
        ).astype(jnp.float32),
        lax.psum_scatter(
            second_grads[2].astype(jnp.bfloat16), "mp", scatter_dimension=0, tiled=True
        ).astype(jnp.float32),
        lax.psum_scatter(
            second_grads[3].astype(jnp.bfloat16), "mp", scatter_dimension=0, tiled=True
        ).astype(jnp.float32),
    )
    summed = (
        lax.psum(shards[0].astype(jnp.bfloat16), "dp").astype(jnp.float32),
        lax.psum(shards[1].astype(jnp.bfloat16), "dp").astype(jnp.float32),
        lax.psum(shards[2].astype(jnp.bfloat16), "dp").astype(jnp.float32),
        lax.psum(shards[3].astype(jnp.bfloat16), "dp").astype(jnp.float32),
        lax.psum(shards[4].astype(jnp.bfloat16), "dp").astype(jnp.float32),
        lax.psum(shards[5].astype(jnp.bfloat16), "dp").astype(jnp.float32),
        lax.psum(shards[6].astype(jnp.bfloat16), "dp").astype(jnp.float32),
        lax.psum(shards[7].astype(jnp.bfloat16), "dp").astype(jnp.float32),
        lax.psum(grad_in_part.astype(jnp.bfloat16), "dp").astype(jnp.float32),
        lax.psum(grad_out_sum.astype(jnp.bfloat16), "dp").astype(jnp.float32),
    )
    return (
        tokens,
        d_patches,
        summed[0],
        summed[1],
        summed[2],
        summed[3],
        summed[4],
        summed[5],
        summed[6],
        summed[7],
        summed[8],
        summed[9],
    )


bf16 = jnp.bfloat16
f32 = jnp.float32
MESH = pl.DeviceIdType.MESH
CELLS = GRID * GRID
POOLED = POOL * POOL
TILE = 96
PIECES = 4
CHUNKS = 8


def dot(left, right, left_dim, right_dim):
    return lax.dot_general(
        left, right, (((left_dim,), (right_dim,)), ((), ())), preferred_element_type=f32
    )


def split_low(values):
    high = values.astype(bf16)
    return high, (values - high.astype(f32)).astype(bf16)


def edge_masks(extent, channels):
    cells = extent * extent
    index = lax.broadcasted_iota(jnp.int32, (cells, channels), 0).astype(f32)
    row = jnp.floor((index + 0.5) * (1.0 / extent))
    col = index - row * extent
    one = jnp.ones_like(index)
    zero = jnp.zeros_like(index)
    return (
        jnp.where(row >= 0.5, one, zero),
        jnp.where(row <= extent - 1.5, one, zero),
        jnp.where(col >= 0.5, one, zero),
        jnp.where(col <= extent - 1.5, one, zero),
    )


def conv_forward(act, taps, extent, masks):
    above, below, left, right = masks
    cells = extent * extent
    up = pltpu.roll(act, extent, 0) * above
    down = pltpu.roll(act, cells - extent, 0) * below
    sums = [up * taps[q] + act * taps[3 + q] + down * taps[6 + q] for q in range(3)]
    return (
        sums[1]
        + pltpu.roll(sums[0], 1, 0) * left
        + pltpu.roll(sums[2], cells - 1, 0) * right
    )


def conv_backward(upstream, act, taps, extent, masks):
    above, below, left, right = masks
    cells = extent * extent
    sides = [pltpu.roll(upstream, cells - 1, 0) * right, upstream, pltpu.roll(upstream, 1, 0) * left]
    sums = [
        sides[0] * taps[3 * r] + sides[1] * taps[3 * r + 1] + sides[2] * taps[3 * r + 2]
        for r in range(3)
    ]
    d_act = (
        sums[1]
        + pltpu.roll(sums[0], cells - extent, 0) * below
        + pltpu.roll(sums[2], extent, 0) * above
    )
    acts = [pltpu.roll(act, extent, 0) * above, act, pltpu.roll(act, cells - extent, 0) * below]
    d_taps = [
        jnp.sum(acts[r] * sides[q], axis=0, keepdims=True) for r in range(3) for q in range(3)
    ]
    return d_act, d_taps


def slot_rows(ref):
    slots, rows, columns = ref.shape
    return ref[...].reshape(slots * rows, columns)


def layer_kernel(
    patches_in, side_in, wr_a_in, taps_a_in, we_a_in, gain_a_in, wr_b_in, taps_b_in, we_b_in, gain_b_in,
    w_in_in, w_out_in, cot_in,
    tok_out, dpat_out, gout_out, gin_out, gblk_out, gsml_out, cot_all, gfl,
    xp, gw, gws, red_a, spa_a, nar_a, norm_a, inv_a, yhi, ylo, dy, dlow, pp,
    tw, poolv, red_b, spa_b, nar_b, norm_b, inv_b,
    wi, wo, qs, actv, slope, dpre, dtv, tp, cr, ps, rl, tstage,
    dps, dr, dz, gos, gis, gyl, land,
    wgs, wgc, xs, xr, zs, zr, ys, yr, sm, smc, smx, smz, smy, gfin,
    loc, w_s, w_rz, w_rx, w_rc, sw_s, sw_r, sy_s, sy_r, q_s, q_r, q_cs, q_rc,
    dt_s, dt_r, dt_cs, dt_cr, t_cs, t_cr, t_s, t_r, credit,
    d_cs, d_cr, d_zs, d_zr, gy_s, gy_r, gx_s, gx_r, ga_s, ga_r, gc_s, gc_r, gl,
    gr_s, gr_r,
):
    dp_at = lax.axis_index("dp")
    mp_at = lax.axis_index("mp")
    y = lax.div(dp_at, 2)
    c = lax.rem(dp_at, 2)
    z = lax.div(mp_at, 2)
    x = lax.rem(mp_at, 2)
    zn = 4

    def device(x_at, y_at, z_at, c_at):
        return (2 * y_at + c_at, 2 * z_at + x_at)

    twin = device(x, y, z, 1 - c)
    x_peer = device(1 - x, y, z, c)
    y_peer = device(x, 1 - y, z, c)
    z_high = lax.div(z, 2)
    z_low = lax.rem(z, 2)
    z_near = z + 1 - 2 * z_low
    z_far = z + 2 - 4 * z_high
    z_peer = device(x, y, z_near, c)
    far_peer = device(x, y, z_far, c)
    cross = device(x, y, z_far, 1 - c)
    corner = device(1 - x, y, z_near, c)
    slot_own = 2 * z_low + x
    slot_x = 2 * z_low + 1 - x
    slot_z = 2 * (1 - z_low) + x
    slot_corner = 2 * (1 - z_low) + 1 - x

    def z_at(step):
        return lax.rem(z + step + zn, zn)

    def z_dev(z_of):
        return device(x, y, z_of, c)

    def remote(src, dst, send, recv, to):
        return pltpu.make_async_remote_copy(
            src_ref=src, dst_ref=dst, send_sem=send, recv_sem=recv, device_id=to, device_id_type=MESH
        )

    def start(src, dst, send, recv, to):
        remote(src, dst, send, recv, to).start()

    def arrived(dst, recv):
        pltpu.make_async_copy(dst, dst, recv).wait()

    def left_here(src, send):
        pltpu.make_async_copy(src, src, send).wait()

    own = z_high == c

    load_patches = pltpu.make_async_copy(patches_in, xp, loc.at[0])
    me = 2 * slot_own + c
    load_patches.start()

    own_rows = pl.ds(pl.multiple_of(16 * c, 16), 16)
    gw[c, mp_at, 0:16, :] = wr_a_in[own_rows, :]
    gw[c, mp_at, 32:48, :] = wr_b_in[own_rows, :]
    gw[c, mp_at, 16:32, :] = we_a_in[own_rows, :]
    gw[c, mp_at, 48:64, :] = we_b_in[own_rows, :]
    unit = lax.broadcasted_iota(jnp.int32, (32, 256), 0)
    lane = lax.broadcasted_iota(jnp.int32, (32, 256), 1)
    place = 16 * mp_at + jnp.where(unit >= 16, unit + 112, unit)
    spread = jnp.where(lane == place, 1.0, 0.0).astype(bf16)
    gws[c, mp_at] = jnp.zeros((16, 256), f32)

    @pl.when(c == 0)
    def _():
        gws[0, mp_at, 0:9, :] = dot(taps_a_in[...], spread, 1, 0)
        gws[0, mp_at, 9:10, 0:128] = gain_a_in[...].astype(f32).reshape(1, 128)

    @pl.when(c == 1)
    def _():
        gws[1, mp_at, 0:9, :] = dot(taps_b_in[...], spread, 1, 0)
        gws[1, mp_at, 9:10, 0:128] = gain_b_in[...].astype(f32).reshape(1, 128)

    barrier = pltpu.get_barrier_semaphore()
    peers = [twin, x_peer, cross, y_peer, corner] + [z_dev(z_at(k)) for k in range(1, zn)]
    for peer in peers:
        pl.semaphore_signal(barrier, inc=1, device_id=peer, device_id_type=MESH)
    pl.semaphore_wait(barrier, len(peers))

    spans = ((0, 16), (16, 16), (32, 32))

    def w_part(b, core, i):
        if b == 3:
            return gws.at[core, i]
        return gw.at[core, i, pl.ds(spans[b][0], spans[b][1])]

    def w_own(b):
        part = w_part(b, c, mp_at)
        for k in range(1, zn):
            start(part, part, w_s.at[b, k - 1], w_rz.at[b, k], z_dev(z_at(k)))
        start(part, part, w_s.at[b, 3], w_rx.at[b, z], x_peer)
        start(part, part, w_s.at[b, 7], w_rc.at[b, mp_at], twin)

    def w_forward(b):
        for k in range(1, zn):
            z_of = z_at(-k)
            i = 2 * z_of + x
            part = w_part(b, c, i)
            arrived(part, w_rz.at[b, k])
            start(part, part, w_s.at[b, 3 + k], w_rx.at[b, z_of], x_peer)
            start(part, part, w_s.at[b, 7 + k], w_rc.at[b, i], twin)

    def w_over(b):
        for k in range(zn):
            z_of = z_at(-k)
            i = 2 * z_of + 1 - x
            part = w_part(b, c, i)
            arrived(part, w_rx.at[b, z_of])
            start(part, part, w_s.at[b, 11 + k], w_rc.at[b, i], twin)

    def w_finish(b):
        for i in range(8):
            arrived(w_part(b, 1 - c, i), w_rc.at[b, i])

    width = cot_in.shape[1] // PIECES

    def cot(slot, c_of, p):
        return cot_all.at[slot, c_of, :, pl.ds(pl.multiple_of(p * width, width), width)]

    def cot_mine(p):
        return cot_in.at[:, pl.ds(pl.multiple_of(p * width, width), width)]

    def cot_twin(slot, p):
        part = cot(slot, c, p)
        start(part, part, dt_cs.at[p, slot], dt_cr.at[p, slot], twin)

    def cot_own_z(p):
        start(cot_mine(p), cot(slot_own, c, p), dt_s.at[p, 1], dt_r.at[p, 1], z_peer)

    def cot_own_x(p):
        start(cot_mine(p), cot(slot_own, c, p), dt_s.at[p, 0], dt_r.at[p, 0], x_peer)

    def cot_own_twin(p):
        start(cot_mine(p), cot(slot_own, c, p), dt_cs.at[p, slot_own], dt_cr.at[p, slot_own], twin)

    def cot_over_z(p):
        part = cot(slot_z, c, p)
        arrived(part, dt_r.at[p, 1])
        start(part, part, dt_s.at[p, 2], dt_r.at[p, 2], x_peer)
        cot_twin(slot_z, p)

    def cot_over_x(p):
        arrived(cot(slot_x, c, p), dt_r.at[p, 0])
        cot_twin(slot_x, p)

    def cot_corner(p):
        arrived(cot(slot_corner, c, p), dt_r.at[p, 2])
        cot_twin(slot_corner, p)

    chunk = w_out_in.shape[1] // CHUNKS

    def w_half(ref, j, half):
        if j == 0:
            return ref.at[pl.ds(pl.multiple_of(512 * half, 512), 512)]
        return ref.at[:, pl.ds(pl.multiple_of((j - 1) * width + half * chunk, chunk), chunk)]

    def swap_refs(j):
        return (w_in_in, wi) if j == 0 else (w_out_in, wo)

    def swap_send(j):
        src, dst = swap_refs(j)

        @pl.when(own)
        def _():
            pltpu.make_async_copy(w_half(src, j, y), w_half(dst, j, y), sw_r.at[j]).start()
            pltpu.make_async_copy(w_half(src, j, 1 - y), w_half(dst, j, 1 - y), sy_r.at[j]).start()

        @pl.when(jnp.logical_not(own))
        def _():
            start(w_half(src, j, y), w_half(dst, j, y), sw_s.at[j], sw_r.at[j], cross)

    def swap_forward(j):
        part = w_half(swap_refs(j)[1], j, y)
        arrived(part, sw_r.at[j])

        @pl.when(jnp.logical_not(own))
        def _():
            start(part, part, sy_s.at[j], sy_r.at[j], y_peer)

    def swap_ready(j):
        arrived(w_half(swap_refs(j)[1], j, 1 - y), sy_r.at[j])

    def reduce_weights(b):
        return gw[:, :, 32 * b : 32 * b + 16, :].reshape(256, 1024)

    def expand_weights(b):
        return gw[:, :, 32 * b + 16 : 32 * b + 32, :].reshape(256, 1024)

    def small_weights(b):
        total = gws[b, 0, 0:9, :]
        for i in range(1, 8):
            total = total + gws[b, i, 0:9, :]
        tw[b, 0:9, 0:256] = total
        for i in range(8):
            tw[b, 9:10, 128 * i : 128 * i + 128] = gws[b, i, 9:10, 0:128]
        return tw[b, 9:10, :]

    def lanes_of(h):
        return pl.ds(pl.multiple_of(h * 128, 128), 128)

    def tap_rows(b, lanes):
        return [tw[b, k : k + 1, lanes] for k in range(9)]

    def normalise(wide_ref, ref, inv_ref, rows):
        widened = wide_ref[rows, :]
        centred = widened - jnp.mean(widened, axis=1, keepdims=True)
        inv = lax.rsqrt(jnp.mean(centred * centred, axis=1, keepdims=True) + epsilon)
        normed = centred * inv
        ref[rows, :] = normed.astype(ref.dtype)
        inv_ref[rows, :] = jnp.broadcast_to(inv, (normed.shape[0], 128))
        return normed

    side = side_in[0].astype(f32)

    def cell_mask():
        index = lax.broadcasted_iota(jnp.int32, (CELLS, 128), 0).astype(f32)
        row = jnp.floor((index + 0.5) * (1.0 / GRID))
        col = index - row * GRID
        return jnp.where((row < side - 0.5) & (col < side - 0.5), 1.0, 0.0).astype(f32)


    def first_conv():
        small_weights(0)
        load_patches.wait()
        red_a[...] = dot(xp[...], reduce_weights(0), 1, 1)

        def conv_half_a(h, carry):
            lanes = lanes_of(h)
            reduced = red_a[:, lanes]
            activated = reduced * jax.nn.sigmoid(reduced) * cell_mask()
            spatial = conv_forward(activated, tap_rows(0, lanes), GRID, edge_masks(GRID, 128))
            spa_a[:, lanes] = spatial
            nar_a[:, lanes] = (spatial * jax.nn.sigmoid(spatial)).astype(bf16)
            return carry

        lax.fori_loop(0, 2, conv_half_a, 0)

    def first_norm():
        dy[...] = dot(nar_a[...], expand_weights(0), 1, 0)
        gain_a = tw[0, 9:10, :]

        def norm_tile(t, carry):
            rows = pl.ds(pl.multiple_of(t * TILE, TILE), TILE)
            normed = normalise(dy, norm_a, inv_a, rows)
            result = xp[rows, :].astype(f32) + normed * gain_a
            high, low = split_low(result)
            yhi[rows, :] = high
            ylo[rows, :] = low
            return carry

        lax.fori_loop(0, CELLS // TILE, norm_tile, 0)

    def first_pool():
        cell = lax.broadcasted_iota(jnp.int32, (POOLED, CELLS), 1).astype(f32)
        bin_of = lax.broadcasted_iota(jnp.int32, (POOLED, CELLS), 0).astype(f32)
        cell_row = jnp.floor((cell + 0.5) * (1.0 / GRID))
        cell_col = cell - cell_row * GRID
        bin_row = jnp.floor((bin_of + 0.5) * (1.0 / POOL))
        bin_col = bin_of - bin_row * POOL

        def table(bins, at):
            lower = jnp.floor((bins * side + 0.5) * (1.0 / POOL))
            upper = jnp.floor(((bins + 1.0) * side + (POOL - 0.5)) * (1.0 / POOL))
            return jnp.where((at > lower - 0.5) & (at < upper - 0.5), 1.0 / (upper - lower), 0.0)

        pp[...] = (table(bin_row, cell_row) * table(bin_col, cell_col)).astype(bf16)
        poolv[...] = dot(pp[...], yhi[...], 1, 0) + dot(pp[...], ylo[...], 1, 0)

    def second_forward():
        gain_b = small_weights(1)
        pooled = poolv[...]
        reduced_b = dot(pooled.astype(bf16), reduce_weights(1), 1, 1)
        red_b[...] = reduced_b
        activated_b = reduced_b * jax.nn.sigmoid(reduced_b)
        spatial_b = conv_forward(activated_b, tap_rows(1, pl.ds(0, 256)), POOL, edge_masks(POOL, 256))
        spa_b[...] = spatial_b
        nar_b[...] = (spatial_b * jax.nn.sigmoid(spatial_b)).astype(bf16)
        norm_b[...] = dot(nar_b[...], expand_weights(1), 1, 0)
        normed_b = normalise(norm_b, norm_b, inv_b, pl.ds(0, POOLED))
        qs[me] = (pooled + normed_b * gain_b).astype(bf16)

    def query_to(k, to):
        start(qs.at[me], qs.at[me], q_s.at[k], q_r.at[k], to)

    def query_twin():
        start(qs.at[me], qs.at[me], q_s.at[3], q_rc.at[slot_own], twin)

    def query_from(k):
        slot = (slot_x, slot_z, slot_corner)[k]
        part = qs.at[2 * slot + c]
        arrived(part, q_r.at[k])
        start(part, part, q_cs.at[k], q_rc.at[slot], twin)

    def query_all():
        for slot in (slot_own, slot_x, slot_z, slot_corner):
            arrived(qs.at[2 * slot + 1 - c], q_rc.at[slot])

    def hidden_units():
        dpre[...] = dot(slot_rows(qs), wi[...], 1, 0)

        def gelu_tile(t, carry):
            rows = pl.ds(pl.multiple_of(t * POOLED, POOLED), POOLED)
            hidden = dpre[rows, :]
            phi = 0.5 * (1.0 + lax.erf(hidden * root_half))
            actv[rows, :] = (hidden * phi).astype(bf16)
            slope[rows, :] = (
                phi + hidden * jnp.exp(-0.5 * hidden * hidden) * inv_root_tau
            ).astype(bf16)
            return carry

        lax.fori_loop(0, 8, gelu_tile, 0)
        dpre[...] = jnp.zeros_like(dpre)

    def item_part(i):
        b = i % 2

        if i >= 2:
            left_here(tp.at[b], t_cs.at[b])
            pl.semaphore_wait(credit, 1)


        weights = wo[:, i * chunk : (i + 1) * chunk]
        partial = dot(actv[...], weights, 1, 0).astype(bf16)
        partial = partial.reshape(4, 2, POOLED, chunk)

        @pl.when(c == 0)
        def _():
            ps[i] = partial[:, 0]
            tp[b] = partial[:, 1]

        @pl.when(c == 1)
        def _():
            ps[i] = partial[:, 1]
            tp[b] = partial[:, 0]

        start(tp.at[b], cr.at[b], t_cs.at[b], t_cr.at[b], twin)

    def item_pair(i):
        b = i % 2
        arrived(cr.at[b], t_cr.at[b])

        def add(d, carry):
            ps[i, d] = (ps[i, d].astype(f32) + cr[b, d].astype(f32)).astype(bf16)
            return carry

        lax.fori_loop(0, 4, add, 0)

        if i < CHUNKS - 2:
            pl.semaphore_signal(credit, inc=1, device_id=twin, device_id_type=MESH)

        start(ps.at[i, slot_corner], rl.at[i, 0], t_s.at[i, 0], t_r.at[i, 0], x_peer)
        start(ps.at[i, slot_x], rl.at[i, 1], t_s.at[i, 1], t_r.at[i, 1], x_peer)

    def item_pass(i):
        arrived(rl.at[i, 0], t_r.at[i, 0])
        ps[i, slot_z] = (ps[i, slot_z].astype(f32) + rl[i, 0].astype(f32)).astype(bf16)
        start(ps.at[i, slot_z], rl.at[i, 2], t_s.at[i, 2], t_r.at[i, 2], z_peer)

    def tok_slice(i):
        return tok_out.at[:, pl.ds(i * chunk, chunk)]

    def item_final(i):
        b = i % 2

        if i >= 2:
            left_here(tstage.at[b], gl.at[8 + b])

        arrived(rl.at[i, 1], t_r.at[i, 1])
        arrived(rl.at[i, 2], t_r.at[i, 2])
        for k in range(3):
            left_here(ps.at[i, 0], t_s.at[i, k])
        tstage[b] = (
            ps[i, slot_own].astype(f32) + rl[i, 1].astype(f32) + rl[i, 2].astype(f32)
        ).astype(bf16)
        pltpu.make_async_copy(tstage.at[b], tok_slice(i), gl.at[8 + b]).start()

    def piece_rows(p):
        for slot in range(4):
            arrived(cot(slot, 1 - c, p), dt_cr.at[p, slot])

            @pl.when(slot_own != slot)
            def _():
                part = cot_all.at[slot, :, :, pl.ds(p * width, width)]
                pltpu.make_async_copy(part, dtv.at[pl.ds(2 * slot, 2)], loc.at[3]).start()

        pltpu.make_async_copy(cot(slot_own, 1 - c, p), dtv.at[2 * slot_own + 1 - c], loc.at[3]).start()
        pltpu.make_async_copy(cot_mine(p), dtv.at[2 * slot_own + c], loc.at[3]).start()
        pltpu.make_async_copy(dtv, dtv, loc.at[3]).wait()

    def half_lanes(half):
        return pl.ds(pl.multiple_of(half * chunk, chunk), chunk)

    def piece_lanes(h):
        return dtv[:, :, half_lanes(h)].reshape(8 * POOLED, chunk)

    def hidden_part(p):
        def hidden_half(h, carry):
            weights = wo[:, pl.ds(pl.multiple_of(p * width + h * chunk, chunk), chunk)]
            dpre[...] += dot(piece_lanes(h), weights, 1, 1)
            return carry

        lax.fori_loop(0, 2, hidden_half, 0)

    def row_part(slot):
        rows = pl.ds(pl.multiple_of(slot * (2 * POOLED), 2 * POOLED), 2 * POOLED)
        d_hidden = (dpre[rows, :] * slope[rows, :].astype(f32)).astype(bf16)
        half = lax.div(slot, 2)
        place = pl.ds(pl.multiple_of((slot - 2 * half) * (2 * POOLED), 2 * POOLED), 2 * POOLED)
        ylo[place, pl.ds(pl.multiple_of(half * 512, 512), 512)] = d_hidden
        dps[slot] = dot(d_hidden, wi[...], 1, 1).astype(bf16).reshape(2, POOLED, 1024)
        start(dps.at[slot, 1 - c], dr.at[slot], d_cs.at[slot], d_cr.at[slot], twin)

    def in_turn(k):
        return jnp.where(k == 0, slot_corner, jnp.where(k == 1, slot_x, jnp.where(k == 2, slot_z, slot_own)))

    def row_gradients():
        def one(k, carry):
            @pl.when(k < 4)
            def _():
                row_part(in_turn(k))

            slot = in_turn(k - 1)

            @pl.when(k >= 1)
            def _():
                arrived(dr.at[slot], d_cr.at[slot])
                dps[slot, c] = (dps[slot, c].astype(f32) + dr[slot].astype(f32)).astype(bf16)

            @pl.when(k == 1)
            def _():
                start(dps.at[slot, c], dz.at[2], d_zs.at[2], d_zr.at[2], corner)

            @pl.when(k == 2)
            def _():
                start(dps.at[slot, c], dz.at[0], d_zs.at[0], d_zr.at[0], x_peer)

            @pl.when(k == 3)
            def _():
                start(dps.at[slot, c], dz.at[1], d_zs.at[1], d_zr.at[1], z_peer)

            return carry

        lax.fori_loop(0, 5, one, 0)

    def drain_first():
        for b in range(4):
            for k in range(15):
                left_here(w_part(b, c, 0), w_s.at[b, k])
        for k in range(4):
            left_here(qs.at[0], q_s.at[k])
        for k in range(3):
            left_here(qs.at[0], q_cs.at[k])
        for p in range(PIECES):
            for slot in range(4):
                left_here(cot(0, 0, p), dt_cs.at[p, slot])
            for k in range(3):
                left_here(cot(0, 0, p), dt_s.at[p, k])

        for j in range(1 + PIECES):
            @pl.when(jnp.logical_not(own))
            def _(j=j):
                part = w_half(swap_refs(j)[1], j, y)
                left_here(part, sw_s.at[j])
                left_here(part, sy_s.at[j])

    def grad_half(j, half):
        if j == PIECES:
            return gis.at[pl.ds(pl.multiple_of(512 * half, 512), 512)]
        return gos.at[j, :, half_lanes(half)]

    def out_half(j, half):
        if j == PIECES:
            return gin_out.at[pl.ds(pl.multiple_of(512 * half, 512), 512)]
        return gout_out.at[:, pl.ds(pl.multiple_of(j * width + half * chunk, chunk), chunk)]

    def grad_send(j, h):
        rows = pl.ds(256 * h, 256)
        if j == PIECES:
            part = gis.at[pl.ds(pl.multiple_of(512 * (1 - y) + 256 * h, 256), 256)]
        else:
            part = gos.at[j, rows, half_lanes(1 - y)]
        start(part, gyl.at[j, rows], gy_s.at[j, h], gy_r.at[j, h], y_peer)

    def grad_part(p):
        def one_half(h, carry):
            gos[p, :, half_lanes(h)] = dot(actv[...], piece_lanes(h), 0, 0).astype(bf16)
            return carry

        lax.fori_loop(0, 2, one_half, 0)

    def gin_part():
        gis[...] = (
            dot(qs[0:4].reshape(4 * POOLED, 1024), ylo[:, 0:512], 0, 0)
            + dot(qs[4:8].reshape(4 * POOLED, 1024), ylo[:, 512:1024], 0, 0)
        ).astype(bf16)

    def grad_pair(j):
        mine = grad_half(j, y)
        for h in range(2):
            arrived(gyl.at[j, pl.ds(256 * h, 256)], gy_r.at[j, h])
        mine[...] = (mine[...].astype(f32) + gyl[j].astype(f32)).astype(bf16)

        @pl.when(jnp.logical_not(own))
        def _():
            start(mine, gfl.at[j], gx_s.at[j], gx_r.at[j], far_peer)

    def grad_sum(j):
        @pl.when(own)
        def _():
            mine = grad_half(j, y)
            arrived(gfl.at[j], gx_r.at[j])
            load = pltpu.make_async_copy(gfl.at[j], land, loc.at[4])
            load.start()
            load.wait()
            mine[...] = (mine[...].astype(f32) + land[...].astype(f32)).astype(bf16)
            start(mine, out_half(j, y), ga_s.at[j], ga_r.at[j], y_peer)
            start(mine, out_half(j, y), gc_s.at[j, 0], gc_r.at[j, 0], twin)
            pltpu.make_async_copy(mine, out_half(j, y), gl.at[j]).start()

    def grad_last(j):
        @pl.when(own)
        def _():
            other = out_half(j, 1 - y)
            arrived(other, ga_r.at[j])
            start(other, other, gc_s.at[j, 1], gc_r.at[j, 1], twin)

    def grad_done(j):
        for h in range(2):
            left_here(gyl.at[j, pl.ds(256 * h, 256)], gy_s.at[j, h])

        @pl.when(own)
        def _():
            left_here(grad_half(j, y), ga_s.at[j])
            left_here(grad_half(j, y), gc_s.at[j, 0])
            left_here(grad_half(j, y), gc_s.at[j, 1])
            pltpu.make_async_copy(grad_half(j, y), out_half(j, y), gl.at[j]).wait()

        @pl.when(jnp.logical_not(own))
        def _():
            left_here(grad_half(j, y), gx_s.at[j])
            arrived(out_half(j, y), gc_r.at[j, 0])
            arrived(out_half(j, 1 - y), gc_r.at[j, 1])

    def widened_back(d_rows, normed, gain, inv):
        dn = d_rows * gain
        return (
            inv
            * (
                dn
                - jnp.mean(dn, axis=1, keepdims=True)
                - normed * jnp.mean(dn * normed, axis=1, keepdims=True)
            )
        ).astype(bf16)

    def pack_small(t, d_gain):
        for k in range(4):
            sm[t, 9 + k : 10 + k, :] = d_gain[:, 256 * k : 256 * k + 256]
        sm[t, 13:16, :] = jnp.zeros((3, 256), f32)

    passes = ((1, 0, 2, 1), (0, 1, 1, None), (0, 0, 1, 0))

    def share_core(p):
        t, k0, n, small = passes[p]
        kinds = pl.ds(k0, n)
        start(
            wgs.at[t, kinds, pl.ds(pl.multiple_of(128 * (1 - c), 128), 128)], wgc.at[t, kinds],
            gr_s.at[p, 0], gr_r.at[p, 0], twin,
        )
        if small is not None:
            start(sm.at[t], smc.at[t], gr_s.at[p, 1], gr_r.at[p, 1], twin)

    def share_x(p):
        t, k0, n, small = passes[p]
        kinds = pl.ds(k0, n)
        arrived(wgc.at[t, kinds], gr_r.at[p, 0])
        for kind in range(k0, k0 + n):
            for i in range(8):
                rows = pl.ds(pl.multiple_of(128 * c + 16 * i, 16), 16)
                xs[t, kind, i % 2, i // 2] = (
                    wgs[t, kind, rows, :].astype(f32) + wgc[t, kind, 16 * i : 16 * i + 16, :].astype(f32)
                ).astype(bf16)
        start(xs.at[t, kinds, 1 - x], xr.at[t, kinds], gr_s.at[p, 2], gr_r.at[p, 2], x_peer)
        if small is not None:
            arrived(smc.at[t], gr_r.at[p, 1])
            left_here(sm.at[t], gr_s.at[p, 1])
            sm[t] = sm[t] + smc[t]
            start(sm.at[t], smx.at[t], gr_s.at[p, 3], gr_r.at[p, 3], x_peer)

    def share_z(p):
        t, k0, n, small = passes[p]
        kinds = pl.ds(k0, n)
        arrived(xr.at[t, kinds], gr_r.at[p, 2])
        for kind in range(k0, k0 + n):
            zs[t, kind] = (xs[t, kind, x].astype(f32) + xr[t, kind].astype(f32)).astype(bf16)
        for k in range(1, zn):
            d = z_at(k)
            start(
                zs.at[t, kinds, d], zr.at[t, kinds, k - 1], gr_s.at[p, 3 + k], gr_r.at[p, 3 + k], z_dev(d)
            )
        if small is not None:
            arrived(smx.at[t], gr_r.at[p, 3])
            left_here(sm.at[t], gr_s.at[p, 3])
            smz[t, z] = sm[t] + smx[t]
            for k in range(1, zn):
                start(
                    smz.at[t, z], smz.at[t, z], gr_s.at[p, 6 + k], gr_r.at[p, 6 + k], z_dev(z_at(k))
                )

    def share_y(p):
        t, k0, n, small = passes[p]
        kinds = pl.ds(k0, n)
        for k in range(1, zn):
            arrived(zr.at[t, kinds, k - 1], gr_r.at[p, 3 + k])
        for kind in range(k0, k0 + n):
            total_rows = zs[t, kind, z].astype(f32)
            for k in range(1, zn):
                total_rows = total_rows + zr[t, kind, k - 1].astype(f32)
            ys[t, kind] = total_rows.astype(bf16)
        start(ys.at[t, kinds], yr.at[t, kinds], gr_s.at[p, 10], gr_r.at[p, 10], y_peer)
        if small is not None:
            for k in range(1, zn):
                arrived(smz.at[t, z_at(-k)], gr_r.at[p, 6 + k])
            sm[t] = (smz[t, 0] + smz[t, 1]) + (smz[t, 2] + smz[t, 3])
            start(sm.at[t], smy.at[t], gr_s.at[p, 11], gr_r.at[p, 11], y_peer)

    def share_twin(p):
        t, k0, n, small = passes[p]
        kinds = pl.ds(k0, n)
        arrived(yr.at[t, kinds], gr_r.at[p, 10])
        for kind in range(k0, k0 + n):
            gfin[c, t, kind] = ys[t, kind].astype(f32) + yr[t, kind].astype(f32)
        part = gfin.at[c, t, kinds]
        start(part, part, gr_s.at[p, 12], gr_r.at[p, 12], twin)
        if small is not None:
            arrived(smy.at[t], gr_r.at[p, 11])
            gsml_out[t] = sm[t] + smy[t]

    def share_done(p):
        t, k0, n, small = passes[p]
        kinds = pl.ds(k0, n)
        arrived(gfin.at[1 - c, t, kinds], gr_r.at[p, 12])
        for kind in range(k0, k0 + n):
            for h in range(2):
                gblk_out[t, kind, 16 * h : 16 * h + 16, :] = gfin[h, t, kind]
        left_here(wgc.at[t, kinds], gr_s.at[p, 0])
        left_here(xr.at[t, kinds], gr_s.at[p, 2])
        for k in range(1, zn):
            left_here(ys.at[t, kinds], gr_s.at[p, 3 + k])
        left_here(ys.at[t, kinds], gr_s.at[p, 10])
        left_here(gfin.at[c, t, kinds], gr_s.at[p, 12])
        if small is not None:
            for k in range(1, zn):
                left_here(sm.at[t], gr_s.at[p, 6 + k])
            left_here(sm.at[t], gr_s.at[p, 11])

    def back_second():
        total = dps[slot_own, c].astype(f32)
        for k in range(3):
            arrived(dz.at[k], d_zr.at[k])
            total = total + dz[k].astype(f32)
        normed_b = norm_b[...]
        d_gain_b = jnp.sum(total * normed_b, axis=0, keepdims=True)
        gain_b = tw[1, 9:10, :]
        dw_b = widened_back(total, normed_b, gain_b, inv_b[:, 0:1])
        wgs[1, 1] = dot(nar_b[...], dw_b, 0, 0).astype(bf16)
        spatial_b = spa_b[...]
        d_spatial_b = dot(dw_b, expand_weights(1), 1, 1) * silu_slope(spatial_b)
        reduced_b = red_b[...]
        sig_b = jax.nn.sigmoid(reduced_b)
        d_act_b, d_taps_b = conv_backward(
            d_spatial_b, reduced_b * sig_b, tap_rows(1, pl.ds(0, 256)), POOL, edge_masks(POOL, 256)
        )
        d_red_b = (d_act_b * (sig_b * (1.0 + reduced_b * (1.0 - sig_b)))).astype(bf16)
        wgs[1, 0] = dot(d_red_b, poolv[...].astype(bf16), 0, 0).astype(bf16)
        for k in range(9):
            sm[1, k : k + 1, :] = d_taps_b[k]
        pack_small(1, d_gain_b)
        d_pool = total + dot(d_red_b, reduce_weights(1), 1, 0)
        high, low = split_low(d_pool)
        dy[...] = dot(pp[...], high, 0, 0) + dot(pp[...], low, 0, 0)

    def back_first_norm():
        gain_a = tw[0, 9:10, :]

        def back_tile(t, d_gain):
            rows = pl.ds(pl.multiple_of(t * TILE, TILE), TILE)
            d_rows = dy[rows, :]
            normed = norm_a[rows, :].astype(f32)
            yhi[rows, :] = widened_back(d_rows, normed, gain_a, inv_a[rows, 0:1])
            return d_gain + jnp.sum(d_rows * normed, axis=0, keepdims=True)

        d_gain_a = lax.fori_loop(0, CELLS // TILE, back_tile, jnp.zeros((1, 1024), f32))
        pack_small(0, d_gain_a)
        wgs[0, 1] = dot(nar_a[...], yhi[...], 0, 0).astype(bf16)

    def back_first_conv():
        spa_a[...] = dot(yhi[...], expand_weights(0), 1, 1) * silu_slope(spa_a[...])

        def conv_back_half_a(h, carry):
            lanes = lanes_of(h)
            reduced = red_a[:, lanes]
            sig = jax.nn.sigmoid(reduced)
            mask = cell_mask()
            d_act, d_taps = conv_backward(
                spa_a[:, lanes], reduced * sig * mask, tap_rows(0, lanes), GRID, edge_masks(GRID, 128)
            )
            dlow[:, lanes] = (d_act * mask * (sig * (1.0 + reduced * (1.0 - sig)))).astype(bf16)
            for k in range(9):
                sm[0, k : k + 1, lanes] = d_taps[k]
            return carry

        lax.fori_loop(0, 2, conv_back_half_a, 0)
        wgs[0, 0] = dot(dlow[...], xp[...], 0, 0).astype(bf16)

    store_dpat = pltpu.make_async_copy(dy, dpat_out, loc.at[5])

    def back_first_rows():
        dy[...] += dot(dlow[...], reduce_weights(0), 1, 0)
        store_dpat.start()

    w_own(1)
    cot_own_twin(0)
    cot_own_x(3)
    cot_own_x(0)
    w_own(3)
    cot_own_twin(3)
    w_own(0)
    w_own(2)
    cot_own_z(0)
    swap_send(0)
    swap_send(1)
    w_forward(3)
    w_forward(1)
    w_forward(0)
    w_over(3)
    w_forward(2)
    w_finish(3)
    cot_own_x(2)
    w_over(0)
    cot_own_z(1)
    swap_send(2)
    w_over(1)
    w_finish(0)
    w_finish(1)
    first_conv()
    first_norm()
    cot_over_z(0)
    cot_own_twin(2)
    cot_over_x(3)
    first_pool()
    w_over(2)
    swap_forward(0)
    w_finish(2)
    swap_forward(1)
    second_forward()
    query_to(2, corner)
    query_twin()
    query_to(1, z_peer)
    query_to(0, x_peer)
    cot_corner(0)
    swap_forward(2)
    cot_over_x(0)
    piece_rows(0)
    swap_ready(1)
    swap_ready(0)
    query_from(2)
    swap_send(3)
    cot_own_z(2)
    cot_own_x(1)
    query_from(1)
    query_from(0)
    swap_send(4)
    cot_over_z(1)
    query_all()
    hidden_units()

    grad_part(0)
    grad_send(0, 0)
    grad_send(0, 1)
    cot_over_x(1)
    cot_over_z(2)
    cot_own_twin(1)
    item_part(0)
    swap_ready(2)
    cot_own_z(3)
    hidden_part(0)
    cot_corner(1)
    swap_forward(3)
    piece_rows(1)
    item_pair(0)
    item_part(1)
    grad_part(1)
    item_part(2)
    grad_send(1, 0)
    grad_pair(0)
    cot_corner(2)
    cot_over_z(3)
    cot_over_x(2)
    item_pair(1)
    swap_ready(3)
    hidden_part(1)
    item_part(3)
    grad_send(1, 1)
    piece_rows(2)
    swap_forward(4)
    grad_part(2)
    hidden_part(2)
    cot_corner(3)
    item_pair(2)
    item_pass(0)
    grad_send(2, 0)
    grad_send(2, 1)
    item_pair(3)
    item_pass(1)
    grad_pair(1)
    piece_rows(3)
    item_part(4)
    swap_ready(4)
    hidden_part(3)
    row_gradients()
    grad_part(3)
    grad_send(3, 1)
    item_pair(4)
    item_part(5)
    item_part(6)
    grad_pair(2)
    item_final(0)
    item_pair(5)
    grad_send(3, 0)
    grad_sum(1)
    gin_part()
    item_final(1)
    item_pass(2)
    grad_pair(3)
    item_pair(6)
    drain_first()
    back_second()
    share_core(0)
    grad_send(PIECES, 0)
    grad_send(PIECES, 1)
    item_pass(3)
    grad_sum(0)
    back_first_norm()
    item_pass(4)
    item_part(7)
    back_first_conv()
    share_core(2)
    grad_sum(3)
    share_x(0)
    grad_sum(2)
    grad_pair(PIECES)
    share_core(1)
    share_x(2)
    item_pass(5)
    share_z(0)
    share_x(1)
    grad_sum(PIECES)
    item_pass(6)
    grad_last(1)
    grad_last(0)
    item_final(2)
    item_final(3)
    item_pair(7)
    item_final(4)
    item_final(5)
    back_first_rows()
    share_z(2)
    grad_last(3)
    item_final(6)
    share_z(1)
    share_y(0)
    share_y(2)
    grad_last(PIECES)
    item_pass(7)
    share_y(1)
    grad_last(2)
    share_twin(2)
    share_twin(0)
    share_twin(1)
    for j in range(3):
        grad_done(j)
    for p in range(2):
        share_done(p)
    item_final(7)

    share_done(2)
    for j in range(3, 1 + PIECES):
        grad_done(j)

    store_dpat.wait()
    for b in range(2):
        pltpu.make_async_copy(tstage.at[b], tok_slice(b), gl.at[8 + b]).wait()
        left_here(tp.at[b], t_cs.at[b])
    for k in range(4):
        left_here(dps.at[0, 0], d_cs.at[k])
    for k in range(3):
        left_here(dps.at[0, 0], d_zs.at[k])


def layer_call(
    patches, grid_sizes, wr_a, taps_a, we_a, gain_a, wr_b, taps_b, we_b, gain_b, w_in, w_out, d_tokens
):
    any_space = pl.BlockSpec(memory_space=pl.ANY)
    vmem = pl.BlockSpec(memory_space=pltpu.VMEM)
    smem = pl.BlockSpec(memory_space=pltpu.SMEM)
    shape = jax.ShapeDtypeStruct
    width = w_out.shape[1] // PIECES
    chunk = w_out.shape[1] // CHUNKS
    out_shape = (
        shape((POOLED, 4096), bf16),
        shape((CELLS, 1024), f32),
        shape((512, 4096), bf16),
        shape((1024, 512), bf16),
        shape((2, 2, 32, 1024), f32),
        shape((2, 16, 256), f32),
        shape((4, 2, POOLED, 4096), bf16),
        shape((1 + PIECES, 512, width // 2), bf16),
    )
    dma = pltpu.SemaphoreType.DMA
    scratch = [
        pltpu.VMEM((CELLS, 1024), bf16),
        pltpu.VMEM((2, 8, 64, 1024), bf16),
        pltpu.VMEM((2, 8, 16, 256), f32),
        pltpu.VMEM((CELLS, 256), f32),
        pltpu.VMEM((CELLS, 256), f32),
        pltpu.VMEM((CELLS, 256), bf16),
        pltpu.VMEM((CELLS, 1024), bf16),
        pltpu.VMEM((CELLS, 128), f32),
        pltpu.VMEM((CELLS, 1024), bf16),
        pltpu.VMEM((CELLS, 1024), bf16),
        pltpu.VMEM((CELLS, 1024), f32),
        pltpu.VMEM((CELLS, 256), bf16),
        pltpu.VMEM((POOLED, CELLS), bf16),
        pltpu.VMEM((2, 16, 1024), f32),
        pltpu.VMEM((POOLED, 1024), f32),
        pltpu.VMEM((POOLED, 256), f32),
        pltpu.VMEM((POOLED, 256), f32),
        pltpu.VMEM((POOLED, 256), bf16),
        pltpu.VMEM((POOLED, 1024), f32),
        pltpu.VMEM((POOLED, 128), f32),
        pltpu.VMEM((1024, 512), bf16),
        pltpu.VMEM((512, 4096), bf16),
        pltpu.VMEM((8, POOLED, 1024), bf16),
        pltpu.VMEM((8 * POOLED, 512), bf16),
        pltpu.VMEM((8 * POOLED, 512), bf16),
        pltpu.VMEM((8 * POOLED, 512), f32),
        pltpu.VMEM((8, POOLED, width), bf16),
        pltpu.VMEM((2, 4, POOLED, chunk), bf16),
        pltpu.VMEM((2, 4, POOLED, chunk), bf16),
        pltpu.VMEM((CHUNKS, 4, POOLED, chunk), bf16),
        pltpu.VMEM((CHUNKS, 3, POOLED, chunk), bf16),
        pltpu.VMEM((2, POOLED, chunk), bf16),
        pltpu.VMEM((4, 2, POOLED, 1024), bf16),
        pltpu.VMEM((4, POOLED, 1024), bf16),
        pltpu.VMEM((3, POOLED, 1024), bf16),
        pltpu.VMEM((PIECES, 512, width), bf16),
        pltpu.VMEM((1024, 512), bf16),
        pltpu.VMEM((1 + PIECES, 512, width // 2), bf16),
        pltpu.VMEM((512, width // 2), bf16),
        pltpu.VMEM((2, 2, 256, 1024), bf16),
        pltpu.VMEM((2, 2, 128, 1024), bf16),
        pltpu.VMEM((2, 2, 2, 4, 16, 1024), bf16),
        pltpu.VMEM((2, 2, 4, 16, 1024), bf16),
        pltpu.VMEM((2, 2, 4, 16, 1024), bf16),
        pltpu.VMEM((2, 2, 3, 16, 1024), bf16),
        pltpu.VMEM((2, 2, 16, 1024), bf16),
        pltpu.VMEM((2, 2, 16, 1024), bf16),
        pltpu.VMEM((2, 16, 256), f32),
        pltpu.VMEM((2, 16, 256), f32),
        pltpu.VMEM((2, 16, 256), f32),
        pltpu.VMEM((2, 4, 16, 256), f32),
        pltpu.VMEM((2, 16, 256), f32),
        pltpu.VMEM((2, 2, 2, 16, 1024), f32),
        dma((6,)),
        dma((4, 15)),
        dma((4, 4)),
        dma((4, 4)),
        dma((4, 8)),
        dma((1 + PIECES,)),
        dma((1 + PIECES,)),
        dma((1 + PIECES,)),
        dma((1 + PIECES,)),
        dma((4,)),
        dma((3,)),
        dma((3,)),
        dma((4,)),
        dma((PIECES, 3)),
        dma((PIECES, 3)),
        dma((PIECES, 4)),
        dma((PIECES, 4)),
        dma((2,)),
        dma((2,)),
        dma((CHUNKS, 3)),
        dma((CHUNKS, 3)),
        pltpu.SemaphoreType.REGULAR,
        dma((4,)),
        dma((4,)),
        dma((3,)),
        dma((3,)),
        dma((1 + PIECES, 2)),
        dma((1 + PIECES, 2)),
        dma((1 + PIECES,)),
        dma((1 + PIECES,)),
        dma((1 + PIECES,)),
        dma((1 + PIECES,)),
        dma((1 + PIECES, 2)),
        dma((1 + PIECES, 2)),
        dma((10,)),
        dma((3, 13)),
        dma((3, 13)),
    ]
    return pl.pallas_call(
        layer_kernel,
        out_shape=out_shape,
        in_specs=[any_space, smem] + [vmem] * 8 + [any_space] * 3,
        out_specs=(any_space, any_space, any_space, any_space, vmem, vmem, any_space, any_space),
        scratch_shapes=scratch,
        compiler_params=pltpu.CompilerParams(
            collective_id=0, has_side_effects=True, vmem_limit_bytes=VMEM_BYTES
        ),
    )(
        patches, grid_sizes, wr_a, taps_a, we_a, gain_a, wr_b, taps_b, we_b, gain_b, w_in, w_out, d_tokens
    )


VMEM_BYTES = 64 * 1024 * 1024


FINISH = 2


def finish_kernel(
    tok_in, dpat_in, gout_in, gin_in, gblk_in, gsml_in,
    tok, dpat, gout, gin, gra, gta, gea, gga, grb, gtb, geb, ggb,
):
    tok[...] = tok_in[...]
    dpat[...] = dpat_in[...]
    gout[...] = gout_in[...].astype(f32)
    gin[...] = gin_in[...].astype(f32)

    @pl.when(pl.program_id(0) == 0)
    def _():
        mp_at = lax.axis_index("mp")
        for t, outs in enumerate(((gra, gta, gea, gga), (grb, gtb, geb, ggb))):
            reduce, taps, expand, gain = outs
            reduce[...] = gblk_in[t, 0]
            expand[...] = gblk_in[t, 1]
            turned = pltpu.roll(gsml_in[t], lax.rem(256 - 16 * mp_at, 256), 1)
            taps[:, 0:16] = turned[0:9, 0:16]
            taps[:, 16:32] = turned[0:9, 128:144]
            for i in range(8):
                @pl.when(mp_at == i)
                def _(t=t, i=i, gain=gain):
                    lanes = 128 * (i % 2)
                    gain[...] = gsml_in[t, 9 + i // 2 : 10 + i // 2, lanes : lanes + 128]


def finish_call(tokens, d_patches, gout, gin, gblk, gsml):
    shape = jax.ShapeDtypeStruct
    columns = tokens.shape[1] // FINISH

    def whole(*dims):
        return pl.BlockSpec(dims, lambda i: (0,) * len(dims))

    one = [whole(32, 1024), whole(9, 32), whole(32, 1024), whole(1, 128)]
    one_shape = [shape((32, 1024), f32), shape((9, 32), f32), shape((32, 1024), f32), shape((1, 128), f32)]
    return pl.pallas_call(
        finish_kernel,
        grid=(FINISH,),
        out_shape=[
            shape(tokens.shape, bf16),
            shape(d_patches.shape, f32),
            shape(gout.shape, f32),
            shape(gin.shape, f32),
        ]
        + one_shape * 2,
        in_specs=[
            pl.BlockSpec((POOLED, columns), lambda i: (0, i)),
            pl.BlockSpec((CELLS // FINISH, 1024), lambda i: (i, 0)),
            pl.BlockSpec((512 // FINISH, 4096), lambda i: (i, 0)),
            pl.BlockSpec((1024 // FINISH, 512), lambda i: (i, 0)),
            whole(2, 2, 32, 1024),
            whole(2, 16, 256),
        ],
        out_specs=[
            pl.BlockSpec((POOLED, columns), lambda i: (0, i)),
            pl.BlockSpec((CELLS // FINISH, 1024), lambda i: (i, 0)),
            pl.BlockSpec((512 // FINISH, 4096), lambda i: (i, 0)),
            pl.BlockSpec((1024 // FINISH, 512), lambda i: (i, 0)),
        ]
        + one * 2,
        compiler_params=pltpu.CompilerParams(vmem_limit_bytes=VMEM_BYTES),
    )(tokens, d_patches, gout, gin, gblk, gsml)


def fast_body(
    patches, grid_sizes, w_reduce_a, taps_a, w_expand_a, gain_a,
    w_reduce_b, taps_b, w_expand_b, gain_b, w_in, w_out, d_tokens,
):
    results = layer_call(
        patches, grid_sizes, w_reduce_a.T, taps_a, w_expand_a, gain_a,
        w_reduce_b.T, taps_b, w_expand_b, gain_b, w_in, w_out, d_tokens,
    )
    (
        tokens, d_patches, gout, gin, reduce_a, tap_a, expand_a, scale_a, reduce_b, tap_b, expand_b, scale_b
    ) = finish_call(*results[:6])
    return (
        tokens, d_patches,
        reduce_a.T, tap_a, expand_a, scale_a.reshape(-1),
        reduce_b.T, tap_b, expand_b, scale_b.reshape(-1),
        gin, gout,
    )


def solution(mesh):
    in_specs = (
        P(("dp", "mp"), None),
        P(("dp", "mp")),
        P(None, "mp"),
        P(None, "mp"),
        P("mp", None),
        P("mp"),
        P(None, "mp"),
        P(None, "mp"),
        P("mp", None),
        P("mp"),
        P(None, "mp"),
        P("mp", None),
        P(("dp", "mp"), None),
    )
    out_specs = (
        P(("dp", "mp"), None),
        P(("dp", "mp"), None),
        P(None, "mp"),
        P(None, "mp"),
        P("mp", None),
        P("mp"),
        P(None, "mp"),
        P(None, "mp"),
        P("mp", None),
        P("mp"),
        P(None, "mp"),
        P("mp", None),
    )
    fits = mesh.shape["dp"] == 4 and mesh.shape["mp"] == 8
    return jax.shard_map(fast_body if fits else body, mesh=mesh, in_specs=in_specs, out_specs=out_specs, check_vma=False)
```

```python
import jax
import jax.numpy as jnp
from jax import lax
from jax.experimental import pallas as pl
from jax.experimental.pallas import tpu as pltpu
from jax.sharding import PartitionSpec as P

GRID = 24
SMALL_GRID = 16
POOL = 12


epsilon = 1e-05
highest = lax.Precision.HIGHEST
root_half = 0.7071067811865476
inv_root_tau = 0.3989422804014327


def silu_slope(values):
    sigmoid = jax.nn.sigmoid(values)
    return sigmoid * (1.0 + values * (1.0 - sigmoid))


def gelu_exact(values):
    return 0.5 * values * (1.0 + lax.erf(values * root_half))


def gelu_slope(values):
    return (
        0.5 * (1.0 + lax.erf(values * root_half))
        + values * jnp.exp(-0.5 * values * values) * inv_root_tau
    )


def outer_rows(left, right):
    return lax.dot_general(
        left, right, (((0,), (0,)), ((), ())), preferred_element_type=jnp.float32
    )


def times_trans(left, right):
    return lax.dot_general(
        left, right, (((1,), (1,)), ((), ())), preferred_element_type=jnp.float32
    )


def map_padding(ndims):
    return [(0, 0)] * (ndims - 3) + [(1, 1), (1, 1), (0, 0)]


def depthwise(feature_map, tap_weights):
    extent = feature_map.shape[-2]
    padded = jnp.pad(feature_map, map_padding(feature_map.ndim))
    result = jnp.zeros_like(feature_map)
    for tap_row in range(3):
        for tap_col in range(3):
            result = (
                result
                + padded[..., tap_row : tap_row + extent, tap_col : tap_col + extent, :]
                * tap_weights[3 * tap_row + tap_col]
            )
    return result


def depthwise_back(upstream, feature_map, tap_weights):
    extent = upstream.shape[-2]
    upstream_pad = jnp.pad(upstream, map_padding(upstream.ndim))
    feature_pad = jnp.pad(feature_map, map_padding(feature_map.ndim))
    d_feature = jnp.zeros_like(upstream)
    tap_grads = []
    leading = tuple(range(upstream.ndim - 1))
    for tap_row in range(3):
        for tap_col in range(3):
            d_feature = (
                d_feature
                + upstream_pad[
                    ..., 2 - tap_row : 2 - tap_row + extent, 2 - tap_col : 2 - tap_col + extent, :
                ]
                * tap_weights[3 * tap_row + tap_col]
            )
            shifted = feature_pad[..., tap_row : tap_row + extent, tap_col : tap_col + extent, :]
            tap_grads.append(jnp.sum(shifted * upstream, axis=leading))
    return (d_feature, jnp.stack(tap_grads))


def block_forward(feature_rows, low_rows, weights_set, extent):
    w_reduce, tap_weights, w_expand, norm_gain = weights_set
    channels = w_reduce.shape[1]
    row_count = feature_rows.shape[0]
    reduced = jnp.dot(low_rows, w_reduce, preferred_element_type=jnp.float32)
    activated = jax.nn.silu(reduced).reshape(-1, extent, extent, channels)
    spatial = depthwise(activated, tap_weights.astype(jnp.float32)).reshape(row_count, channels)
    narrow = jax.nn.silu(spatial).astype(jnp.bfloat16)
    widened = jnp.dot(narrow, w_expand, preferred_element_type=jnp.float32)
    centred = widened - jnp.mean(widened, axis=1, keepdims=True)
    inv_scale = lax.rsqrt(jnp.mean(centred * centred, axis=1, keepdims=True) + epsilon)
    normed = centred * inv_scale
    result = feature_rows + normed * norm_gain.astype(jnp.float32)
    return (result, (reduced, activated, spatial, narrow, normed, inv_scale))


def block_backward(d_result, low_rows, weights_set, saved):
    w_reduce, tap_weights, w_expand, norm_gain = weights_set
    reduced, activated, spatial, narrow, normed, inv_scale = saved
    d_gain = jnp.sum(d_result * normed, axis=0)
    d_normed = d_result * norm_gain.astype(jnp.float32)
    d_widened = inv_scale * (
        d_normed
        - jnp.mean(d_normed, axis=1, keepdims=True)
        - normed * jnp.mean(d_normed * normed, axis=1, keepdims=True)
    )
    d_widened = d_widened.astype(jnp.bfloat16)
    grad_expand = outer_rows(narrow, d_widened)
    d_spatial = times_trans(d_widened, w_expand) * silu_slope(spatial)
    d_activated, grad_taps = depthwise_back(
        d_spatial.reshape(activated.shape), activated, tap_weights.astype(jnp.float32)
    )
    d_reduced = (d_activated.reshape(reduced.shape) * silu_slope(reduced)).astype(jnp.bfloat16)
    grad_reduce = outer_rows(low_rows, d_reduced)
    d_rows = d_result + times_trans(d_reduced, w_reduce)
    return (d_rows, (grad_reduce, grad_taps, grad_expand, d_gain))


def crop_rows(pixels, extent):
    features = pixels.shape[-1]
    return pixels.reshape(GRID, GRID, features)[:extent, :extent].reshape(extent * extent, features)


def widen_grid(values, extent):
    features = values.shape[-1]
    return jnp.pad(
        values.reshape(extent, extent, features), ((0, GRID - extent), (0, GRID - extent), (0, 0))
    )


def first_forward(weights_set, extent):

    def compute(pixels):
        cropped = crop_rows(pixels, extent)
        result, unused = block_forward(cropped.astype(jnp.float32), cropped, weights_set, extent)
        return widen_grid(result, extent)

    return compute


def first_backward(weights_set, extent):

    def compute(pixels, upstream):
        cropped = crop_rows(pixels, extent)
        sliced = crop_rows(upstream, extent)
        unused, saved = block_forward(cropped.astype(jnp.float32), cropped, weights_set, extent)
        d_rows, grads = block_backward(sliced, cropped, weights_set, saved)
        return (widen_grid(d_rows, extent).reshape(GRID * GRID, -1), grads)

    return compute


def pool_table(grid_side):
    bin_index = lax.iota(jnp.int32, POOL)
    bin_lower = bin_index * grid_side // POOL
    bin_upper = ((bin_index + 1) * grid_side + POOL - 1) // POOL
    cell_index = lax.iota(jnp.int32, GRID)
    inside = (cell_index[None, :] >= bin_lower[:, None]) & (
        cell_index[None, :] < bin_upper[:, None]
    )
    weights = jnp.where(inside, 1.0, 0.0) / (bin_upper - bin_lower)[:, None]
    return weights.astype(jnp.float32)


def body(
    patches,
    grid_sizes,
    w_reduce_a,
    taps_a,
    w_expand_a,
    gain_a,
    w_reduce_b,
    taps_b,
    w_expand_b,
    gain_b,
    w_in,
    w_out,
    d_tokens,
):
    gathered = (
        lax.all_gather(w_reduce_a, "mp", axis=1, tiled=True),
        lax.all_gather(taps_a, "mp", axis=1, tiled=True),
        lax.all_gather(w_expand_a, "mp", axis=0, tiled=True),
        lax.all_gather(gain_a, "mp", axis=0, tiled=True),
        lax.all_gather(w_reduce_b, "mp", axis=1, tiled=True),
        lax.all_gather(taps_b, "mp", axis=1, tiled=True),
        lax.all_gather(w_expand_b, "mp", axis=0, tiled=True),
        lax.all_gather(gain_b, "mp", axis=0, tiled=True),
    )
    first_set = gathered[0:4]
    second_set = gathered[4:8]
    features = patches.shape[1]
    pictures = patches.reshape(-1, GRID * GRID, features)
    picture_count = pictures.shape[0]
    tables = jax.vmap(pool_table)(grid_sizes)

    def forward_one(element):
        pixels, grid_side, pool_weights = element
        result = lax.cond(
            grid_side == GRID,
            first_forward(first_set, GRID),
            first_forward(first_set, SMALL_GRID),
            pixels,
        )
        return jnp.einsum("ia,jb,abd->ijd", pool_weights, pool_weights, result, precision=highest)

    pooled = lax.map(forward_one, (pictures, grid_sizes, tables))
    pooled_rows = pooled.reshape(picture_count * POOL * POOL, features)
    pooled_low = pooled_rows.astype(jnp.bfloat16)
    mixed_rows, second_saved = block_forward(pooled_rows, pooled_low, second_set, POOL)
    queries = mixed_rows.astype(jnp.bfloat16)
    hidden = jnp.dot(
        lax.all_gather(queries, "mp", axis=0, tiled=True), w_in, preferred_element_type=jnp.float32
    )
    active = gelu_exact(hidden).astype(jnp.bfloat16)
    tokens = lax.psum_scatter(
        jnp.dot(active, w_out, preferred_element_type=jnp.float32).astype(jnp.bfloat16),
        "mp",
        scatter_dimension=0,
        tiled=True,
    )
    piece = lax.all_gather(d_tokens, "mp", axis=0, tiled=True)
    d_part = (times_trans(piece, w_out) * gelu_slope(hidden)).astype(jnp.bfloat16)
    grad_out_sum = outer_rows(active, piece)
    d_hidden = d_part
    d_part = d_hidden
    grad_in_part = outer_rows(lax.all_gather(queries, "mp", axis=0, tiled=True), d_part)
    d_part = d_hidden
    d_mixed = lax.psum_scatter(times_trans(d_part, w_in), "mp", scatter_dimension=0, tiled=True)
    d_pooled, second_grads = block_backward(d_mixed, pooled_low, second_set, second_saved)
    d_pooled = d_pooled.reshape(picture_count, POOL, POOL, features)

    def backward_one(totals, element):
        pixels, grid_side, pool_weights, upstream = element
        d_grid = jnp.einsum(
            "ia,jb,ijd->abd", pool_weights, pool_weights, upstream, precision=highest
        )
        d_pixels, grads = lax.cond(
            grid_side == GRID,
            first_backward(first_set, GRID),
            first_backward(first_set, SMALL_GRID),
            pixels,
            d_grid,
        )
        return (
            tuple((total_part + grad_part for total_part, grad_part in zip(totals, grads))),
            d_pixels,
        )

    zero_grads = tuple((jnp.zeros(weight.shape, jnp.float32) for weight in first_set))
    first_grads, d_pictures = lax.scan(
        backward_one, zero_grads, (pictures, grid_sizes, tables, d_pooled)
    )
    d_patches = d_pictures.reshape(-1, features)
    shards = (
        lax.psum_scatter(
            first_grads[0].astype(jnp.bfloat16), "mp", scatter_dimension=1, tiled=True
        ).astype(jnp.float32),
        lax.psum_scatter(
            first_grads[1].astype(jnp.bfloat16), "mp", scatter_dimension=1, tiled=True
        ).astype(jnp.float32),
        lax.psum_scatter(
            first_grads[2].astype(jnp.bfloat16), "mp", scatter_dimension=0, tiled=True
        ).astype(jnp.float32),
        lax.psum_scatter(
            first_grads[3].astype(jnp.bfloat16), "mp", scatter_dimension=0, tiled=True
        ).astype(jnp.float32),
        lax.psum_scatter(
            second_grads[0].astype(jnp.bfloat16), "mp", scatter_dimension=1, tiled=True
        ).astype(jnp.float32),
        lax.psum_scatter(
            second_grads[1].astype(jnp.bfloat16), "mp", scatter_dimension=1, tiled=True
        ).astype(jnp.float32),
        lax.psum_scatter(
            second_grads[2].astype(jnp.bfloat16), "mp", scatter_dimension=0, tiled=True
        ).astype(jnp.float32),
        lax.psum_scatter(
            second_grads[3].astype(jnp.bfloat16), "mp", scatter_dimension=0, tiled=True
        ).astype(jnp.float32),
    )
    summed = (
        lax.psum(shards[0].astype(jnp.bfloat16), "dp").astype(jnp.float32),
        lax.psum(shards[1].astype(jnp.bfloat16), "dp").astype(jnp.float32),
        lax.psum(shards[2].astype(jnp.bfloat16), "dp").astype(jnp.float32),
        lax.psum(shards[3].astype(jnp.bfloat16), "dp").astype(jnp.float32),
        lax.psum(shards[4].astype(jnp.bfloat16), "dp").astype(jnp.float32),
        lax.psum(shards[5].astype(jnp.bfloat16), "dp").astype(jnp.float32),
        lax.psum(shards[6].astype(jnp.bfloat16), "dp").astype(jnp.float32),
        lax.psum(shards[7].astype(jnp.bfloat16), "dp").astype(jnp.float32),
        lax.psum(grad_in_part.astype(jnp.bfloat16), "dp").astype(jnp.float32),
        lax.psum(grad_out_sum.astype(jnp.bfloat16), "dp").astype(jnp.float32),
    )
    return (
        tokens,
        d_patches,
        summed[0],
        summed[1],
        summed[2],
        summed[3],
        summed[4],
        summed[5],
        summed[6],
        summed[7],
        summed[8],
        summed[9],
    )


bf16 = jnp.bfloat16
f32 = jnp.float32
MESH = pl.DeviceIdType.MESH
CELLS = GRID * GRID
POOLED = POOL * POOL
TILE = 96
PIECES = 4
CHUNKS = 8


def dot(left, right, left_dim, right_dim):
    return lax.dot_general(
        left, right, (((left_dim,), (right_dim,)), ((), ())), preferred_element_type=f32
    )


def split_low(values):
    high = values.astype(bf16)
    return high, (values - high.astype(f32)).astype(bf16)


def edge_masks(extent, channels):
    cells = extent * extent
    index = lax.broadcasted_iota(jnp.int32, (cells, channels), 0).astype(f32)
    row = jnp.floor((index + 0.5) * (1.0 / extent))
    col = index - row * extent
    one = jnp.ones_like(index)
    zero = jnp.zeros_like(index)
    return (
        jnp.where(row >= 0.5, one, zero),
        jnp.where(row <= extent - 1.5, one, zero),
        jnp.where(col >= 0.5, one, zero),
        jnp.where(col <= extent - 1.5, one, zero),
    )


def conv_forward(act, taps, extent, masks):
    above, below, left, right = masks
    cells = extent * extent
    up = pltpu.roll(act, extent, 0) * above
    down = pltpu.roll(act, cells - extent, 0) * below
    sums = [up * taps[q] + act * taps[3 + q] + down * taps[6 + q] for q in range(3)]
    return (
        sums[1]
        + pltpu.roll(sums[0], 1, 0) * left
        + pltpu.roll(sums[2], cells - 1, 0) * right
    )


def conv_backward(upstream, act, taps, extent, masks):
    above, below, left, right = masks
    cells = extent * extent
    sides = [pltpu.roll(upstream, cells - 1, 0) * right, upstream, pltpu.roll(upstream, 1, 0) * left]
    sums = [
        sides[0] * taps[3 * r] + sides[1] * taps[3 * r + 1] + sides[2] * taps[3 * r + 2]
        for r in range(3)
    ]
    d_act = (
        sums[1]
        + pltpu.roll(sums[0], cells - extent, 0) * below
        + pltpu.roll(sums[2], extent, 0) * above
    )
    acts = [pltpu.roll(act, extent, 0) * above, act, pltpu.roll(act, cells - extent, 0) * below]
    d_taps = [
        jnp.sum(acts[r] * sides[q], axis=0, keepdims=True) for r in range(3) for q in range(3)
    ]
    return d_act, d_taps


def slot_rows(ref):
    slots, rows, columns = ref.shape
    return ref[...].reshape(slots * rows, columns)


def layer_kernel(
    patches_in, side_in, wr_a_in, taps_a_in, we_a_in, gain_a_in, wr_b_in, taps_b_in, we_b_in, gain_b_in,
    w_in_in, w_out_in, cot_in,
    tok_out, dpat_out, gout_out, gin_out, gblk_out, gsml_out, cot_all, gfl,
    xp, gw, gws, red_a, spa_a, nar_a, norm_a, inv_a, yhi, ylo, dy, dlow, pp,
    tw, poolv, red_b, spa_b, nar_b, norm_b, inv_b,
    wi, wo, qs, actv, slope, dpre, dtv, tp, cr, ps, rl, tstage,
    dps, dr, dz, gos, gis, gyl, land,
    wgs, wgc, xs, xr, zs, zr, ys, yr, sm, smc, smx, smz, smy, gfin,
    loc, w_s, w_rz, w_rx, w_rc, sw_s, sw_r, sy_s, sy_r, q_s, q_r, q_cs, q_rc,
    dt_s, dt_r, dt_cs, dt_cr, t_cs, t_cr, t_s, t_r, credit,
    d_cs, d_cr, d_zs, d_zr, gy_s, gy_r, gx_s, gx_r, ga_s, ga_r, gc_s, gc_r, gl,
    gr_s, gr_r,
):
    dp_at = lax.axis_index("dp")
    mp_at = lax.axis_index("mp")
    y = lax.div(dp_at, 2)
    c = lax.rem(dp_at, 2)
    z = lax.div(mp_at, 2)
    x = lax.rem(mp_at, 2)
    zn = 4

    def device(x_at, y_at, z_at, c_at):
        return (2 * y_at + c_at, 2 * z_at + x_at)

    twin = device(x, y, z, 1 - c)
    x_peer = device(1 - x, y, z, c)
    y_peer = device(x, 1 - y, z, c)
    z_high = lax.div(z, 2)
    z_low = lax.rem(z, 2)
    z_near = z + 1 - 2 * z_low
    z_far = z + 2 - 4 * z_high
    z_peer = device(x, y, z_near, c)
    far_peer = device(x, y, z_far, c)
    cross = device(x, y, z_far, 1 - c)
    corner = device(1 - x, y, z_near, c)
    slot_own = 2 * z_low + x
    slot_x = 2 * z_low + 1 - x
    slot_z = 2 * (1 - z_low) + x
    slot_corner = 2 * (1 - z_low) + 1 - x

    def z_at(step):
        return lax.rem(z + step + zn, zn)

    def z_dev(z_of):
        return device(x, y, z_of, c)

    def remote(src, dst, send, recv, to):
        return pltpu.make_async_remote_copy(
            src_ref=src, dst_ref=dst, send_sem=send, recv_sem=recv, device_id=to, device_id_type=MESH
        )

    def start(src, dst, send, recv, to):
        remote(src, dst, send, recv, to).start()

    def arrived(dst, recv):
        pltpu.make_async_copy(dst, dst, recv).wait()

    def left_here(src, send):
        pltpu.make_async_copy(src, src, send).wait()

    own = z_high == c

    load_patches = pltpu.make_async_copy(patches_in, xp, loc.at[0])
    me = 2 * slot_own + c
    load_patches.start()

    own_rows = pl.ds(pl.multiple_of(16 * c, 16), 16)
    gw[c, mp_at, 0:16, :] = wr_a_in[own_rows, :]
    gw[c, mp_at, 32:48, :] = wr_b_in[own_rows, :]
    gw[c, mp_at, 16:32, :] = we_a_in[own_rows, :]
    gw[c, mp_at, 48:64, :] = we_b_in[own_rows, :]
    unit = lax.broadcasted_iota(jnp.int32, (32, 256), 0)
    lane = lax.broadcasted_iota(jnp.int32, (32, 256), 1)
    place = 16 * mp_at + jnp.where(unit >= 16, unit + 112, unit)
    spread = jnp.where(lane == place, 1.0, 0.0).astype(bf16)
    gws[c, mp_at] = jnp.zeros((16, 256), f32)

    @pl.when(c == 0)
    def _():
        gws[0, mp_at, 0:9, :] = dot(taps_a_in[...], spread, 1, 0)
        gws[0, mp_at, 9:10, 0:128] = gain_a_in[...].astype(f32).reshape(1, 128)

    @pl.when(c == 1)
    def _():
        gws[1, mp_at, 0:9, :] = dot(taps_b_in[...], spread, 1, 0)
        gws[1, mp_at, 9:10, 0:128] = gain_b_in[...].astype(f32).reshape(1, 128)

    barrier = pltpu.get_barrier_semaphore()
    peers = [twin, x_peer, cross, y_peer, corner] + [z_dev(z_at(k)) for k in range(1, zn)]
    for peer in peers:
        pl.semaphore_signal(barrier, inc=1, device_id=peer, device_id_type=MESH)
    pl.semaphore_wait(barrier, len(peers))

    spans = ((0, 16), (16, 16), (32, 32))

    def w_part(b, core, i):
        if b == 3:
            return gws.at[core, i]
        return gw.at[core, i, pl.ds(spans[b][0], spans[b][1])]

    def w_own(b):
        part = w_part(b, c, mp_at)
        for k in range(1, zn):
            start(part, part, w_s.at[b, k - 1], w_rz.at[b, k], z_dev(z_at(k)))
        start(part, part, w_s.at[b, 3], w_rx.at[b, z], x_peer)
        start(part, part, w_s.at[b, 7], w_rc.at[b, mp_at], twin)

    def w_forward(b):
        for k in range(1, zn):
            z_of = z_at(-k)
            i = 2 * z_of + x
            part = w_part(b, c, i)
            arrived(part, w_rz.at[b, k])
            start(part, part, w_s.at[b, 3 + k], w_rx.at[b, z_of], x_peer)
            start(part, part, w_s.at[b, 7 + k], w_rc.at[b, i], twin)

    def w_over(b):
        for k in range(zn):
            z_of = z_at(-k)
            i = 2 * z_of + 1 - x
            part = w_part(b, c, i)
            arrived(part, w_rx.at[b, z_of])
            start(part, part, w_s.at[b, 11 + k], w_rc.at[b, i], twin)

    def w_finish(b):
        for i in range(8):
            arrived(w_part(b, 1 - c, i), w_rc.at[b, i])

    width = cot_in.shape[1] // PIECES

    def cot(slot, c_of, p):
        return cot_all.at[slot, c_of, :, pl.ds(pl.multiple_of(p * width, width), width)]

    def cot_mine(p):
        return cot_in.at[:, pl.ds(pl.multiple_of(p * width, width), width)]

    def cot_twin(slot, p):
        part = cot(slot, c, p)
        start(part, part, dt_cs.at[p, slot], dt_cr.at[p, slot], twin)

    def cot_own_z(p):
        start(cot_mine(p), cot(slot_own, c, p), dt_s.at[p, 1], dt_r.at[p, 1], z_peer)

    def cot_own_x(p):
        start(cot_mine(p), cot(slot_own, c, p), dt_s.at[p, 0], dt_r.at[p, 0], x_peer)

    def cot_own_twin(p):
        start(cot_mine(p), cot(slot_own, c, p), dt_cs.at[p, slot_own], dt_cr.at[p, slot_own], twin)

    def cot_over_z(p):
        part = cot(slot_z, c, p)
        arrived(part, dt_r.at[p, 1])
        start(part, part, dt_s.at[p, 2], dt_r.at[p, 2], x_peer)
        cot_twin(slot_z, p)

    def cot_over_x(p):
        arrived(cot(slot_x, c, p), dt_r.at[p, 0])
        cot_twin(slot_x, p)

    def cot_corner(p):
        arrived(cot(slot_corner, c, p), dt_r.at[p, 2])
        cot_twin(slot_corner, p)

    chunk = w_out_in.shape[1] // CHUNKS

    def w_half(ref, j, half):
        if j == 0:
            return ref.at[pl.ds(pl.multiple_of(512 * half, 512), 512)]
        return ref.at[:, pl.ds(pl.multiple_of((j - 1) * width + half * chunk, chunk), chunk)]

    def swap_refs(j):
        return (w_in_in, wi) if j == 0 else (w_out_in, wo)

    def swap_send(j):
        src, dst = swap_refs(j)

        @pl.when(own)
        def _():
            pltpu.make_async_copy(w_half(src, j, y), w_half(dst, j, y), sw_r.at[j]).start()
            pltpu.make_async_copy(w_half(src, j, 1 - y), w_half(dst, j, 1 - y), sy_r.at[j]).start()

        @pl.when(jnp.logical_not(own))
        def _():
            start(w_half(src, j, y), w_half(dst, j, y), sw_s.at[j], sw_r.at[j], cross)

    def swap_forward(j):
        part = w_half(swap_refs(j)[1], j, y)
        arrived(part, sw_r.at[j])

        @pl.when(jnp.logical_not(own))
        def _():
            start(part, part, sy_s.at[j], sy_r.at[j], y_peer)

    def swap_ready(j):
        arrived(w_half(swap_refs(j)[1], j, 1 - y), sy_r.at[j])

    def reduce_weights(b):
        return gw[:, :, 32 * b : 32 * b + 16, :].reshape(256, 1024)

    def expand_weights(b):
        return gw[:, :, 32 * b + 16 : 32 * b + 32, :].reshape(256, 1024)

    def small_weights(b):
        total = gws[b, 0, 0:9, :]
        for i in range(1, 8):
            total = total + gws[b, i, 0:9, :]
        tw[b, 0:9, 0:256] = total
        for i in range(8):
            tw[b, 9:10, 128 * i : 128 * i + 128] = gws[b, i, 9:10, 0:128]
        return tw[b, 9:10, :]

    def lanes_of(h):
        return pl.ds(pl.multiple_of(h * 128, 128), 128)

    def tap_rows(b, lanes):
        return [tw[b, k : k + 1, lanes] for k in range(9)]

    def normalise(wide_ref, ref, inv_ref, rows):
        widened = wide_ref[rows, :]
        centred = widened - jnp.mean(widened, axis=1, keepdims=True)
        inv = lax.rsqrt(jnp.mean(centred * centred, axis=1, keepdims=True) + epsilon)
        normed = centred * inv
        ref[rows, :] = normed.astype(ref.dtype)
        inv_ref[rows, :] = jnp.broadcast_to(inv, (normed.shape[0], 128))
        return normed

    side = side_in[0].astype(f32)

    def cell_mask():
        index = lax.broadcasted_iota(jnp.int32, (CELLS, 128), 0).astype(f32)
        row = jnp.floor((index + 0.5) * (1.0 / GRID))
        col = index - row * GRID
        return jnp.where((row < side - 0.5) & (col < side - 0.5), 1.0, 0.0).astype(f32)


    def first_conv():
        small_weights(0)
        load_patches.wait()
        red_a[...] = dot(xp[...], reduce_weights(0), 1, 1)

        def conv_half_a(h, carry):
            lanes = lanes_of(h)
            reduced = red_a[:, lanes]
            activated = reduced * jax.nn.sigmoid(reduced) * cell_mask()
            spatial = conv_forward(activated, tap_rows(0, lanes), GRID, edge_masks(GRID, 128))
            spa_a[:, lanes] = spatial
            nar_a[:, lanes] = (spatial * jax.nn.sigmoid(spatial)).astype(bf16)
            return carry

        lax.fori_loop(0, 2, conv_half_a, 0)

    def first_norm():
        dy[...] = dot(nar_a[...], expand_weights(0), 1, 0)
        gain_a = tw[0, 9:10, :]

        def norm_tile(t, carry):
            rows = pl.ds(pl.multiple_of(t * TILE, TILE), TILE)
            normed = normalise(dy, norm_a, inv_a, rows)
            result = xp[rows, :].astype(f32) + normed * gain_a
            high, low = split_low(result)
            yhi[rows, :] = high
            ylo[rows, :] = low
            return carry

        lax.fori_loop(0, CELLS // TILE, norm_tile, 0)

    def first_pool():
        cell = lax.broadcasted_iota(jnp.int32, (POOLED, CELLS), 1).astype(f32)
        bin_of = lax.broadcasted_iota(jnp.int32, (POOLED, CELLS), 0).astype(f32)
        cell_row = jnp.floor((cell + 0.5) * (1.0 / GRID))
        cell_col = cell - cell_row * GRID
        bin_row = jnp.floor((bin_of + 0.5) * (1.0 / POOL))
        bin_col = bin_of - bin_row * POOL

        def table(bins, at):
            lower = jnp.floor((bins * side + 0.5) * (1.0 / POOL))
            upper = jnp.floor(((bins + 1.0) * side + (POOL - 0.5)) * (1.0 / POOL))
            return jnp.where((at > lower - 0.5) & (at < upper - 0.5), 1.0 / (upper - lower), 0.0)

        pp[...] = (table(bin_row, cell_row) * table(bin_col, cell_col)).astype(bf16)
        poolv[...] = dot(pp[...], yhi[...], 1, 0) + dot(pp[...], ylo[...], 1, 0)

    def second_forward():
        gain_b = small_weights(1)
        pooled = poolv[...]
        reduced_b = dot(pooled.astype(bf16), reduce_weights(1), 1, 1)
        red_b[...] = reduced_b
        activated_b = reduced_b * jax.nn.sigmoid(reduced_b)
        spatial_b = conv_forward(activated_b, tap_rows(1, pl.ds(0, 256)), POOL, edge_masks(POOL, 256))
        spa_b[...] = spatial_b
        nar_b[...] = (spatial_b * jax.nn.sigmoid(spatial_b)).astype(bf16)
        norm_b[...] = dot(nar_b[...], expand_weights(1), 1, 0)
        normed_b = normalise(norm_b, norm_b, inv_b, pl.ds(0, POOLED))
        qs[me] = (pooled + normed_b * gain_b).astype(bf16)

    def query_to(k, to):
        start(qs.at[me], qs.at[me], q_s.at[k], q_r.at[k], to)

    def query_twin():
        start(qs.at[me], qs.at[me], q_s.at[3], q_rc.at[slot_own], twin)

    def query_from(k):
        slot = (slot_x, slot_z, slot_corner)[k]
        part = qs.at[2 * slot + c]
        arrived(part, q_r.at[k])
        start(part, part, q_cs.at[k], q_rc.at[slot], twin)

    def query_all():
        for slot in (slot_own, slot_x, slot_z, slot_corner):
            arrived(qs.at[2 * slot + 1 - c], q_rc.at[slot])

    def hidden_units():
        dpre[...] = dot(slot_rows(qs), wi[...], 1, 0)

        def gelu_tile(t, carry):
            rows = pl.ds(pl.multiple_of(t * POOLED, POOLED), POOLED)
            hidden = dpre[rows, :]
            phi = 0.5 * (1.0 + lax.erf(hidden * root_half))
            actv[rows, :] = (hidden * phi).astype(bf16)
            slope[rows, :] = (
                phi + hidden * jnp.exp(-0.5 * hidden * hidden) * inv_root_tau
            ).astype(bf16)
            return carry

        lax.fori_loop(0, 8, gelu_tile, 0)
        dpre[...] = jnp.zeros_like(dpre)

    def item_part(i):
        b = i % 2

        if i >= 2:
            left_here(tp.at[b], t_cs.at[b])
            pl.semaphore_wait(credit, 1)


        weights = wo[:, i * chunk : (i + 1) * chunk]
        partial = dot(actv[...], weights, 1, 0).astype(bf16)
        partial = partial.reshape(4, 2, POOLED, chunk)

        @pl.when(c == 0)
        def _():
            ps[i] = partial[:, 0]
            tp[b] = partial[:, 1]

        @pl.when(c == 1)
        def _():
            ps[i] = partial[:, 1]
            tp[b] = partial[:, 0]

        start(tp.at[b], cr.at[b], t_cs.at[b], t_cr.at[b], twin)

    def item_pair(i):
        b = i % 2
        arrived(cr.at[b], t_cr.at[b])

        def add(d, carry):
            ps[i, d] = (ps[i, d].astype(f32) + cr[b, d].astype(f32)).astype(bf16)
            return carry

        lax.fori_loop(0, 4, add, 0)

        if i < CHUNKS - 2:
            pl.semaphore_signal(credit, inc=1, device_id=twin, device_id_type=MESH)

        start(ps.at[i, slot_corner], rl.at[i, 0], t_s.at[i, 0], t_r.at[i, 0], x_peer)
        start(ps.at[i, slot_x], rl.at[i, 1], t_s.at[i, 1], t_r.at[i, 1], x_peer)

    def item_pass(i):
        arrived(rl.at[i, 0], t_r.at[i, 0])
        ps[i, slot_z] = (ps[i, slot_z].astype(f32) + rl[i, 0].astype(f32)).astype(bf16)
        start(ps.at[i, slot_z], rl.at[i, 2], t_s.at[i, 2], t_r.at[i, 2], z_peer)

    def tok_slice(i):
        return tok_out.at[:, pl.ds(i * chunk, chunk)]

    def item_final(i):
        b = i % 2

        if i >= 2:
            left_here(tstage.at[b], gl.at[8 + b])

        arrived(rl.at[i, 1], t_r.at[i, 1])
        arrived(rl.at[i, 2], t_r.at[i, 2])
        for k in range(3):
            left_here(ps.at[i, 0], t_s.at[i, k])
        tstage[b] = (
            ps[i, slot_own].astype(f32) + rl[i, 1].astype(f32) + rl[i, 2].astype(f32)
        ).astype(bf16)
        pltpu.make_async_copy(tstage.at[b], tok_slice(i), gl.at[8 + b]).start()

    def piece_rows(p):
        for slot in range(4):
            arrived(cot(slot, 1 - c, p), dt_cr.at[p, slot])

            @pl.when(slot_own != slot)
            def _():
                part = cot_all.at[slot, :, :, pl.ds(p * width, width)]
                pltpu.make_async_copy(part, dtv.at[pl.ds(2 * slot, 2)], loc.at[3]).start()

        pltpu.make_async_copy(cot(slot_own, 1 - c, p), dtv.at[2 * slot_own + 1 - c], loc.at[3]).start()
        pltpu.make_async_copy(cot_mine(p), dtv.at[2 * slot_own + c], loc.at[3]).start()
        pltpu.make_async_copy(dtv, dtv, loc.at[3]).wait()

    def half_lanes(half):
        return pl.ds(pl.multiple_of(half * chunk, chunk), chunk)

    def piece_lanes(h):
        return dtv[:, :, half_lanes(h)].reshape(8 * POOLED, chunk)

    def hidden_part(p):
        def hidden_half(h, carry):
            weights = wo[:, pl.ds(pl.multiple_of(p * width + h * chunk, chunk), chunk)]
            dpre[...] += dot(piece_lanes(h), weights, 1, 1)
            return carry

        lax.fori_loop(0, 2, hidden_half, 0)

    def row_part(slot):
        rows = pl.ds(pl.multiple_of(slot * (2 * POOLED), 2 * POOLED), 2 * POOLED)
        d_hidden = (dpre[rows, :] * slope[rows, :].astype(f32)).astype(bf16)
        half = lax.div(slot, 2)
        place = pl.ds(pl.multiple_of((slot - 2 * half) * (2 * POOLED), 2 * POOLED), 2 * POOLED)
        ylo[place, pl.ds(pl.multiple_of(half * 512, 512), 512)] = d_hidden
        dps[slot] = dot(d_hidden, wi[...], 1, 1).astype(bf16).reshape(2, POOLED, 1024)
        start(dps.at[slot, 1 - c], dr.at[slot], d_cs.at[slot], d_cr.at[slot], twin)

    def in_turn(k):
        return jnp.where(k == 0, slot_corner, jnp.where(k == 1, slot_x, jnp.where(k == 2, slot_z, slot_own)))

    def row_gradients():
        def one(k, carry):
            @pl.when(k < 4)
            def _():
                row_part(in_turn(k))

            slot = in_turn(k - 1)

            @pl.when(k >= 1)
            def _():
                arrived(dr.at[slot], d_cr.at[slot])
                dps[slot, c] = (dps[slot, c].astype(f32) + dr[slot].astype(f32)).astype(bf16)

            @pl.when(k == 1)
            def _():
                start(dps.at[slot, c], dz.at[2], d_zs.at[2], d_zr.at[2], corner)

            @pl.when(k == 2)
            def _():
                start(dps.at[slot, c], dz.at[0], d_zs.at[0], d_zr.at[0], x_peer)

            @pl.when(k == 3)
            def _():
                start(dps.at[slot, c], dz.at[1], d_zs.at[1], d_zr.at[1], z_peer)

            return carry

        lax.fori_loop(0, 5, one, 0)

    def drain_first():
        for b in range(4):
            for k in range(15):
                left_here(w_part(b, c, 0), w_s.at[b, k])
        for k in range(4):
            left_here(qs.at[0], q_s.at[k])
        for k in range(3):
            left_here(qs.at[0], q_cs.at[k])
        for p in range(PIECES):
            for slot in range(4):
                left_here(cot(0, 0, p), dt_cs.at[p, slot])
            for k in range(3):
                left_here(cot(0, 0, p), dt_s.at[p, k])

        for j in range(1 + PIECES):
            @pl.when(jnp.logical_not(own))
            def _(j=j):
                part = w_half(swap_refs(j)[1], j, y)
                left_here(part, sw_s.at[j])
                left_here(part, sy_s.at[j])

    def grad_half(j, half):
        if j == PIECES:
            return gis.at[pl.ds(pl.multiple_of(512 * half, 512), 512)]
        return gos.at[j, :, half_lanes(half)]

    def out_half(j, half):
        if j == PIECES:
            return gin_out.at[pl.ds(pl.multiple_of(512 * half, 512), 512)]
        return gout_out.at[:, pl.ds(pl.multiple_of(j * width + half * chunk, chunk), chunk)]

    def grad_send(j, h):
        rows = pl.ds(256 * h, 256)
        if j == PIECES:
            part = gis.at[pl.ds(pl.multiple_of(512 * (1 - y) + 256 * h, 256), 256)]
        else:
            part = gos.at[j, rows, half_lanes(1 - y)]
        start(part, gyl.at[j, rows], gy_s.at[j, h], gy_r.at[j, h], y_peer)

    def grad_part(p):
        def one_half(h, carry):
            gos[p, :, half_lanes(h)] = dot(actv[...], piece_lanes(h), 0, 0).astype(bf16)
            return carry

        lax.fori_loop(0, 2, one_half, 0)

    def gin_part():
        gis[...] = (
            dot(qs[0:4].reshape(4 * POOLED, 1024), ylo[:, 0:512], 0, 0)
            + dot(qs[4:8].reshape(4 * POOLED, 1024), ylo[:, 512:1024], 0, 0)
        ).astype(bf16)

    def grad_pair(j):
        mine = grad_half(j, y)
        for h in range(2):
            arrived(gyl.at[j, pl.ds(256 * h, 256)], gy_r.at[j, h])
        mine[...] = (mine[...].astype(f32) + gyl[j].astype(f32)).astype(bf16)

        @pl.when(jnp.logical_not(own))
        def _():
            start(mine, gfl.at[j], gx_s.at[j], gx_r.at[j], far_peer)

    def grad_sum(j):
        @pl.when(own)
        def _():
            mine = grad_half(j, y)
            arrived(gfl.at[j], gx_r.at[j])
            load = pltpu.make_async_copy(gfl.at[j], land, loc.at[4])
            load.start()
            load.wait()
            mine[...] = (mine[...].astype(f32) + land[...].astype(f32)).astype(bf16)
            start(mine, out_half(j, y), ga_s.at[j], ga_r.at[j], y_peer)
            start(mine, out_half(j, y), gc_s.at[j, 0], gc_r.at[j, 0], twin)
            pltpu.make_async_copy(mine, out_half(j, y), gl.at[j]).start()

    def grad_last(j):
        @pl.when(own)
        def _():
            other = out_half(j, 1 - y)
            arrived(other, ga_r.at[j])
            start(other, other, gc_s.at[j, 1], gc_r.at[j, 1], twin)

    def grad_done(j):
        for h in range(2):
            left_here(gyl.at[j, pl.ds(256 * h, 256)], gy_s.at[j, h])

        @pl.when(own)
        def _():
            left_here(grad_half(j, y), ga_s.at[j])
            left_here(grad_half(j, y), gc_s.at[j, 0])
            left_here(grad_half(j, y), gc_s.at[j, 1])
            pltpu.make_async_copy(grad_half(j, y), out_half(j, y), gl.at[j]).wait()

        @pl.when(jnp.logical_not(own))
        def _():
            left_here(grad_half(j, y), gx_s.at[j])
            arrived(out_half(j, y), gc_r.at[j, 0])
            arrived(out_half(j, 1 - y), gc_r.at[j, 1])

    def widened_back(d_rows, normed, gain, inv):
        dn = d_rows * gain
        return (
            inv
            * (
                dn
                - jnp.mean(dn, axis=1, keepdims=True)
                - normed * jnp.mean(dn * normed, axis=1, keepdims=True)
            )
        ).astype(bf16)

    def pack_small(t, d_gain):
        for k in range(4):
            sm[t, 9 + k : 10 + k, :] = d_gain[:, 256 * k : 256 * k + 256]
        sm[t, 13:16, :] = jnp.zeros((3, 256), f32)

    passes = ((1, 0, 2, 1), (0, 1, 1, None), (0, 0, 1, 0))

    def share_core(p):
        t, k0, n, small = passes[p]
        kinds = pl.ds(k0, n)
        start(
            wgs.at[t, kinds, pl.ds(pl.multiple_of(128 * (1 - c), 128), 128)], wgc.at[t, kinds],
            gr_s.at[p, 0], gr_r.at[p, 0], twin,
        )
        if small is not None:
            start(sm.at[t], smc.at[t], gr_s.at[p, 1], gr_r.at[p, 1], twin)

    def share_x(p):
        t, k0, n, small = passes[p]
        kinds = pl.ds(k0, n)
        arrived(wgc.at[t, kinds], gr_r.at[p, 0])
        for kind in range(k0, k0 + n):
            for i in range(8):
                rows = pl.ds(pl.multiple_of(128 * c + 16 * i, 16), 16)
                xs[t, kind, i % 2, i // 2] = (
                    wgs[t, kind, rows, :].astype(f32) + wgc[t, kind, 16 * i : 16 * i + 16, :].astype(f32)
                ).astype(bf16)
        start(xs.at[t, kinds, 1 - x], xr.at[t, kinds], gr_s.at[p, 2], gr_r.at[p, 2], x_peer)
        if small is not None:
            arrived(smc.at[t], gr_r.at[p, 1])
            left_here(sm.at[t], gr_s.at[p, 1])
            sm[t] = sm[t] + smc[t]
            start(sm.at[t], smx.at[t], gr_s.at[p, 3], gr_r.at[p, 3], x_peer)

    def share_z(p):
        t, k0, n, small = passes[p]
        kinds = pl.ds(k0, n)
        arrived(xr.at[t, kinds], gr_r.at[p, 2])
        for kind in range(k0, k0 + n):
            zs[t, kind] = (xs[t, kind, x].astype(f32) + xr[t, kind].astype(f32)).astype(bf16)
        for k in range(1, zn):
            d = z_at(k)
            start(
                zs.at[t, kinds, d], zr.at[t, kinds, k - 1], gr_s.at[p, 3 + k], gr_r.at[p, 3 + k], z_dev(d)
            )
        if small is not None:
            arrived(smx.at[t], gr_r.at[p, 3])
            left_here(sm.at[t], gr_s.at[p, 3])
            smz[t, z] = sm[t] + smx[t]
            for k in range(1, zn):
                start(
                    smz.at[t, z], smz.at[t, z], gr_s.at[p, 6 + k], gr_r.at[p, 6 + k], z_dev(z_at(k))
                )

    def share_y(p):
        t, k0, n, small = passes[p]
        kinds = pl.ds(k0, n)
        for k in range(1, zn):
            arrived(zr.at[t, kinds, k - 1], gr_r.at[p, 3 + k])
        for kind in range(k0, k0 + n):
            total_rows = zs[t, kind, z].astype(f32)
            for k in range(1, zn):
                total_rows = total_rows + zr[t, kind, k - 1].astype(f32)
            ys[t, kind] = total_rows.astype(bf16)
        start(ys.at[t, kinds], yr.at[t, kinds], gr_s.at[p, 10], gr_r.at[p, 10], y_peer)
        if small is not None:
            for k in range(1, zn):
                arrived(smz.at[t, z_at(-k)], gr_r.at[p, 6 + k])
            sm[t] = (smz[t, 0] + smz[t, 1]) + (smz[t, 2] + smz[t, 3])
            start(sm.at[t], smy.at[t], gr_s.at[p, 11], gr_r.at[p, 11], y_peer)

    def share_twin(p):
        t, k0, n, small = passes[p]
        kinds = pl.ds(k0, n)
        arrived(yr.at[t, kinds], gr_r.at[p, 10])
        for kind in range(k0, k0 + n):
            gfin[c, t, kind] = ys[t, kind].astype(f32) + yr[t, kind].astype(f32)
        part = gfin.at[c, t, kinds]
        start(part, part, gr_s.at[p, 12], gr_r.at[p, 12], twin)
        if small is not None:
            arrived(smy.at[t], gr_r.at[p, 11])
            gsml_out[t] = sm[t] + smy[t]

    def share_done(p):
        t, k0, n, small = passes[p]
        kinds = pl.ds(k0, n)
        arrived(gfin.at[1 - c, t, kinds], gr_r.at[p, 12])
        for kind in range(k0, k0 + n):
            for h in range(2):
                gblk_out[t, kind, 16 * h : 16 * h + 16, :] = gfin[h, t, kind]
        left_here(wgc.at[t, kinds], gr_s.at[p, 0])
        left_here(xr.at[t, kinds], gr_s.at[p, 2])
        for k in range(1, zn):
            left_here(ys.at[t, kinds], gr_s.at[p, 3 + k])
        left_here(ys.at[t, kinds], gr_s.at[p, 10])
        left_here(gfin.at[c, t, kinds], gr_s.at[p, 12])
        if small is not None:
            for k in range(1, zn):
                left_here(sm.at[t], gr_s.at[p, 6 + k])
            left_here(sm.at[t], gr_s.at[p, 11])

    def back_second():
        total = dps[slot_own, c].astype(f32)
        for k in range(3):
            arrived(dz.at[k], d_zr.at[k])
            total = total + dz[k].astype(f32)
        normed_b = norm_b[...]
        d_gain_b = jnp.sum(total * normed_b, axis=0, keepdims=True)
        gain_b = tw[1, 9:10, :]
        dw_b = widened_back(total, normed_b, gain_b, inv_b[:, 0:1])
        wgs[1, 1] = dot(nar_b[...], dw_b, 0, 0).astype(bf16)
        spatial_b = spa_b[...]
        d_spatial_b = dot(dw_b, expand_weights(1), 1, 1) * silu_slope(spatial_b)
        reduced_b = red_b[...]
        sig_b = jax.nn.sigmoid(reduced_b)
        d_act_b, d_taps_b = conv_backward(
            d_spatial_b, reduced_b * sig_b, tap_rows(1, pl.ds(0, 256)), POOL, edge_masks(POOL, 256)
        )
        d_red_b = (d_act_b * (sig_b * (1.0 + reduced_b * (1.0 - sig_b)))).astype(bf16)
        wgs[1, 0] = dot(d_red_b, poolv[...].astype(bf16), 0, 0).astype(bf16)
        for k in range(9):
            sm[1, k : k + 1, :] = d_taps_b[k]
        pack_small(1, d_gain_b)
        d_pool = total + dot(d_red_b, reduce_weights(1), 1, 0)
        high, low = split_low(d_pool)
        dy[...] = dot(pp[...], high, 0, 0) + dot(pp[...], low, 0, 0)

    def back_first_norm():
        gain_a = tw[0, 9:10, :]

        def back_tile(t, d_gain):
            rows = pl.ds(pl.multiple_of(t * TILE, TILE), TILE)
            d_rows = dy[rows, :]
            normed = norm_a[rows, :].astype(f32)
            yhi[rows, :] = widened_back(d_rows, normed, gain_a, inv_a[rows, 0:1])
            return d_gain + jnp.sum(d_rows * normed, axis=0, keepdims=True)

        d_gain_a = lax.fori_loop(0, CELLS // TILE, back_tile, jnp.zeros((1, 1024), f32))
        pack_small(0, d_gain_a)
        wgs[0, 1] = dot(nar_a[...], yhi[...], 0, 0).astype(bf16)

    def back_first_conv():
        spa_a[...] = dot(yhi[...], expand_weights(0), 1, 1) * silu_slope(spa_a[...])

        def conv_back_half_a(h, carry):
            lanes = lanes_of(h)
            reduced = red_a[:, lanes]
            sig = jax.nn.sigmoid(reduced)
            mask = cell_mask()
            d_act, d_taps = conv_backward(
                spa_a[:, lanes], reduced * sig * mask, tap_rows(0, lanes), GRID, edge_masks(GRID, 128)
            )
            dlow[:, lanes] = (d_act * mask * (sig * (1.0 + reduced * (1.0 - sig)))).astype(bf16)
            for k in range(9):
                sm[0, k : k + 1, lanes] = d_taps[k]
            return carry

        lax.fori_loop(0, 2, conv_back_half_a, 0)
        wgs[0, 0] = dot(dlow[...], xp[...], 0, 0).astype(bf16)

    store_dpat = pltpu.make_async_copy(dy, dpat_out, loc.at[5])

    def back_first_rows():
        dy[...] += dot(dlow[...], reduce_weights(0), 1, 0)
        store_dpat.start()

    cot_own_x(0)
    w_own(3)
    w_own(1)
    w_own(0)
    cot_own_z(0)
    cot_own_x(3)
    w_forward(3)
    w_own(2)
    swap_send(0)
    swap_send(1)
    w_forward(1)
    swap_send(2)
    w_forward(0)
    cot_own_x(2)
    w_over(3)
    w_finish(3)
    cot_own_twin(1)
    cot_over_x(0)
    w_over(0)
    cot_own_z(1)
    w_finish(0)
    w_over(1)
    w_forward(2)
    first_conv()
    w_finish(1)
    first_norm()
    cot_over_z(0)
    cot_own_twin(2)
    w_over(2)
    first_pool()
    cot_own_twin(0)
    w_finish(2)
    second_forward()
    swap_forward(0)
    query_to(0, x_peer)
    query_twin()
    query_to(2, corner)
    swap_forward(1)
    query_to(1, z_peer)
    swap_ready(0)
    cot_corner(0)
    piece_rows(0)
    query_from(0)
    query_from(2)
    swap_send(3)
    swap_ready(1)
    swap_forward(2)
    cot_own_z(2)
    cot_own_x(1)
    query_from(1)
    query_all()
    cot_over_z(1)
    swap_send(4)
    hidden_units()

    grad_part(0)
    grad_send(0, 1)
    item_part(0)
    hidden_part(0)
    grad_send(0, 0)
    cot_over_x(1)
    swap_forward(3)
    cot_own_z(3)
    cot_over_z(2)
    cot_over_x(3)
    cot_corner(1)
    piece_rows(1)
    item_pair(0)
    grad_part(1)
    grad_send(1, 1)
    grad_send(1, 0)
    item_part(1)
    cot_over_x(2)
    swap_ready(3)
    swap_ready(2)
    cot_corner(2)
    cot_over_z(3)
    cot_own_twin(3)
    grad_pair(0)
    item_part(2)
    item_pair(1)
    item_part(3)
    swap_forward(4)
    item_pass(0)
    hidden_part(1)
    piece_rows(2)
    grad_part(2)
    cot_corner(3)
    item_pair(2)
    item_pair(3)
    grad_send(2, 0)
    hidden_part(2)
    grad_send(2, 1)
    grad_pair(1)
    item_part(4)
    item_pass(1)
    piece_rows(3)
    grad_part(3)
    grad_send(3, 1)
    swap_ready(4)
    hidden_part(3)
    row_gradients()
    item_final(0)
    item_pair(4)
    grad_send(3, 0)
    gin_part()
    grad_sum(1)
    grad_pair(2)
    item_part(5)
    item_part(6)
    item_pair(5)
    grad_pair(3)
    drain_first()
    back_second()
    item_pass(2)
    item_pass(3)
    grad_last(1)
    grad_send(PIECES, 1)
    item_pass(4)
    share_core(0)
    grad_send(PIECES, 0)
    grad_sum(0)
    item_pair(6)
    back_first_norm()
    back_first_conv()
    share_core(2)
    share_x(0)
    item_final(1)
    grad_sum(3)
    grad_sum(2)
    grad_pair(PIECES)
    share_x(2)
    share_core(1)
    item_part(7)
    item_pass(5)
    share_z(0)
    item_pass(6)
    item_final(2)
    item_final(3)
    item_final(4)
    grad_last(0)
    item_final(5)
    share_x(1)
    grad_sum(PIECES)
    back_first_rows()
    share_z(2)
    item_final(6)
    item_pair(7)
    share_z(1)
    share_y(0)
    grad_last(2)
    share_y(2)
    grad_last(PIECES)
    grad_last(3)
    item_pass(7)
    share_y(1)
    share_twin(2)
    share_twin(0)
    share_twin(1)
    for j in range(3):
        grad_done(j)
    for p in range(2):
        share_done(p)
    item_final(7)

    share_done(2)
    for j in range(3, 1 + PIECES):
        grad_done(j)

    store_dpat.wait()
    for b in range(2):
        pltpu.make_async_copy(tstage.at[b], tok_slice(b), gl.at[8 + b]).wait()
        left_here(tp.at[b], t_cs.at[b])
    for k in range(4):
        left_here(dps.at[0, 0], d_cs.at[k])
    for k in range(3):
        left_here(dps.at[0, 0], d_zs.at[k])


def layer_call(
    patches, grid_sizes, wr_a, taps_a, we_a, gain_a, wr_b, taps_b, we_b, gain_b, w_in, w_out, d_tokens
):
    any_space = pl.BlockSpec(memory_space=pl.ANY)
    vmem = pl.BlockSpec(memory_space=pltpu.VMEM)
    smem = pl.BlockSpec(memory_space=pltpu.SMEM)
    shape = jax.ShapeDtypeStruct
    width = w_out.shape[1] // PIECES
    chunk = w_out.shape[1] // CHUNKS
    out_shape = (
        shape((POOLED, 4096), bf16),
        shape((CELLS, 1024), f32),
        shape((512, 4096), bf16),
        shape((1024, 512), bf16),
        shape((2, 2, 32, 1024), f32),
        shape((2, 16, 256), f32),
        shape((4, 2, POOLED, 4096), bf16),
        shape((1 + PIECES, 512, width // 2), bf16),
    )
    dma = pltpu.SemaphoreType.DMA
    scratch = [
        pltpu.VMEM((CELLS, 1024), bf16),
        pltpu.VMEM((2, 8, 64, 1024), bf16),
        pltpu.VMEM((2, 8, 16, 256), f32),
        pltpu.VMEM((CELLS, 256), f32),
        pltpu.VMEM((CELLS, 256), f32),
        pltpu.VMEM((CELLS, 256), bf16),
        pltpu.VMEM((CELLS, 1024), bf16),
        pltpu.VMEM((CELLS, 128), f32),
        pltpu.VMEM((CELLS, 1024), bf16),
        pltpu.VMEM((CELLS, 1024), bf16),
        pltpu.VMEM((CELLS, 1024), f32),
        pltpu.VMEM((CELLS, 256), bf16),
        pltpu.VMEM((POOLED, CELLS), bf16),
        pltpu.VMEM((2, 16, 1024), f32),
        pltpu.VMEM((POOLED, 1024), f32),
        pltpu.VMEM((POOLED, 256), f32),
        pltpu.VMEM((POOLED, 256), f32),
        pltpu.VMEM((POOLED, 256), bf16),
        pltpu.VMEM((POOLED, 1024), f32),
        pltpu.VMEM((POOLED, 128), f32),
        pltpu.VMEM((1024, 512), bf16),
        pltpu.VMEM((512, 4096), bf16),
        pltpu.VMEM((8, POOLED, 1024), bf16),
        pltpu.VMEM((8 * POOLED, 512), bf16),
        pltpu.VMEM((8 * POOLED, 512), bf16),
        pltpu.VMEM((8 * POOLED, 512), f32),
        pltpu.VMEM((8, POOLED, width), bf16),
        pltpu.VMEM((2, 4, POOLED, chunk), bf16),
        pltpu.VMEM((2, 4, POOLED, chunk), bf16),
        pltpu.VMEM((CHUNKS, 4, POOLED, chunk), bf16),
        pltpu.VMEM((CHUNKS, 3, POOLED, chunk), bf16),
        pltpu.VMEM((2, POOLED, chunk), bf16),
        pltpu.VMEM((4, 2, POOLED, 1024), bf16),
        pltpu.VMEM((4, POOLED, 1024), bf16),
        pltpu.VMEM((3, POOLED, 1024), bf16),
        pltpu.VMEM((PIECES, 512, width), bf16),
        pltpu.VMEM((1024, 512), bf16),
        pltpu.VMEM((1 + PIECES, 512, width // 2), bf16),
        pltpu.VMEM((512, width // 2), bf16),
        pltpu.VMEM((2, 2, 256, 1024), bf16),
        pltpu.VMEM((2, 2, 128, 1024), bf16),
        pltpu.VMEM((2, 2, 2, 4, 16, 1024), bf16),
        pltpu.VMEM((2, 2, 4, 16, 1024), bf16),
        pltpu.VMEM((2, 2, 4, 16, 1024), bf16),
        pltpu.VMEM((2, 2, 3, 16, 1024), bf16),
        pltpu.VMEM((2, 2, 16, 1024), bf16),
        pltpu.VMEM((2, 2, 16, 1024), bf16),
        pltpu.VMEM((2, 16, 256), f32),
        pltpu.VMEM((2, 16, 256), f32),
        pltpu.VMEM((2, 16, 256), f32),
        pltpu.VMEM((2, 4, 16, 256), f32),
        pltpu.VMEM((2, 16, 256), f32),
        pltpu.VMEM((2, 2, 2, 16, 1024), f32),
        dma((6,)),
        dma((4, 15)),
        dma((4, 4)),
        dma((4, 4)),
        dma((4, 8)),
        dma((1 + PIECES,)),
        dma((1 + PIECES,)),
        dma((1 + PIECES,)),
        dma((1 + PIECES,)),
        dma((4,)),
        dma((3,)),
        dma((3,)),
        dma((4,)),
        dma((PIECES, 3)),
        dma((PIECES, 3)),
        dma((PIECES, 4)),
        dma((PIECES, 4)),
        dma((2,)),
        dma((2,)),
        dma((CHUNKS, 3)),
        dma((CHUNKS, 3)),
        pltpu.SemaphoreType.REGULAR,
        dma((4,)),
        dma((4,)),
        dma((3,)),
        dma((3,)),
        dma((1 + PIECES, 2)),
        dma((1 + PIECES, 2)),
        dma((1 + PIECES,)),
        dma((1 + PIECES,)),
        dma((1 + PIECES,)),
        dma((1 + PIECES,)),
        dma((1 + PIECES, 2)),
        dma((1 + PIECES, 2)),
        dma((10,)),
        dma((3, 13)),
        dma((3, 13)),
    ]
    return pl.pallas_call(
        layer_kernel,
        out_shape=out_shape,
        in_specs=[any_space, smem] + [vmem] * 8 + [any_space] * 3,
        out_specs=(any_space, any_space, any_space, any_space, vmem, vmem, any_space, any_space),
        scratch_shapes=scratch,
        compiler_params=pltpu.CompilerParams(
            collective_id=0, has_side_effects=True, vmem_limit_bytes=VMEM_BYTES
        ),
    )(
        patches, grid_sizes, wr_a, taps_a, we_a, gain_a, wr_b, taps_b, we_b, gain_b, w_in, w_out, d_tokens
    )


VMEM_BYTES = 64 * 1024 * 1024


FINISH = 2


def finish_kernel(
    tok_in, dpat_in, gout_in, gin_in, gblk_in, gsml_in,
    tok, dpat, gout, gin, gra, gta, gea, gga, grb, gtb, geb, ggb,
):
    tok[...] = tok_in[...]
    dpat[...] = dpat_in[...]
    gout[...] = gout_in[...].astype(f32)
    gin[...] = gin_in[...].astype(f32)

    @pl.when(pl.program_id(0) == 0)
    def _():
        mp_at = lax.axis_index("mp")
        for t, outs in enumerate(((gra, gta, gea, gga), (grb, gtb, geb, ggb))):
            reduce, taps, expand, gain = outs
            reduce[...] = gblk_in[t, 0]
            expand[...] = gblk_in[t, 1]
            turned = pltpu.roll(gsml_in[t], lax.rem(256 - 16 * mp_at, 256), 1)
            taps[:, 0:16] = turned[0:9, 0:16]
            taps[:, 16:32] = turned[0:9, 128:144]
            for i in range(8):
                @pl.when(mp_at == i)
                def _(t=t, i=i, gain=gain):
                    lanes = 128 * (i % 2)
                    gain[...] = gsml_in[t, 9 + i // 2 : 10 + i // 2, lanes : lanes + 128]


def finish_call(tokens, d_patches, gout, gin, gblk, gsml):
    shape = jax.ShapeDtypeStruct
    columns = tokens.shape[1] // FINISH

    def whole(*dims):
        return pl.BlockSpec(dims, lambda i: (0,) * len(dims))

    one = [whole(32, 1024), whole(9, 32), whole(32, 1024), whole(1, 128)]
    one_shape = [shape((32, 1024), f32), shape((9, 32), f32), shape((32, 1024), f32), shape((1, 128), f32)]
    return pl.pallas_call(
        finish_kernel,
        grid=(FINISH,),
        out_shape=[
            shape(tokens.shape, bf16),
            shape(d_patches.shape, f32),
            shape(gout.shape, f32),
            shape(gin.shape, f32),
        ]
        + one_shape * 2,
        in_specs=[
            pl.BlockSpec((POOLED, columns), lambda i: (0, i)),
            pl.BlockSpec((CELLS // FINISH, 1024), lambda i: (i, 0)),
            pl.BlockSpec((512 // FINISH, 4096), lambda i: (i, 0)),
            pl.BlockSpec((1024 // FINISH, 512), lambda i: (i, 0)),
            whole(2, 2, 32, 1024),
            whole(2, 16, 256),
        ],
        out_specs=[
            pl.BlockSpec((POOLED, columns), lambda i: (0, i)),
            pl.BlockSpec((CELLS // FINISH, 1024), lambda i: (i, 0)),
            pl.BlockSpec((512 // FINISH, 4096), lambda i: (i, 0)),
            pl.BlockSpec((1024 // FINISH, 512), lambda i: (i, 0)),
        ]
        + one * 2,
        compiler_params=pltpu.CompilerParams(vmem_limit_bytes=VMEM_BYTES),
    )(tokens, d_patches, gout, gin, gblk, gsml)


def fast_body(
    patches, grid_sizes, w_reduce_a, taps_a, w_expand_a, gain_a,
    w_reduce_b, taps_b, w_expand_b, gain_b, w_in, w_out, d_tokens,
):
    results = layer_call(
        patches, grid_sizes, w_reduce_a.T, taps_a, w_expand_a, gain_a,
        w_reduce_b.T, taps_b, w_expand_b, gain_b, w_in, w_out, d_tokens,
    )
    (
        tokens, d_patches, gout, gin, reduce_a, tap_a, expand_a, scale_a, reduce_b, tap_b, expand_b, scale_b
    ) = finish_call(*results[:6])
    return (
        tokens, d_patches,
        reduce_a.T, tap_a, expand_a, scale_a.reshape(-1),
        reduce_b.T, tap_b, expand_b, scale_b.reshape(-1),
        gin, gout,
    )


def solution(mesh):
    in_specs = (
        P(("dp", "mp"), None),
        P(("dp", "mp")),
        P(None, "mp"),
        P(None, "mp"),
        P("mp", None),
        P("mp"),
        P(None, "mp"),
        P(None, "mp"),
        P("mp", None),
        P("mp"),
        P(None, "mp"),
        P("mp", None),
        P(("dp", "mp"), None),
    )
    out_specs = (
        P(("dp", "mp"), None),
        P(("dp", "mp"), None),
        P(None, "mp"),
        P(None, "mp"),
        P("mp", None),
        P("mp"),
        P(None, "mp"),
        P(None, "mp"),
        P("mp", None),
        P("mp"),
        P(None, "mp"),
        P("mp", None),
    )
    fits = mesh.shape["dp"] == 4 and mesh.shape["mp"] == 8
    return jax.shard_map(fast_body if fits else body, mesh=mesh, in_specs=in_specs, out_specs=out_specs, check_vma=False)
```
